128 devices in a mesh: group: 16 (over z, x_lo, core), tp: 8 (over y, x_hi).
Axes of the slice: x: 4 (x_hi: 2, x_lo: 2; x = x_hi * 2 + x_lo), y: 4, z: 4, core: 2. Of those that a mesh axis runs over, the one named last changes fastest.
Arguments:
- dec_rows: bfloat16 [224, 5120], P('group'), may hold values from -6 to 6
- kv_cache: bfloat16 [224, 2, 768, 1024], P('group', None, None, 'tp'), may hold values from -40 to 40
- lengths: int32 [224], replicated, may hold values from 1 to 766, as said below
- dest_group: int32 [224], replicated, may hold values from 0 to 15, as said below
- dest_slot: int32 [224], replicated, may hold values from 0 to 13, as said below
- score_rows: bfloat16 [7168, 5120], P(('group', 'tp')), may hold values from -6 to 6
- doc_ids: int32 [16, 448], P('group'), may hold values from 0 to 8, never falling along the last dimension, each value on 1 to 336 neighbouring positions
- norm_gain: float32 [5120], replicated, may hold values from 0.1 to 1.9
- query_gain: float32 [128], replicated, may hold values from 0.5 to 42
- key_gain: float32 [128], replicated, may hold values from 0.5 to 42
- w_query: bfloat16 [5120, 4096], P(None, 'tp'), may hold values from -0.078125 to 0.078125
- w_keyval: bfloat16 [5120, 2, 1024], P(None, None, 'tp'), may hold values from -0.078125 to 0.078125
- w_out: bfloat16 [4096, 5120], P('tp'), may hold values from -0.09375 to 0.09375
Outputs:
- dec_out: bfloat16 [224, 5120], P('group')
- dec_cache: bfloat16 [224, 2, 768, 1024], P('group', None, None, 'tp')
- score_out: bfloat16 [7168, 5120], P(('group', 'tp'))
The draws below stay inside these ranges and needn't reach their ends.
Inputs may be any that keep to these rules, and one draw needn't show every extreme that they name: `lengths`: every decode row has room for two more positions; some row has exactly 766 cached positions. `dest_group`: A group sends either none or exactly 1 of its rows to any one group (possibly itself), and every group receives exactly 14 rows in all. `dest_slot`: the rows that reach one group take its slots 0 to 13, each slot once.
All inputs are finite; a program needn't handle non-finite values.
Results may differ from the reference program's by a relative error of at most 0.03615.
The reference program's roundings to bfloat16 on the way count: a program that leaves them out, or rounds other values in their place, can miss the bound.
Values may be sent and summed in bfloat16 or wider, within the bound.
A program may use at most 128 MiB of HBM per device.

```python
import math
import jax
import jax.numpy as jnp
import numpy as np
from jax import lax

D = 5120
HD = 128
CTX = 768
R_DEV = 14
QW = 4096
KVW = 1024
ROWS = 224
P_SIZE = 448
PTOK = 7168
N_GROUP = 16
N_TP = 8


def routing(key):
    first, second, third = jax.random.split(jax.random.fold_in(key, 200), 3)
    ngroup = ROWS // R_DEV
    most = (R_DEV + ngroup - 1) // ngroup
    pairs = R_DEV // most
    owners = jax.random.permutation(first, ngroup)
    shifts = jax.random.permutation(second, ngroup)[:pairs]
    scores = jax.random.randint(third, (ngroup, R_DEV), 0, 1 << 20) * R_DEV + jnp.arange(R_DEV)[None, :]
    place = jnp.argsort(jnp.argsort(scores, axis=1), axis=1).astype(jnp.int32)
    source = jnp.arange(ngroup, dtype=jnp.int32)[:, None]
    target = owners[(source + shifts[place // most]) % ngroup]
    return (target.reshape(-1).astype(jnp.int32), place.reshape(-1).astype(jnp.int32))


def draw_dest_group(key, part):
    target, place = routing(key)
    return target


def draw_dest_slot(key, part):
    target, place = routing(key)
    return place


def draw_lengths(key, part):
    key = jax.random.fold_in(key, 5)
    first, second = jax.random.split(key)
    base = jax.random.randint(first, (ROWS,), 1, CTX - 1)
    chosen = jax.random.randint(second, (), 0, ROWS)
    return base.at[chosen].set(CTX - 2).astype(jnp.int32)


def gain_values(key, shift):
    key = jax.random.fold_in(key, shift)
    first = jax.random.fold_in(key, 0)
    return jax.random.uniform(first, (HD,), jnp.float32, 0.6, 1.6)


def draw_query_gain(key, part):
    return gain_values(key, 11)


def draw_key_gain(key, part):
    return gain_values(key, 12)


def draw_kv_cache(key, part):
    key = jax.random.fold_in(key, 7)
    shape = (ROWS, 2, CTX, KVW)
    values = jax.random.truncated_normal(key, -4.0, 4.0, shape, jnp.float32)
    return values.astype(jnp.bfloat16)


def block_levels(own_key, shape, cuts, low, high):
    def one(dim, blocks):
        heights = jax.random.uniform(jax.random.fold_in(jax.random.fold_in(own_key, 6), dim), (blocks,), jnp.float32, low / len(cuts), high / len(cuts))
        return jnp.repeat(jnp.exp(heights), shape[dim] // blocks).reshape((-1,) + (1,) * (len(shape) - dim - 1))

    level = one(*cuts[0])
    for cut in cuts[1:]:
        level = level * one(*cut)
    return level


def split_up(number_of, total, bound, skew):
    weights = [(1 << 20) // math.isqrt(rank ** skew) + 1 for rank in range(2, number_of + 1)]
    spare, counts = total - bound - (number_of - 1), [1] * (number_of - 1)
    while spare > 0:
        movable = [i for i in range(number_of - 1) if counts[i] < bound]
        whole, left = sum([weights[i] for i in movable]), spare
        for i in movable:
            more = min(bound - counts[i], max(1, left * weights[i] // whole), spare)
            counts[i] = counts[i] + more
            spare = spare - more
    return np.array([bound] + counts)


def ragged_sizes(key, count, total, most, lean):
    if count == 2:
        one = jax.random.randint(key, (), max(1, total - most), min(most, total - 1) + 1)
        return jnp.stack([one, total - one])
    tallies = jnp.asarray(split_up(count, total, most, lean), jnp.int32)
    twos = (count - 1) // 2
    source_of, taker = tallies[1:1 + 2 * twos:2], tallies[2:2 + 2 * twos:2]
    slack = jnp.minimum(source_of - 1, most - taker)
    moved = jax.random.randint(jax.random.fold_in(key, 1), (twos,), 0, 1 << 20) % (slack + 1)
    tallies = tallies.at[1:1 + 2 * twos:2].set(source_of - moved).at[2:2 + 2 * twos:2].set(taker + moved)
    return tallies[jax.random.permutation(jax.random.fold_in(key, 2), count)]


def bell_draw(own_key, shape, spread, bound, shards=(), held_as=jnp.bfloat16):
    level = block_levels(own_key, shape, shards, -0.22, 0.18) if shards else 1.0
    array = jax.random.normal(own_key, shape, jnp.float32) * spread * level
    return jnp.minimum(jnp.maximum(array, -bound), bound).astype(held_as)


def setup_inputs(seed: int = 0) -> dict:
    key_list = jax.random.split(jax.random.key(seed), 14)
    return {
        "dec_rows": bell_draw(key_list[0], (ROWS, D), 1.0, 6.0, ((0, 16),)),
        "kv_cache": draw_kv_cache(jax.random.fold_in(key_list[13], 71), 0),
        "lengths": draw_lengths(jax.random.fold_in(key_list[13], 71), 0),
        "dest_group": draw_dest_group(jax.random.fold_in(key_list[13], 71), 0),
        "dest_slot": draw_dest_slot(jax.random.fold_in(key_list[13], 71), 0),
        "score_rows": bell_draw(key_list[5], (PTOK, D), 1.0, 6.0, ((0, 128),)),
        "doc_ids": jax.vmap(lambda own: jnp.searchsorted(jnp.cumsum(ragged_sizes(own, max(2, P_SIZE // 48), P_SIZE, P_SIZE // 2 + P_SIZE // 4, 1)), jnp.arange(P_SIZE), side="right"))(jax.random.split(key_list[6], N_GROUP)).reshape((N_GROUP, P_SIZE)).astype(jnp.int32),
        "norm_gain": jnp.clip(1.0 + 0.18 * jax.random.normal(key_list[7], (D,), jnp.float32), 0.1, 1.9),
        "query_gain": draw_query_gain(jax.random.fold_in(key_list[13], 71), 0),
        "key_gain": draw_key_gain(jax.random.fold_in(key_list[13], 71), 0),
        "w_query": bell_draw(key_list[10], (D, QW), D ** -0.5, 0.078125, ((1, 8),)),
        "w_keyval": bell_draw(key_list[11], (D, 2, KVW), D ** -0.5, 0.078125, ((2, 8),)),
        "w_out": bell_draw(key_list[12], (QW, D), QW ** -0.5, 0.09375, ((0, 8),)),
    }


EPS = 1e-06

def row_scale(wide):
    return lax.rsqrt(lax.optimization_barrier(jnp.mean(wide * wide, axis=-1, keepdims=True)) + EPS)

def project(rows, norm_gain, w_query, w_keyval):
    wide = rows.astype(jnp.float32)
    scale = row_scale(wide)
    normed = (wide * norm_gain).astype(jnp.bfloat16)
    query = jnp.dot(normed, w_query, preferred_element_type=jnp.float32) * scale
    flat = w_keyval.reshape(w_keyval.shape[0], -1)
    keyval = jnp.dot(normed, flat, preferred_element_type=jnp.float32) * scale
    return (query, keyval)

def head_norm(vectors, gain):
    return (vectors * row_scale(vectors) * gain).astype(jnp.bfloat16)

def softmax_rows(scores):
    top = lax.optimization_barrier(jnp.max(scores, axis=-1, keepdims=True))
    expo = jnp.exp(scores - top)
    return (expo / lax.optimization_barrier(jnp.sum(expo, axis=-1, keepdims=True))).astype(jnp.bfloat16)

def decode_block(rows, cache, lengths, norm_gain, query_gain, key_gain, w_query, w_keyval, w_out):
    count = rows.shape[0]
    ctx = cache.shape[2]
    width = cache.shape[3]
    kvh = width // HD
    for step in range(2):
        positions = lengths + step
        query, keyval = project(rows, norm_gain, w_query, w_keyval)
        group = query.shape[1] // width
        heads = head_norm(query.reshape(count, kvh, group, HD), query_gain)
        new_keys = head_norm(keyval[:, :width].reshape(count, kvh, HD), key_gain).reshape(count, 1, width)
        new_vals = keyval[:, width:].astype(jnp.bfloat16).reshape(count, 1, width)
        spots = lax.broadcasted_iota(jnp.int32, (count, ctx, 1), 1) == positions[:, None, None]
        keys = jnp.where(spots, new_keys, cache[:, 0])
        vals = jnp.where(spots, new_vals, cache[:, 1])
        cache = jnp.stack([keys, vals], axis=1)
        scores = jnp.einsum('nkgd,nckd->nkgc', heads.astype(jnp.float32), keys.reshape(count, ctx, kvh, HD).astype(jnp.float32)) * (1.0 / math.sqrt(HD))
        live = lax.broadcasted_iota(jnp.int32, (count, 1, 1, ctx), 3) <= positions[:, None, None, None]
        weights = softmax_rows(jnp.where(live, scores, -jnp.inf))
        attn = jnp.einsum('nkgc,nckd->nkgd', weights.astype(jnp.float32), vals.reshape(count, ctx, kvh, HD).astype(jnp.float32))
        attn = attn.astype(jnp.bfloat16).reshape(count, -1)
        rows = (rows.astype(jnp.float32) + jnp.dot(attn, w_out, preferred_element_type=jnp.float32)).astype(jnp.bfloat16)
    return (rows, cache)

def score_block(rows, docs, norm_gain, query_gain, key_gain, w_query, w_keyval, w_out):
    count = rows.shape[0]
    width = w_keyval.shape[2]
    kvh = width // HD
    query, keyval = project(rows, norm_gain, w_query, w_keyval)
    group = query.shape[1] // width
    heads = head_norm(query.reshape(count, kvh, group, HD), query_gain)
    keys = head_norm(keyval[:, :width].reshape(count, kvh, HD), key_gain)
    vals = keyval[:, width:].astype(jnp.bfloat16).reshape(count, kvh, HD)
    scores = jnp.einsum('pkgd,qkd->kgpq', heads.astype(jnp.float32), keys.astype(jnp.float32)) * (1.0 / math.sqrt(HD))
    later = lax.broadcasted_iota(jnp.int32, (count, count), 1) <= lax.broadcasted_iota(jnp.int32, (count, count), 0)
    live = (docs[:, None] == docs[None, :]) & later
    weights = softmax_rows(jnp.where(live[None, None], scores, -jnp.inf))
    attn = jnp.einsum('kgpq,qkd->pkgd', weights.astype(jnp.float32), vals.astype(jnp.float32))
    attn = attn.astype(jnp.bfloat16).reshape(count, N_TP, -1)
    blocks = w_out.reshape(N_TP, -1, w_out.shape[1])
    parts = jnp.einsum('ptc,tcd->tpd', attn.astype(jnp.float32), blocks.astype(jnp.float32))
    rounded = lax.optimization_barrier(parts.astype(jnp.bfloat16))
    total = lax.optimization_barrier(jnp.sum(rounded.astype(jnp.float32), axis=0))
    return (rows.astype(jnp.float32) + total).astype(jnp.bfloat16)

def reference(dec_rows, kv_cache, lengths, dest_group, dest_slot, score_rows, doc_ids, norm_gain, query_gain, key_gain, w_query, w_keyval, w_out):
    groups = dec_rows.shape[0] // R_DEV

    def one_group(packed):
        rows, cache, lens = packed
        return decode_block(rows, cache, lens, norm_gain, query_gain, key_gain, w_query, w_keyval, w_out)
    new_rows, new_cache = lax.map(one_group, (dec_rows.reshape(groups, R_DEV, -1), kv_cache.reshape((groups, R_DEV) + kv_cache.shape[1:]), lengths.reshape(groups, R_DEV)))
    new_rows = new_rows.reshape(dec_rows.shape)
    new_cache = new_cache.reshape(kv_cache.shape)
    target = (dest_group * R_DEV + dest_slot).astype(jnp.int32)
    source = jnp.zeros(target.shape, jnp.int32).at[target].set(jnp.arange(target.shape[0], dtype=jnp.int32))
    dec_out = jnp.take(new_rows, source, axis=0)
    dec_cache = jnp.take(new_cache, source, axis=0)

    def one_pack(packed):
        rows, docs = packed
        return score_block(rows, docs, norm_gain, query_gain, key_gain, w_query, w_keyval, w_out)
    score_out = lax.map(one_pack, (score_rows.reshape(groups, -1, score_rows.shape[1]), doc_ids))
    score_out = score_out.reshape(score_rows.shape)
    return (dec_out, dec_cache, score_out)
```

```python
import functools
import math

import jax
import jax.numpy as jnp
from jax import lax
from jax.experimental import pallas as pl
from jax.experimental.pallas import tpu as pltpu
from jax.sharding import PartitionSpec as P

HD = 128
EPS = 1e-06
MESH = pl.DeviceIdType.MESH
BF = jnp.bfloat16
F32 = jnp.float32
LOW = -1e30
INV = 1.0 / math.sqrt(HD)

D = 5120
CTX = 768
NG = 16
NT = 8
R = 14
RP = 16
SH = 56
SP = 64
TOK = NT * SP
HALF = D // 2
QUART = D // 4
SL = D // NT
MSG = SL + 4 * HD


def head_norm(vectors, gain):
    mean = jnp.mean(vectors * vectors, axis=-1, keepdims=True)
    return (vectors * lax.rsqrt(mean + EPS) * gain).astype(BF)


def dot(a, b):
    return jnp.dot(a, b, preferred_element_type=F32)


def dot_t(a, b):
    return lax.dot_general(a, b, (((1,), (1,)), ((), ())), preferred_element_type=F32)


def main_kernel(
    dest_ref, slot_ref, len_ref,
    dec_ref, score_ref, gain_ref, qgain_ref, kgain_ref, doc_ref,
    cache_hbm, wq_hbm, wkv_hbm, wo_hbm,
    got_ref, patch_ref, plan_ref, dec_out_ref, score_out_ref,
    cache, wkv, wqkv, wo, xin, docr_ref, docc_ref, packed, xg, xn, sc, qs, kt, vs, terms,
    relay, arrive, cross, score_sum, part, gather_part, xbuf, nx, scores, pick, fin, obuf,
    load_sem, a2a_send, a2a_recv, ag_send, ag_recv, rs_send, rs_recv,
    dp_send, dp_recv, dx_send, dx_recv, fin_send, fin_recv, o_send, o_recv,
):
    g = lax.axis_index("group")
    t = lax.axis_index("tp")
    y, h = t // 2, t % 2
    z, xl, core = g // 4, (g // 2) % 2, g % 2
    oh = 1 - h
    up, down, far = (y + 1) % 4, (y + 3) % 4, (y + 2) % 4
    mine, partner = t, y * 2 + oh
    to_up, to_down, to_x = {"tp": up * 2 + h}, {"tp": down * 2 + h}, {"tp": partner}

    def remote(src, dst, send, recv, device):
        return pltpu.make_async_remote_copy(
            src_ref=src, dst_ref=dst, send_sem=send, recv_sem=recv,
            device_id=device, device_id_type=MESH,
        )

    loads = [
        pltpu.make_async_copy(cache_hbm, cache, load_sem.at[0]),
        pltpu.make_async_copy(wq_hbm, wqkv.at[:, pl.ds(0, 512)], load_sem.at[1]),
        pltpu.make_async_copy(wkv_hbm, wkv, load_sem.at[2]),
        pltpu.make_async_copy(wo_hbm, wo, load_sem.at[3]),
    ]
    for load in loads:
        load.start()

    barrier = pltpu.get_barrier_semaphore()

    def greet_tp(k, c):
        pl.semaphore_signal(barrier, inc=1, device_id={"tp": (t + k) % NT}, device_id_type=MESH)
        return c

    def greet_group(k, c):
        pl.semaphore_signal(barrier, inc=1, device_id={"group": (g + k) % NG}, device_id_type=MESH)
        return c

    lax.fori_loop(1, NT, greet_tp, 0)
    lax.fori_loop(1, NG, greet_group, 0)

    for a in range(2):
        lo = score_ref[:, a * HALF : a * HALF + QUART].astype(F32)
        hi = score_ref[:, a * HALF + QUART : (a + 1) * HALF].astype(F32)
        xg[mine, a] = jnp.concatenate([lo, hi], axis=0).astype(BF)

    xin[...] = jnp.zeros_like(xin)
    xin[0:R, :] = dec_ref[...].astype(F32)
    token = lax.broadcasted_iota(jnp.int32, (TOK, NT * SH), 1)
    place = lax.broadcasted_iota(jnp.int32, (TOK, NT * SH), 0)
    inside = (place & (SP - 1)) < SH
    spread = ((place - (place >> 6) * (SP - SH) == token) & inside).astype(F32).astype(BF)
    ids = jnp.broadcast_to(doc_ref[...].astype(F32) + 1.0, (HD, NT * SH)).astype(BF)
    docr_ref[...] = dot_t(ids[:16], spread)
    docc_ref[...] = dot_t(spread, ids)

    lane = lax.broadcasted_iota(jnp.int32, (RP, NG * RP), 1)
    slot_row = lax.broadcasted_iota(jnp.int32, (RP, NG * RP), 0)

    def wanted(e, c):
        want, span = c
        for r in range(R):
            here = jnp.where(dest_ref[e * R + r] == g, slot_ref[e * R + r], -1)
            spot = lane == e * RP + r
            want = jnp.where(spot, here, want)
            span = jnp.where(spot, len_ref[e * R + r], span)
        return want, span

    none = jnp.full((RP, NG * RP), -1, jnp.int32)
    want, span = lax.fori_loop(0, NG, wanted, (none, jnp.zeros_like(none)))
    pick[...] = (want == slot_row).astype(F32).astype(BF)
    source = jnp.sum(jnp.where(want == slot_row, lane >> 4, 0), axis=-1, keepdims=True)
    length = jnp.sum(jnp.where(want == slot_row, span, 0), axis=-1, keepdims=True)
    plan_lane = lax.broadcasted_iota(jnp.int32, (RP, HD), 1)
    plan_ref[...] = jnp.where(plan_lane == 0, source, length)

    pl.semaphore_wait(barrier, NT - 1 + NG - 1)

    def ag(i, shard, a, device):
        where = xg.at[shard, a]
        return remote(where, where, ag_send.at[i], ag_recv.at[i], device)

    first = [ag(a, mine, a, to_up) for a in range(2)]
    first += [ag(2 + a, mine, a, to_down) for a in range(2)]
    first += [ag(4 + a, mine, a, to_x) for a in range(2)]
    for c in (first[4], first[0], first[3], first[1], first[2]):
        c.start()
    second = [ag(6 + a, partner, a, to_up) for a in range(2)]
    second += [ag(8 + a, partner, a, to_down) for a in range(2)]
    fwd_up = [ag(10, down * 2 + h, 0, to_up), ag(12, down * 2 + oh, 0, to_up)]
    fwd_down = [ag(11, up * 2 + h, 1, to_down), ag(13, up * 2 + oh, 1, to_down)]

    def a2a(j):
        dz, dx, dc = j // 4, (j // 2) % 2, j % 2
        target = ((z + dz) % 4) * 4 + ((xl + dx) % 2) * 2 + (core + dc) % 2
        copy = remote(packed.at[j], got_ref.at[g], a2a_send.at[j], a2a_recv.at[j], {"group": target})
        return target, copy

    def fill(j, target):
        row = 0
        for r in range(1, R):
            row = jnp.where(dest_ref[g * R + r] == target, r, row)
        for kv in range(2):
            packed[j, kv] = cache[row, kv]

    def send_cache(dx, i):
        j = (i // 2) * 4 + dx * 2 + i % 2
        target, copy = a2a(j)
        fill(j, target)
        copy.start()

    loads[0].wait()
    send_cache(1, 0)
    send_cache(0, 1)
    fill(0, g)
    own_copy = pltpu.make_async_copy(packed.at[0], got_ref.at[g], a2a_send.at[0])
    own_copy.start()

    row_of = lax.broadcasted_iota(jnp.int32, (4 * RP, HD), 0) & (RP - 1)
    column_row = lax.broadcasted_iota(jnp.int32, (HD, 4 * RP), 1) & (RP - 1)
    lens = jnp.ones((4 * RP, HD), jnp.int32)
    for r in range(R):
        lens = jnp.where(row_of == r, len_ref[g * R + r], lens)
    cached = lax.broadcasted_iota(jnp.int32, (4 * RP, CTX), 1) < lens[:, 0:1]

    def stack4(v):
        return jnp.concatenate([v] * 4, axis=0)

    def dec_project(step, x):
        wide = x.astype(F32)
        scale = lax.rsqrt(jnp.mean(wide * wide, axis=-1, keepdims=True) + EPS)
        nx[...] = (wide * gain_ref[...]).astype(BF)

        def chunk(k, acc):
            cols = pl.ds(pl.multiple_of(k * 1024, 1024), 1024)
            return acc + dot(nx[:, cols], wqkv[cols, :])

        proj = lax.fori_loop(0, 5, chunk, jnp.zeros((RP, 768), F32)) * scale
        q = jnp.concatenate([proj[:, i * HD : (i + 1) * HD] for i in range(4)], axis=0)
        q = head_norm(q, qgain_ref[...])
        return q, (head_norm(proj[:, 512:640], kgain_ref[...]), proj[:, 640:768].astype(BF))

    def dec_weights(q, new):
        qf = q.astype(F32)
        qt = qf.T.astype(BF)

        def chunk(n, c):
            spots = pl.ds(pl.multiple_of(n * HD, HD), HD)
            acc = jnp.zeros((HD, 4 * RP), F32)
            for r in range(R):
                acc = jnp.where(column_row == r, dot(cache[r, 0, spots, :], qt), acc)
            scores[:, spots] = acc.T
            return c

        lax.fori_loop(0, CTX // HD, chunk, 0)
        s = jnp.where(cached, scores[...] * INV, LOW)
        fresh = [
            jnp.sum(qf * stack4(k.astype(F32)), axis=-1, keepdims=True) * INV for k, _ in new
        ]
        top = functools.reduce(jnp.maximum, fresh, jnp.max(s, axis=-1, keepdims=True))
        e = jnp.exp(s - top)
        ef = [jnp.exp(f - top) for f in fresh]
        total = functools.reduce(jnp.add, ef, jnp.sum(e, axis=-1, keepdims=True))
        inv = 1.0 / total
        return (e * inv).astype(BF), [(f * inv).astype(BF).astype(F32) for f in ef]

    def dec_out(step, w, wf, new):
        def value_row(r, acc):
            return acc + jnp.where(row_of == r, dot(w, cache[r, 1]), 0.0)

        o = lax.fori_loop(0, R, value_row, jnp.zeros((4 * RP, HD), F32), unroll=True)
        for f, (_, v) in zip(wf, new):
            o = o + f * stack4(v.astype(F32))
        o = o.astype(BF)
        o = jnp.concatenate([o[i * RP : (i + 1) * RP] for i in range(4)], axis=1)

        def out_slice(p, c):
            part[step, p] = dot(o, wo[:, pl.ds(pl.multiple_of(p * SL, SL), SL)])
            return c

        lax.fori_loop(0, NT, out_slice, 0)
        lax.fori_loop(1, NT, lambda k, c: (part_copy(step, k).start(), c)[1], 0)

    def part_copy(step, k):
        peer = (t + k) % NT
        return remote(
            part.at[step, peer], gather_part.at[step, t],
            dp_send.at[step, k], dp_recv.at[step, k], {"tp": peer},
        )

    def reduce_parts(step, base):
        lax.fori_loop(1, NT, lambda k, c: (part_copy(step, k).wait_recv(), c)[1], 0)
        total = lax.fori_loop(
            1, NT, lambda k, acc: acc + gather_part[step, (t + k) % NT], part[step, t]
        )
        return (base.astype(F32) + total).astype(BF)

    def x_copy(k):
        return remote(xbuf.at[t], xbuf.at[t], dx_send.at[k], dx_recv.at[k], {"tp": (t + k) % NT})

    loads[2].wait()
    to_row = lax.broadcasted_iota(jnp.int32, (256, 256), 0)
    from_row = lax.broadcasted_iota(jnp.int32, (256, 256), 1)
    parting = (from_row == 2 * (to_row & (HD - 1)) + (to_row >= HD).astype(jnp.int32)).astype(F32).astype(BF)

    def part_rows(b, c):
        both = dot(parting, wkv[pl.ds(pl.multiple_of(b * 256, 256), 256), :]).astype(BF)
        rows = pl.ds(pl.multiple_of(b * HD, HD), HD)
        wqkv[rows, 512:640] = both[:HD]
        wqkv[rows, 640:768] = both[HD:]
        return c

    lax.fori_loop(0, D // HD, part_rows, 0, unroll=8)

    def prepare(p, c):
        total = jnp.zeros((SH, 1), F32)
        rows = pl.ds(pl.multiple_of(p * SP, SP), SP)
        for a in range(2):
            both = xg[p, a].astype(F32)
            for i in range(2):
                x = both[i * SH : (i + 1) * SH]
                total = total + jnp.sum(x * x, axis=-1, keepdims=True)
                start = a * HALF + i * QUART
                n = x * gain_ref[:, start : start + QUART]
                n = jnp.concatenate([n, jnp.zeros((SP - SH, QUART), F32)], axis=0)
                xn[rows, start : start + QUART] = n.astype(BF)
        scale = lax.rsqrt(total / D + EPS)
        scale = jnp.concatenate([scale, jnp.zeros((SP - SH, 1), F32)], axis=0)
        sc[rows, :] = jnp.broadcast_to(scale, (SP, HD))
        return c

    def project(block):
        rows = pl.ds(pl.multiple_of(block * 2 * SP, 2 * SP), 2 * SP)

        def tile(j):
            return dot(xn[rows, :], wqkv[:, j * 256 : (j + 1) * 256]) * sc[rows, 0:1]

        for j in range(2):
            v = tile(j)
            for i in range(2):
                qs[2 * j + i, rows, :] = head_norm(v[:, i * HD : (i + 1) * HD], qgain_ref[...])
        v = tile(2)
        k = head_norm(v[:, :HD], kgain_ref[...])
        kt[:, rows] = k.astype(F32).T.astype(BF)
        vs[rows, :] = v[:, HD:].astype(BF)

    loads[1].wait()
    q0, new0 = dec_project(0, xin[...])
    first[4].wait_send()
    first[5].start()
    send_cache(0, 2)
    send_cache(1, 1)
    w0, wf0 = dec_weights(q0, [new0])
    first[4].wait_recv()
    second[0].start()
    second[2].start()
    first[0].wait_recv()
    fwd_up[0].start()
    first[3].wait_recv()
    fwd_down[0].start()
    send_cache(1, 2)
    send_cache(0, 3)
    loads[3].wait()
    dec_out(0, w0, wf0, [new0])
    first[5].wait_recv()
    second[3].start()
    second[1].start()
    prepare(mine, 0)
    prepare(partner, 0)
    project(y)
    send_cache(1, 3)
    send_cache(0, 4)
    second[0].wait_recv()
    fwd_up[1].start()
    second[3].wait_recv()
    fwd_down[1].start()

    base0 = xin[:, pl.ds(pl.multiple_of(t * SL, SL), SL)]
    xbuf[t] = reduce_parts(0, base0)
    lax.fori_loop(1, NT, lambda k, c: (x_copy(k).start(), c)[1], 0)

    first[1].wait_recv()
    prepare(down * 2 + h, 0)
    first[2].wait_recv()
    prepare(up * 2 + h, 0)
    send_cache(1, 4)
    send_cache(0, 5)
    second[1].wait_recv()
    prepare(down * 2 + oh, 0)
    project(down)
    lax.fori_loop(1, NT, lambda k, c: (x_copy(k).wait_recv(), c)[1], 0)
    q1, new1 = dec_project(1, jnp.concatenate([xbuf[p] for p in range(NT)], axis=1))
    second[2].wait_recv()
    prepare(up * 2 + oh, 0)
    project(up)
    send_cache(1, 5)
    send_cache(0, 6)
    w1, wf1 = dec_weights(q1, [new0, new1])
    fwd_up[0].wait_recv()
    fwd_down[0].wait_recv()
    prepare(far * 2 + h, 0)
    fwd_up[1].wait_recv()
    fwd_down[1].wait_recv()
    prepare(far * 2 + oh, 0)
    project(far)
    send_cache(1, 6)

    later_col = lax.broadcasted_iota(jnp.int32, (2 * SP, TOK), 1)
    later_row = lax.broadcasted_iota(jnp.int32, (2 * SP, TOK), 0)

    def attend(block):
        rows = pl.ds(pl.multiple_of(block * 2 * SP, 2 * SP), 2 * SP)
        live = (docc_ref[rows, 0:1] == docr_ref[0:1, :]) & (later_col <= later_row + block * (2 * SP))
        heads = []
        for i in range(4):
            s = jnp.where(live, dot(qs[i, rows, :], kt[...]) * INV, LOW)
            e = jnp.exp(s - jnp.max(s, axis=-1, keepdims=True))
            inv = 1.0 / jnp.sum(e, axis=-1, keepdims=True)
            heads.append(dot((e * inv).astype(BF), vs[...]).astype(BF))
        attn = jnp.concatenate(heads, axis=1)
        for a in range(2):
            def columns(j, c):
                start = pl.multiple_of(a * HALF + j * 640, 640)
                lo = dot(attn, wo[:, pl.ds(start, 640)])
                hi = dot(attn, wo[:, pl.ds(pl.multiple_of(start + QUART, 640), 640)])
                for i in range(2):
                    pair = [v[i * SP : i * SP + SH] for v in (lo, hi)]
                    cols = pl.ds(pl.multiple_of(j * 640, 640), 640)
                    terms[block * 2 + i, a, :, cols] = jnp.concatenate(pair, axis=0).astype(BF)
                return c

            lax.fori_loop(0, 2, columns, 0)

    order = (oh, h)

    def rs(n, src, dst, device):
        return remote(src, dst, rs_send.at[n], rs_recv.at[n], device)

    far_up = [rs(i, terms.at[far * 2 + order[i], 0], relay.at[0, i], to_up) for i in range(2)]
    far_down = [rs(2 + i, terms.at[far * 2 + order[i], 1], relay.at[1, i], to_down) for i in range(2)]
    near_up = [
        [rs(4 + 2 * i + a, terms.at[up * 2 + order[i], a], arrive.at[0, i, a], to_up) for a in range(2)]
        for i in range(2)
    ]
    near_down = [
        [rs(8 + 2 * i + a, terms.at[down * 2 + order[i], a], arrive.at[1, i, a], to_down) for a in range(2)]
        for i in range(2)
    ]
    over = [rs(12 + a, cross.at[0, a], cross.at[1, a], to_x) for a in range(2)]

    def relay_up(i):
        far_up[i].wait_recv()
        spot = up * 2 + order[i]
        terms[spot, 0] = (terms[spot, 0].astype(F32) + relay[0, i].astype(F32)).astype(BF)
        near_up[i][0].start()

    def relay_down(i):
        far_down[i].wait_recv()
        spot = down * 2 + order[i]
        terms[spot, 1] = (terms[spot, 1].astype(F32) + relay[1, i].astype(F32)).astype(BF)
        near_down[i][1].start()

    def summed(i, a):
        near_up[i][a].wait_recv()
        near_down[i][a].wait_recv()
        return (
            terms[y * 2 + order[i], a].astype(F32)
            + arrive[0, i, a].astype(F32)
            + arrive[1, i, a].astype(F32)
        )

    attend(far)
    far_up[0].start()
    far_down[0].start()
    attend(up)
    near_up[0][1].start()
    send_cache(1, 7)
    attend(down)
    near_down[0][0].start()
    relay_up(0)
    relay_down(0)
    far_up[1].start()
    far_down[1].start()
    dec_out(1, w1, wf1, [new0, new1])
    attend(y)
    send_cache(0, 7)

    near_up[0][1].wait_send()
    near_up[1][1].start()
    near_down[0][0].wait_send()
    near_down[1][0].start()
    relay_up(1)
    relay_down(1)

    mine_rows = pl.ds(pl.multiple_of(g * RP, RP), RP)
    fin[mine_rows, 0:SL] = reduce_parts(1, xbuf[t])
    for i, (k, v) in enumerate([new0, new1]):
        start = SL + 2 * i * HD
        fin[mine_rows, start : start + HD] = k
        fin[mine_rows, start + HD : start + 2 * HD] = v

    def fin_copy(k):
        where = fin.at[mine_rows]
        return remote(where, where, fin_send.at[k], fin_recv.at[k], {"group": (g + k) % NG})

    lax.fori_loop(1, NG, lambda k, c: (fin_copy(k).start(), c)[1], 0)

    for a in range(2):
        cross[0, a] = summed(0, a).astype(BF)
        over[a].start()

    for a in range(2):
        near = summed(1, a)
        for i in range(2):
            cols = slice(a * HALF + i * QUART, a * HALF + (i + 1) * QUART)
            add = near[i * SH : (i + 1) * SH]
            score_sum[:, cols] = score_ref[:, cols].astype(F32) + add

    lax.fori_loop(1, NG, lambda k, c: (fin_copy(k).wait_recv(), c)[1], 0)
    placed = dot(pick[...], fin[...])
    obuf[t] = placed[:, :SL].astype(BF)
    patch_ref[...] = placed[:, SL:]

    def o_copy(k):
        return remote(obuf.at[t], obuf.at[t], o_send.at[k], o_recv.at[k], {"tp": (t + k) % NT})

    lax.fori_loop(1, NT, lambda k, c: (o_copy(k).start(), c)[1], 0)

    for a in range(2):
        over[a].wait_recv()
        far_half = cross[1, a].astype(F32)
        for i in range(2):
            cols = slice(a * HALF + i * QUART, a * HALF + (i + 1) * QUART)
            add = far_half[i * SH : (i + 1) * SH]
            score_out_ref[:, cols] = (score_sum[:, cols] + add).astype(BF)

    lax.fori_loop(1, NT, lambda k, c: (o_copy(k).wait_recv(), c)[1], 0)
    for p in range(NT):
        dec_out_ref[:, p * SL : (p + 1) * SL] = obuf[p]

    def end_a2a(j, c):
        a2a(j)[1].wait()
        return c

    lax.fori_loop(1, NG, end_a2a, 0)
    own_copy.wait()
    ended = first[:4] + first[5:] + second + fwd_up + fwd_down + far_up + far_down + over
    ended += near_up[1] + near_down[1] + [near_up[0][0], near_down[0][1]]
    for c in ended:
        c.wait_send()

    def end_tp(k, c):
        part_copy(0, k).wait_send()
        part_copy(1, k).wait_send()
        x_copy(k).wait_send()
        o_copy(k).wait_send()
        return c

    lax.fori_loop(1, NT, end_tp, 0)
    lax.fori_loop(1, NG, lambda k, c: (fin_copy(k).wait_send(), c)[1], 0)


def place_kernel(
    plan_ref, patch_ref, dec_ref, got_hbm, score_hbm,
    dec_out_ref, cache_out, score_out, rows, score_rows, in_sem, out_sem, score_sem,
):
    score_in = pltpu.make_async_copy(score_hbm, score_rows, score_sem.at[0])
    score_end = pltpu.make_async_copy(score_rows, score_out, score_sem.at[1])
    score_in.start()

    def get(s, c):
        pltpu.make_async_copy(got_hbm.at[plan_ref[s, 0]], rows.at[s], in_sem.at[s]).start()
        return c

    lax.fori_loop(0, R, get, 0)
    dec_out_ref[...] = dec_ref[:R, :]
    score_in.wait()
    score_end.start()

    def put(s, c):
        pltpu.make_async_copy(got_hbm.at[0], rows.at[s], in_sem.at[s]).wait()
        entry = patch_ref[pl.ds(s, 1), :]
        for step in range(2):
            pos = plan_ref[s, 1] + step
            base = pl.multiple_of((pos // 16) * 16, 16)
            here = lax.broadcasted_iota(jnp.int32, (16, HD), 0) == pos - base
            for kv in range(2):
                start = (2 * step + kv) * HD
                old = rows[s, kv, pl.ds(base, 16), :].astype(F32)
                both = jnp.where(here, entry[:, start : start + HD], old)
                rows[s, kv, pl.ds(base, 16), :] = both.astype(BF)
        pltpu.make_async_copy(rows.at[s], cache_out.at[s], out_sem.at[s]).start()
        return c

    lax.fori_loop(0, R, put, 0)

    def end(s, c):
        pltpu.make_async_copy(rows.at[s], cache_out.at[s], out_sem.at[s]).wait()
        return c

    lax.fori_loop(0, R, end, 0)
    score_end.wait()


def per_device(
    dec_rows, kv_cache, lengths, dest_group, dest_slot, score_rows, doc_ids,
    norm_gain, query_gain, key_gain, w_query, w_keyval, w_out,
):
    smem = pl.BlockSpec(memory_space=pltpu.SMEM)
    vmem = pl.BlockSpec(memory_space=pltpu.VMEM)
    hbm = pl.BlockSpec(memory_space=pl.ANY)
    dma = pltpu.SemaphoreType.DMA
    got, patch, plan, dec_out16, score_sum = pl.pallas_call(
        main_kernel,
        name="decode_and_score",
        out_shape=(
            jax.ShapeDtypeStruct((NG, 2, CTX, HD), BF),
            jax.ShapeDtypeStruct((RP, 4 * HD), F32),
            jax.ShapeDtypeStruct((RP, HD), jnp.int32),
            jax.ShapeDtypeStruct((RP, D), BF),
            jax.ShapeDtypeStruct((SH, D), BF),
        ),
        in_specs=[smem] * 3 + [vmem] * 6 + [hbm] * 4,
        out_specs=(hbm, vmem, vmem, vmem, vmem),
        scratch_shapes=[
            pltpu.VMEM((R, 2, CTX, HD), BF),
            pltpu.VMEM((2 * D, HD), BF),
            pltpu.VMEM((D, 768), BF),
            pltpu.VMEM((512, D), BF),
            pltpu.VMEM((RP, D), F32),
            pltpu.VMEM((16, TOK), F32),
            pltpu.VMEM((TOK, HD), F32),
            pltpu.VMEM((NG, 2, CTX, HD), BF),
            pltpu.VMEM((NT, 2, 2 * SH, QUART), BF),
            pltpu.VMEM((TOK, D), BF),
            pltpu.VMEM((TOK, HD), F32),
            pltpu.VMEM((4, TOK, HD), BF),
            pltpu.VMEM((HD, TOK), BF),
            pltpu.VMEM((TOK, HD), BF),
            pltpu.VMEM((NT, 2, 2 * SH, QUART), BF),
            pltpu.VMEM((2, 2, 2 * SH, QUART), BF),
            pltpu.VMEM((2, 2, 2, 2 * SH, QUART), BF),
            pltpu.VMEM((2, 2, 2 * SH, QUART), BF),
            pltpu.VMEM((SH, D), F32),
            pltpu.VMEM((2, NT, RP, SL), F32),
            pltpu.VMEM((2, NT, RP, SL), F32),
            pltpu.VMEM((NT, RP, SL), BF),
            pltpu.VMEM((RP, D), BF),
            pltpu.VMEM((4 * RP, CTX), F32),
            pltpu.VMEM((RP, NG * RP), BF),
            pltpu.VMEM((NG * RP, MSG), BF),
            pltpu.VMEM((NT, RP, SL), BF),
            dma((4,)), dma((NG,)), dma((NG,)), dma((14,)), dma((14,)), dma((14,)), dma((14,)),
            dma((2, NT)), dma((2, NT)), dma((NT,)), dma((NT,)), dma((NG,)), dma((NG,)),
            dma((NT,)), dma((NT,)),
        ],
        compiler_params=pltpu.CompilerParams(
            collective_id=0, has_side_effects=True, vmem_limit_bytes=60 * 1024 * 1024
        ),
        cost_estimate=pl.CostEstimate(flops=8 * 10**9, bytes_accessed=30 * 10**6, transcendentals=10**6),
    )(
        dest_group, dest_slot, lengths, dec_rows, score_rows, norm_gain.reshape(1, D),
        query_gain.reshape(1, HD), key_gain.reshape(1, HD), doc_ids,
        kv_cache, w_query, w_keyval.reshape(2 * D, HD), w_out,
    )
    return pl.pallas_call(
        place_kernel,
        name="place_rows",
        out_shape=(
            jax.ShapeDtypeStruct((R, D), BF),
            jax.ShapeDtypeStruct((R, 2, CTX, HD), BF),
            jax.ShapeDtypeStruct((SH, D), BF),
        ),
        in_specs=[smem] + [vmem] * 2 + [hbm] * 2,
        out_specs=(vmem, hbm, hbm),
        scratch_shapes=[
            pltpu.VMEM((R, 2, CTX, HD), BF),
            pltpu.VMEM((SH, D), BF),
            dma((R,)), dma((R,)), dma((2,)),
        ],
        compiler_params=pltpu.CompilerParams(vmem_limit_bytes=60 * 1024 * 1024),
        cost_estimate=pl.CostEstimate(flops=10**6, bytes_accessed=12 * 10**6, transcendentals=0),
    )(plan, patch, dec_out16, got, score_sum)


def solution(mesh):
    placed = (
        P("group", None),
        P("group", None, None, "tp"),
        P(),
        P(),
        P(),
        P(("group", "tp"), None),
        P("group", None),
        P(),
        P(),
        P(),
        P(None, "tp"),
        P(None, None, "tp"),
        P("tp", None),
    )
    return jax.shard_map(
        per_device,
        mesh=mesh,
        in_specs=placed,
        out_specs=(P("group", None), P("group", None, None, "tp"), P(("group", "tp"), None)),
        check_vma=False,
    )
```

```python
import functools
import math

import jax
import jax.numpy as jnp
from jax import lax
from jax.experimental import pallas as pl
from jax.experimental.pallas import tpu as pltpu
from jax.sharding import PartitionSpec as P

HD = 128
EPS = 1e-06
MESH = pl.DeviceIdType.MESH
BF = jnp.bfloat16
F32 = jnp.float32
LOW = -1e30
INV = 1.0 / math.sqrt(HD)

D = 5120
CTX = 768
NG = 16
NT = 8
R = 14
RP = 16
SH = 56
SP = 64
TOK = NT * SP
HALF = D // 2
QUART = D // 4
SL = D // NT
MSG = SL + 4 * HD


def head_norm(vectors, gain):
    mean = jnp.mean(vectors * vectors, axis=-1, keepdims=True)
    return (vectors * lax.rsqrt(mean + EPS) * gain).astype(BF)


def dot(a, b):
    return jnp.dot(a, b, preferred_element_type=F32)


def dot_t(a, b):
    return lax.dot_general(a, b, (((1,), (1,)), ((), ())), preferred_element_type=F32)


def main_kernel(
    dest_ref, slot_ref, len_ref,
    dec_ref, score_ref, gain_ref, qgain_ref, kgain_ref, doc_ref,
    cache_hbm, wq_hbm, wkv_hbm, wo_hbm,
    got_ref, patch_ref, plan_ref, dec_out_ref, score_out_ref,
    cache, wkv, wqkv, wo, xin, docr_ref, docc_ref, packed, xg, xn, sc, qs, kt, vs, terms,
    relay, arrive, cross, score_sum, part, gather_part, xbuf, nx, scores, pick, fin, obuf,
    load_sem, a2a_send, a2a_recv, ag_send, ag_recv, rs_send, rs_recv,
    dp_send, dp_recv, dx_send, dx_recv, fin_send, fin_recv, o_send, o_recv,
):
    g = lax.axis_index("group")
    t = lax.axis_index("tp")
    y, h = t // 2, t % 2
    z, xl, core = g // 4, (g // 2) % 2, g % 2
    oh = 1 - h
    up, down, far = (y + 1) % 4, (y + 3) % 4, (y + 2) % 4
    mine, partner = t, y * 2 + oh
    to_up, to_down, to_x = {"tp": up * 2 + h}, {"tp": down * 2 + h}, {"tp": partner}

    def remote(src, dst, send, recv, device):
        return pltpu.make_async_remote_copy(
            src_ref=src, dst_ref=dst, send_sem=send, recv_sem=recv,
            device_id=device, device_id_type=MESH,
        )

    loads = [
        pltpu.make_async_copy(cache_hbm, cache, load_sem.at[0]),
        pltpu.make_async_copy(wq_hbm, wqkv.at[:, pl.ds(0, 512)], load_sem.at[1]),
        pltpu.make_async_copy(wkv_hbm, wkv, load_sem.at[2]),
        pltpu.make_async_copy(wo_hbm, wo, load_sem.at[3]),
    ]
    for load in loads:
        load.start()

    barrier = pltpu.get_barrier_semaphore()

    def greet_tp(k, c):
        pl.semaphore_signal(barrier, inc=1, device_id={"tp": (t + k) % NT}, device_id_type=MESH)
        return c

    def greet_group(k, c):
        pl.semaphore_signal(barrier, inc=1, device_id={"group": (g + k) % NG}, device_id_type=MESH)
        return c

    lax.fori_loop(1, NT, greet_tp, 0)
    lax.fori_loop(1, NG, greet_group, 0)

    for a in range(2):
        lo = score_ref[:, a * HALF : a * HALF + QUART].astype(F32)
        hi = score_ref[:, a * HALF + QUART : (a + 1) * HALF].astype(F32)
        xg[mine, a] = jnp.concatenate([lo, hi], axis=0).astype(BF)

    pl.semaphore_wait(barrier, NT - 1 + NG - 1)

    def ag(i, where, device):
        return remote(where, where, ag_send.at[i], ag_recv.at[i], device)

    over_x = ag(0, xg.at[mine], to_x)
    first_up, first_down = ag(1, xg.at[mine], to_up), ag(2, xg.at[mine], to_down)
    for c in (over_x, first_up, first_down):
        c.start()
    second_up, second_down = ag(3, xg.at[partner], to_up), ag(4, xg.at[partner], to_down)
    fwd_up = [ag(5 + i, xg.at[down * 2 + hh, 0], to_up) for i, hh in enumerate((h, oh))]
    fwd_down = [ag(7 + i, xg.at[up * 2 + hh, 1], to_down) for i, hh in enumerate((h, oh))]

    def a2a(j):
        dz, dx, dc = j // 4, (j // 2) % 2, j % 2
        target = ((z + dz) % 4) * 4 + ((xl + dx) % 2) * 2 + (core + dc) % 2
        copy = remote(packed.at[j], got_ref.at[g], a2a_send.at[j], a2a_recv.at[j], {"group": target})
        return target, copy

    def fill(j, target):
        row = 0
        for r in range(1, R):
            row = jnp.where(dest_ref[g * R + r] == target, r, row)
        for kv in range(2):
            packed[j, kv] = cache[row, kv]

    def send_caches(along, across=()):
        for dx, some in ((1, across), (0, along)):
            for i in some:
                j = (i // 2) * 4 + dx * 2 + i % 2
                target, copy = a2a(j)
                fill(j, target)
                copy.start()

    loads[0].wait()
    send_caches((1, 2, 6))
    fill(0, g)
    own_copy = pltpu.make_async_copy(packed.at[0], got_ref.at[g], a2a_send.at[0])
    own_copy.start()

    xin[...] = jnp.zeros_like(xin)
    xin[0:R, :] = dec_ref[...].astype(F32)
    token = lax.broadcasted_iota(jnp.int32, (TOK, NT * SH), 1)
    place = lax.broadcasted_iota(jnp.int32, (TOK, NT * SH), 0)
    inside = (place & (SP - 1)) < SH
    spread = ((place - (place >> 6) * (SP - SH) == token) & inside).astype(F32).astype(BF)
    ids = jnp.broadcast_to(doc_ref[...].astype(F32) + 1.0, (HD, NT * SH)).astype(BF)
    docr_ref[...] = dot_t(ids[:16], spread)
    docc_ref[...] = dot_t(spread, ids)

    lane = lax.broadcasted_iota(jnp.int32, (RP, NG * RP), 1)
    slot_row = lax.broadcasted_iota(jnp.int32, (RP, NG * RP), 0)

    def wanted(e, c):
        want, span = c
        for r in range(R):
            here = jnp.where(dest_ref[e * R + r] == g, slot_ref[e * R + r], -1)
            spot = lane == e * RP + r
            want = jnp.where(spot, here, want)
            span = jnp.where(spot, len_ref[e * R + r], span)
        return want, span

    none = jnp.full((RP, NG * RP), -1, jnp.int32)
    want, span = lax.fori_loop(0, NG, wanted, (none, jnp.zeros_like(none)))
    pick[...] = (want == slot_row).astype(F32).astype(BF)
    source = jnp.sum(jnp.where(want == slot_row, lane >> 4, 0), axis=-1, keepdims=True)
    length = jnp.sum(jnp.where(want == slot_row, span, 0), axis=-1, keepdims=True)
    plan_lane = lax.broadcasted_iota(jnp.int32, (RP, HD), 1)
    plan_ref[...] = jnp.where(plan_lane == 0, source, length)

    row_of = lax.broadcasted_iota(jnp.int32, (4 * RP, HD), 0) & (RP - 1)
    column_row = lax.broadcasted_iota(jnp.int32, (HD, 4 * RP), 1) & (RP - 1)
    lens = jnp.ones((4 * RP, HD), jnp.int32)
    for r in range(R):
        lens = jnp.where(row_of == r, len_ref[g * R + r], lens)
    cached = lax.broadcasted_iota(jnp.int32, (4 * RP, CTX), 1) < lens[:, 0:1]

    def stack4(v):
        return jnp.concatenate([v] * 4, axis=0)

    def dec_project(step, x):
        wide = x.astype(F32)
        scale = lax.rsqrt(jnp.mean(wide * wide, axis=-1, keepdims=True) + EPS)
        nx[...] = (wide * gain_ref[...]).astype(BF)

        def chunk(k, acc):
            cols = pl.ds(pl.multiple_of(k * 1024, 1024), 1024)
            return acc + dot(nx[:, cols], wqkv[cols, :])

        proj = lax.fori_loop(0, 5, chunk, jnp.zeros((RP, 768), F32)) * scale
        q = jnp.concatenate([proj[:, i * HD : (i + 1) * HD] for i in range(4)], axis=0)
        q = head_norm(q, qgain_ref[...])
        return q, (head_norm(proj[:, 512:640], kgain_ref[...]), proj[:, 640:768].astype(BF))

    def dec_weights(q, new):
        qf = q.astype(F32)
        qt = qf.T.astype(BF)

        def chunk(n, c):
            spots = pl.ds(pl.multiple_of(n * HD, HD), HD)
            acc = jnp.zeros((HD, 4 * RP), F32)
            for r in range(R):
                acc = jnp.where(column_row == r, dot(cache[r, 0, spots, :], qt), acc)
            scores[:, spots] = acc.T
            return c

        lax.fori_loop(0, CTX // HD, chunk, 0)
        s = jnp.where(cached, scores[...] * INV, LOW)
        fresh = [
            jnp.sum(qf * stack4(k.astype(F32)), axis=-1, keepdims=True) * INV for k, _ in new
        ]
        top = functools.reduce(jnp.maximum, fresh, jnp.max(s, axis=-1, keepdims=True))
        e = jnp.exp(s - top)
        ef = [jnp.exp(f - top) for f in fresh]
        total = functools.reduce(jnp.add, ef, jnp.sum(e, axis=-1, keepdims=True))
        inv = 1.0 / total
        return (e * inv).astype(BF), [(f * inv).astype(BF).astype(F32) for f in ef]

    def dec_out(step, w, wf, new):
        def value_row(r, acc):
            return acc + jnp.where(row_of == r, dot(w, cache[r, 1]), 0.0)

        o = lax.fori_loop(0, R, value_row, jnp.zeros((4 * RP, HD), F32), unroll=True)
        for f, (_, v) in zip(wf, new):
            o = o + f * stack4(v.astype(F32))
        o = o.astype(BF)
        o = jnp.concatenate([o[i * RP : (i + 1) * RP] for i in range(4)], axis=1)

        def out_slice(p, c):
            part[step, p] = dot(o, wo[:, pl.ds(pl.multiple_of(p * SL, SL), SL)])
            return c

        lax.fori_loop(0, NT, out_slice, 0)
        lax.fori_loop(1, NT, lambda k, c: (part_copy(step, k).start(), c)[1], 0)

    def part_copy(step, k):
        peer = (t + k) % NT
        return remote(
            part.at[step, peer], gather_part.at[step, t],
            dp_send.at[step, k], dp_recv.at[step, k], {"tp": peer},
        )

    def reduce_parts(step, base):
        lax.fori_loop(1, NT, lambda k, c: (part_copy(step, k).wait_recv(), c)[1], 0)
        total = lax.fori_loop(
            1, NT, lambda k, acc: acc + gather_part[step, (t + k) % NT], part[step, t]
        )
        return (base.astype(F32) + total).astype(BF)

    def x_copy(k):
        return remote(xbuf.at[t], xbuf.at[t], dx_send.at[k], dx_recv.at[k], {"tp": (t + k) % NT})

    loads[2].wait()
    to_row = lax.broadcasted_iota(jnp.int32, (256, 256), 0)
    from_row = lax.broadcasted_iota(jnp.int32, (256, 256), 1)
    parting = (from_row == 2 * (to_row & (HD - 1)) + (to_row >= HD).astype(jnp.int32)).astype(F32).astype(BF)

    def part_rows(b, c):
        both = dot(parting, wkv[pl.ds(pl.multiple_of(b * 256, 256), 256), :]).astype(BF)
        rows = pl.ds(pl.multiple_of(b * HD, HD), HD)
        wqkv[rows, 512:640] = both[:HD]
        wqkv[rows, 640:768] = both[HD:]
        return c

    lax.fori_loop(0, D // HD, part_rows, 0, unroll=8)

    def prepare(p, c):
        total = jnp.zeros((SH, 1), F32)
        rows = pl.ds(pl.multiple_of(p * SP, SP), SP)
        for a in range(2):
            both = xg[p, a].astype(F32)
            for i in range(2):
                x = both[i * SH : (i + 1) * SH]
                total = total + jnp.sum(x * x, axis=-1, keepdims=True)
                start = a * HALF + i * QUART
                n = x * gain_ref[:, start : start + QUART]
                n = jnp.concatenate([n, jnp.zeros((SP - SH, QUART), F32)], axis=0)
                xn[rows, start : start + QUART] = n.astype(BF)
        scale = lax.rsqrt(total / D + EPS)
        scale = jnp.concatenate([scale, jnp.zeros((SP - SH, 1), F32)], axis=0)
        sc[rows, :] = jnp.broadcast_to(scale, (SP, HD))
        return c

    def project(block):
        rows = pl.ds(pl.multiple_of(block * 2 * SP, 2 * SP), 2 * SP)

        def tile(j):
            return dot(xn[rows, :], wqkv[:, j * 256 : (j + 1) * 256]) * sc[rows, 0:1]

        for j in range(2):
            v = tile(j)
            for i in range(2):
                qs[2 * j + i, rows, :] = head_norm(v[:, i * HD : (i + 1) * HD], qgain_ref[...])
        v = tile(2)
        k = head_norm(v[:, :HD], kgain_ref[...])
        kt[:, rows] = k.astype(F32).T.astype(BF)
        vs[rows, :] = v[:, HD:].astype(BF)

    loads[1].wait()
    q0, new0 = dec_project(0, xin[...])
    over_x.wait_recv()
    second_up.start()
    second_down.start()
    first_up.wait_recv()
    fwd_up[0].start()
    first_down.wait_recv()
    fwd_down[0].start()
    send_caches((3, 7), (0, 1))
    w0, wf0 = dec_weights(q0, [new0])
    loads[3].wait()
    dec_out(0, w0, wf0, [new0])
    prepare(mine, 0)
    prepare(partner, 0)
    project(y)
    prepare(down * 2 + h, 0)
    prepare(up * 2 + h, 0)

    base0 = xin[:, pl.ds(pl.multiple_of(t * SL, SL), SL)]
    xbuf[t] = reduce_parts(0, base0)
    lax.fori_loop(1, NT, lambda k, c: (x_copy(k).start(), c)[1], 0)

    second_up.wait_recv()
    fwd_up[1].start()
    second_down.wait_recv()
    fwd_down[1].start()
    send_caches((4,), (2, 3))
    prepare(down * 2 + oh, 0)
    project(down)
    prepare(up * 2 + oh, 0)
    project(up)
    lax.fori_loop(1, NT, lambda k, c: (x_copy(k).wait_recv(), c)[1], 0)
    q1, new1 = dec_project(1, jnp.concatenate([xbuf[p] for p in range(NT)], axis=1))
    fwd_up[0].wait_recv()
    fwd_down[0].wait_recv()
    prepare(far * 2 + h, 0)
    fwd_up[1].wait_recv()
    fwd_down[1].wait_recv()
    prepare(far * 2 + oh, 0)
    project(far)
    send_caches((5,), (4, 5))

    later_col = lax.broadcasted_iota(jnp.int32, (2 * SP, TOK), 1)
    later_row = lax.broadcasted_iota(jnp.int32, (2 * SP, TOK), 0)

    def attend(block):
        rows = pl.ds(pl.multiple_of(block * 2 * SP, 2 * SP), 2 * SP)
        live = (docc_ref[rows, 0:1] == docr_ref[0:1, :]) & (later_col <= later_row + block * (2 * SP))
        heads = []
        for i in range(4):
            s = jnp.where(live, dot(qs[i, rows, :], kt[...]) * INV, LOW)
            e = jnp.exp(s - jnp.max(s, axis=-1, keepdims=True))
            inv = 1.0 / jnp.sum(e, axis=-1, keepdims=True)
            heads.append(dot((e * inv).astype(BF), vs[...]).astype(BF))
        attn = jnp.concatenate(heads, axis=1)
        for a in range(2):
            def columns(j, c):
                start = pl.multiple_of(a * HALF + j * 640, 640)
                lo = dot(attn, wo[:, pl.ds(start, 640)])
                hi = dot(attn, wo[:, pl.ds(pl.multiple_of(start + QUART, 640), 640)])
                for i in range(2):
                    pair = [v[i * SP : i * SP + SH] for v in (lo, hi)]
                    cols = pl.ds(pl.multiple_of(j * 640, 640), 640)
                    terms[block * 2 + i, a, :, cols] = jnp.concatenate(pair, axis=0).astype(BF)
                return c

            lax.fori_loop(0, 2, columns, 0)

    order = (oh, h)

    def rs(n, src, dst, device):
        return remote(src, dst, rs_send.at[n], rs_recv.at[n], device)

    far_up = [rs(i, terms.at[far * 2 + order[i], 0], relay.at[0, i], to_up) for i in range(2)]
    far_down = [rs(2 + i, terms.at[far * 2 + order[i], 1], relay.at[1, i], to_down) for i in range(2)]
    near_up = [
        [rs(4 + 2 * i + a, terms.at[up * 2 + order[i], a], arrive.at[0, i, a], to_up) for a in range(2)]
        for i in range(2)
    ]
    near_down = [
        [rs(8 + 2 * i + a, terms.at[down * 2 + order[i], a], arrive.at[1, i, a], to_down) for a in range(2)]
        for i in range(2)
    ]
    over = [rs(12 + a, cross.at[0, a], cross.at[1, a], to_x) for a in range(2)]

    def relay_up(i):
        far_up[i].wait_recv()
        spot = up * 2 + order[i]
        terms[spot, 0] = (terms[spot, 0].astype(F32) + relay[0, i].astype(F32)).astype(BF)
        near_up[i][0].start()

    def relay_down(i):
        far_down[i].wait_recv()
        spot = down * 2 + order[i]
        terms[spot, 1] = (terms[spot, 1].astype(F32) + relay[1, i].astype(F32)).astype(BF)
        near_down[i][1].start()

    def summed(i, a):
        near_up[i][a].wait_recv()
        near_down[i][a].wait_recv()
        return (
            terms[y * 2 + order[i], a].astype(F32)
            + arrive[0, i, a].astype(F32)
            + arrive[1, i, a].astype(F32)
        )

    attend(far)
    far_up[0].start()
    far_down[0].start()
    attend(up)
    attend(down)
    far_up[0].wait_send()
    near_up[0][1].start()
    far_down[0].wait_send()
    near_down[0][0].start()
    relay_up(0)
    relay_down(0)
    send_caches((), (6, 7))
    w1, wf1 = dec_weights(q1, [new0, new1])
    dec_out(1, w1, wf1, [new0, new1])
    attend(y)
    near_up[0][0].wait_send()
    far_up[1].start()
    near_down[0][1].wait_send()
    far_down[1].start()
    for a in range(2):
        cross[0, a] = summed(0, a).astype(BF)
        over[a].start()

    mine_rows = pl.ds(pl.multiple_of(g * RP, RP), RP)
    fin[mine_rows, 0:SL] = reduce_parts(1, xbuf[t])
    for i, (k, v) in enumerate([new0, new1]):
        start = SL + 2 * i * HD
        fin[mine_rows, start : start + HD] = k
        fin[mine_rows, start + HD : start + 2 * HD] = v

    def fin_copy(k):
        where = fin.at[mine_rows]
        return remote(where, where, fin_send.at[k], fin_recv.at[k], {"group": (g + k) % NG})

    lax.fori_loop(1, NG, lambda k, c: (fin_copy(k).start(), c)[1], 0)

    far_up[1].wait_send()
    near_up[1][1].start()
    far_down[1].wait_send()
    near_down[1][0].start()
    relay_up(1)
    relay_down(1)

    for a in range(2):
        near = summed(1, a)
        for i in range(2):
            cols = slice(a * HALF + i * QUART, a * HALF + (i + 1) * QUART)
            add = near[i * SH : (i + 1) * SH]
            score_sum[:, cols] = score_ref[:, cols].astype(F32) + add

    lax.fori_loop(1, NG, lambda k, c: (fin_copy(k).wait_recv(), c)[1], 0)
    placed = dot(pick[...], fin[...])
    obuf[t] = placed[:, :SL].astype(BF)
    patch_ref[...] = placed[:, SL:]

    def o_copy(k):
        return remote(obuf.at[t], obuf.at[t], o_send.at[k], o_recv.at[k], {"tp": (t + k) % NT})

    lax.fori_loop(1, NT, lambda k, c: (o_copy(k).start(), c)[1], 0)

    for a in range(2):
        over[a].wait_recv()
        far_half = cross[1, a].astype(F32)
        for i in range(2):
            cols = slice(a * HALF + i * QUART, a * HALF + (i + 1) * QUART)
            add = far_half[i * SH : (i + 1) * SH]
            score_out_ref[:, cols] = (score_sum[:, cols] + add).astype(BF)

    lax.fori_loop(1, NT, lambda k, c: (o_copy(k).wait_recv(), c)[1], 0)
    for p in range(NT):
        dec_out_ref[:, p * SL : (p + 1) * SL] = obuf[p]

    def end_a2a(j, c):
        a2a(j)[1].wait()
        return c

    lax.fori_loop(1, NG, end_a2a, 0)
    own_copy.wait()
    ended = [over_x, first_up, first_down, second_up, second_down] + fwd_up + fwd_down + over
    ended += near_up[1] + near_down[1] + [near_up[0][1], near_down[0][0]]
    for c in ended:
        c.wait_send()

    def end_tp(k, c):
        part_copy(0, k).wait_send()
        part_copy(1, k).wait_send()
        x_copy(k).wait_send()
        o_copy(k).wait_send()
        return c

    lax.fori_loop(1, NT, end_tp, 0)
    lax.fori_loop(1, NG, lambda k, c: (fin_copy(k).wait_send(), c)[1], 0)


def place_kernel(
    plan_ref, patch_ref, dec_ref, got_hbm, score_hbm,
    dec_out_ref, cache_out, score_out, rows, score_rows, in_sem, out_sem, score_sem,
):
    score_in = pltpu.make_async_copy(score_hbm, score_rows, score_sem.at[0])
    score_end = pltpu.make_async_copy(score_rows, score_out, score_sem.at[1])
    score_in.start()

    def get(s, c):
        pltpu.make_async_copy(got_hbm.at[plan_ref[s, 0]], rows.at[s], in_sem.at[s]).start()
        return c

    lax.fori_loop(0, R, get, 0)
    dec_out_ref[...] = dec_ref[:R, :]
    score_in.wait()
    score_end.start()

    def put(s, c):
        pltpu.make_async_copy(got_hbm.at[0], rows.at[s], in_sem.at[s]).wait()
        entry = patch_ref[pl.ds(s, 1), :]
        for step in range(2):
            pos = plan_ref[s, 1] + step
            base = pl.multiple_of((pos // 16) * 16, 16)
            here = lax.broadcasted_iota(jnp.int32, (16, HD), 0) == pos - base
            for kv in range(2):
                start = (2 * step + kv) * HD
                old = rows[s, kv, pl.ds(base, 16), :].astype(F32)
                both = jnp.where(here, entry[:, start : start + HD], old)
                rows[s, kv, pl.ds(base, 16), :] = both.astype(BF)
        pltpu.make_async_copy(rows.at[s], cache_out.at[s], out_sem.at[s]).start()
        return c

    lax.fori_loop(0, R, put, 0)

    def end(s, c):
        pltpu.make_async_copy(rows.at[s], cache_out.at[s], out_sem.at[s]).wait()
        return c

    lax.fori_loop(0, R, end, 0)
    score_end.wait()


def per_device(
    dec_rows, kv_cache, lengths, dest_group, dest_slot, score_rows, doc_ids,
    norm_gain, query_gain, key_gain, w_query, w_keyval, w_out,
):
    smem = pl.BlockSpec(memory_space=pltpu.SMEM)
    vmem = pl.BlockSpec(memory_space=pltpu.VMEM)
    hbm = pl.BlockSpec(memory_space=pl.ANY)
    dma = pltpu.SemaphoreType.DMA
    got, patch, plan, dec_out16, score_sum = pl.pallas_call(
        main_kernel,
        name="decode_and_score",
        out_shape=(
            jax.ShapeDtypeStruct((NG, 2, CTX, HD), BF),
            jax.ShapeDtypeStruct((RP, 4 * HD), F32),
            jax.ShapeDtypeStruct((RP, HD), jnp.int32),
            jax.ShapeDtypeStruct((RP, D), BF),
            jax.ShapeDtypeStruct((SH, D), BF),
        ),
        in_specs=[smem] * 3 + [vmem] * 6 + [hbm] * 4,
        out_specs=(hbm, vmem, vmem, vmem, vmem),
        scratch_shapes=[
            pltpu.VMEM((R, 2, CTX, HD), BF),
            pltpu.VMEM((2 * D, HD), BF),
            pltpu.VMEM((D, 768), BF),
            pltpu.VMEM((512, D), BF),
            pltpu.VMEM((RP, D), F32),
            pltpu.VMEM((16, TOK), F32),
            pltpu.VMEM((TOK, HD), F32),
            pltpu.VMEM((NG, 2, CTX, HD), BF),
            pltpu.VMEM((NT, 2, 2 * SH, QUART), BF),
            pltpu.VMEM((TOK, D), BF),
            pltpu.VMEM((TOK, HD), F32),
            pltpu.VMEM((4, TOK, HD), BF),
            pltpu.VMEM((HD, TOK), BF),
            pltpu.VMEM((TOK, HD), BF),
            pltpu.VMEM((NT, 2, 2 * SH, QUART), BF),
            pltpu.VMEM((2, 2, 2 * SH, QUART), BF),
            pltpu.VMEM((2, 2, 2, 2 * SH, QUART), BF),
            pltpu.VMEM((2, 2, 2 * SH, QUART), BF),
            pltpu.VMEM((SH, D), F32),
            pltpu.VMEM((2, NT, RP, SL), F32),
            pltpu.VMEM((2, NT, RP, SL), F32),
            pltpu.VMEM((NT, RP, SL), BF),
            pltpu.VMEM((RP, D), BF),
            pltpu.VMEM((4 * RP, CTX), F32),
            pltpu.VMEM((RP, NG * RP), BF),
            pltpu.VMEM((NG * RP, MSG), BF),
            pltpu.VMEM((NT, RP, SL), BF),
            dma((4,)), dma((NG,)), dma((NG,)), dma((9,)), dma((9,)), dma((14,)), dma((14,)),
            dma((2, NT)), dma((2, NT)), dma((NT,)), dma((NT,)), dma((NG,)), dma((NG,)),
            dma((NT,)), dma((NT,)),
        ],
        compiler_params=pltpu.CompilerParams(
            collective_id=0, has_side_effects=True, vmem_limit_bytes=60 * 1024 * 1024
        ),
        cost_estimate=pl.CostEstimate(flops=8 * 10**9, bytes_accessed=30 * 10**6, transcendentals=10**6),
    )(
        dest_group, dest_slot, lengths, dec_rows, score_rows, norm_gain.reshape(1, D),
        query_gain.reshape(1, HD), key_gain.reshape(1, HD), doc_ids,
        kv_cache, w_query, w_keyval.reshape(2 * D, HD), w_out,
    )
    return pl.pallas_call(
        place_kernel,
        name="place_rows",
        out_shape=(
            jax.ShapeDtypeStruct((R, D), BF),
            jax.ShapeDtypeStruct((R, 2, CTX, HD), BF),
            jax.ShapeDtypeStruct((SH, D), BF),
        ),
        in_specs=[smem] + [vmem] * 2 + [hbm] * 2,
        out_specs=(vmem, hbm, hbm),
        scratch_shapes=[
            pltpu.VMEM((R, 2, CTX, HD), BF),
            pltpu.VMEM((SH, D), BF),
            dma((R,)), dma((R,)), dma((2,)),
        ],
        compiler_params=pltpu.CompilerParams(vmem_limit_bytes=60 * 1024 * 1024),
        cost_estimate=pl.CostEstimate(flops=10**6, bytes_accessed=12 * 10**6, transcendentals=0),
    )(plan, patch, dec_out16, got, score_sum)


def solution(mesh):
    placed = (
        P("group", None),
        P("group", None, None, "tp"),
        P(),
        P(),
        P(),
        P(("group", "tp"), None),
        P("group", None),
        P(),
        P(),
        P(),
        P(None, "tp"),
        P(None, None, "tp"),
        P("tp", None),
    )
    return jax.shard_map(
        per_device,
        mesh=mesh,
        in_specs=placed,
        out_specs=(P("group", None), P("group", None, None, "tp"), P(("group", "tp"), None)),
        check_vma=False,
    )
```

```python
import functools
import math

import jax
import jax.numpy as jnp
from jax import lax
from jax.experimental import pallas as pl
from jax.experimental.pallas import tpu as pltpu
from jax.sharding import PartitionSpec as P

HD = 128
EPS = 1e-06
MESH = pl.DeviceIdType.MESH
BF = jnp.bfloat16
F32 = jnp.float32
LOW = -1e30
INV = 1.0 / math.sqrt(HD)

D = 5120
CTX = 768
NG = 16
NT = 8
R = 14
RP = 16
SH = 56
SP = 64
TOK = NT * SP
HALF = D // 2
QUART = D // 4
SL = D // NT
MSG = SL + 4 * HD
GATHER_CUTS = ((0, 64), (64, 48))
SUM_CUTS = ((0, 48), (48, 32), (80, 32))


def head_norm(vectors, gain):
    mean = jnp.mean(vectors * vectors, axis=-1, keepdims=True)
    return (vectors * lax.rsqrt(mean + EPS) * gain).astype(BF)


def dot(a, b):
    return jnp.dot(a, b, preferred_element_type=F32)


class Several:
    def __init__(self, copies):
        self.copies = copies

    def start(self):
        for copy in self.copies:
            copy.start()

    def wait_recv(self):
        for copy in self.copies:
            copy.wait_recv()

    def wait_send(self):
        for copy in self.copies:
            copy.wait_send()


def dot_t(a, b):
    return lax.dot_general(a, b, (((1,), (1,)), ((), ())), preferred_element_type=F32)


def main_kernel(
    dest_ref, slot_ref, len_ref,
    dec_ref, score_ref, gain_ref, qgain_ref, kgain_ref, doc_ref,
    cache_hbm, wq_hbm, wkv_hbm, wo_hbm,
    got_ref, patch_ref, plan_ref, dec_out_ref, score_out_ref,
    cache, wkv, wqkv, wo, xin, docr_ref, docc_ref, packed, xg, xn, sc, qs, kt, vs, terms,
    relay, arrive, cross, score_sum, part, gather_part, xbuf, nx, scores, pick, fin, obuf,
    load_sem, a2a_send, a2a_recv, ag_send, ag_recv, rs_send, rs_recv,
    dp_send, dp_recv, dx_send, dx_recv, fin_send, fin_recv, o_send, o_recv,
):
    g = lax.axis_index("group")
    t = lax.axis_index("tp")
    y, h = t // 2, t % 2
    z, xl, core = g // 4, (g // 2) % 2, g % 2
    oh = 1 - h
    up, down, far = (y + 1) % 4, (y + 3) % 4, (y + 2) % 4
    mine, partner = t, y * 2 + oh
    to_up, to_down, to_x = {"tp": up * 2 + h}, {"tp": down * 2 + h}, {"tp": partner}

    def remote(src, dst, send, recv, device):
        return pltpu.make_async_remote_copy(
            src_ref=src, dst_ref=dst, send_sem=send, recv_sem=recv,
            device_id=device, device_id_type=MESH,
        )

    loads = [
        pltpu.make_async_copy(cache_hbm, cache, load_sem.at[0]),
        pltpu.make_async_copy(wq_hbm, wqkv.at[:, pl.ds(0, 512)], load_sem.at[1]),
        pltpu.make_async_copy(wkv_hbm, wkv, load_sem.at[2]),
        pltpu.make_async_copy(wo_hbm, wo, load_sem.at[3]),
    ]
    for load in loads:
        load.start()

    barrier = pltpu.get_barrier_semaphore()

    def greet_tp(k, c):
        pl.semaphore_signal(barrier, inc=1, device_id={"tp": (t + k) % NT}, device_id_type=MESH)
        return c

    def greet_group(k, c):
        pl.semaphore_signal(barrier, inc=1, device_id={"group": (g + k) % NG}, device_id_type=MESH)
        return c

    lax.fori_loop(1, NT, greet_tp, 0)
    lax.fori_loop(1, NG, greet_group, 0)

    for a in range(2):
        lo = score_ref[:, a * HALF : a * HALF + QUART].astype(F32)
        hi = score_ref[:, a * HALF + QUART : (a + 1) * HALF].astype(F32)
        xg[mine, a] = jnp.concatenate([lo, hi], axis=0).astype(BF)

    pl.semaphore_wait(barrier, NT - 1 + NG - 1)

    def pieces(cuts, src, dst, send, recv, base, device):
        return [
            remote(
                src.at[pl.ds(lo, n), :], dst.at[pl.ds(lo, n), :],
                send.at[base + i], recv.at[base + i], device,
            )
            for i, (lo, n) in enumerate(cuts)
        ]

    def ag(base, shard, halves, device):
        copies = []
        for i, a in enumerate(halves):
            where = xg.at[shard, a]
            copies += pieces(GATHER_CUTS, where, where, ag_send, ag_recv, base + 2 * i, device)
        return Several(copies)

    over_x = ag(0, mine, (0, 1), to_x)
    first_up, first_down = ag(4, mine, (0, 1), to_up), ag(8, mine, (0, 1), to_down)
    for c in (over_x, first_up, first_down):
        c.start()
    second_up, second_down = ag(12, partner, (0, 1), to_up), ag(16, partner, (0, 1), to_down)
    fwd_up = [ag(20 + 2 * i, down * 2 + hh, (0,), to_up) for i, hh in enumerate((h, oh))]
    fwd_down = [ag(24 + 2 * i, up * 2 + hh, (1,), to_down) for i, hh in enumerate((h, oh))]

    def a2a(j):
        dz, dx, dc = j // 4, (j // 2) % 2, j % 2
        target = ((z + dz) % 4) * 4 + ((xl + dx) % 2) * 2 + (core + dc) % 2
        copy = remote(packed.at[j], got_ref.at[g], a2a_send.at[j], a2a_recv.at[j], {"group": target})
        return target, copy

    def fill(j, target):
        row = 0
        for r in range(1, R):
            row = jnp.where(dest_ref[g * R + r] == target, r, row)
        for kv in range(2):
            packed[j, kv] = cache[row, kv]

    def send_caches(along, across=()):
        for dx, some in ((1, across), (0, along)):
            for i in some:
                j = (i // 2) * 4 + dx * 2 + i % 2
                target, copy = a2a(j)
                fill(j, target)
                copy.start()

    loads[0].wait()
    send_caches((1, 2, 6))
    fill(0, g)
    own_copy = pltpu.make_async_copy(packed.at[0], got_ref.at[g], a2a_send.at[0])
    own_copy.start()

    xin[...] = jnp.zeros_like(xin)
    xin[0:R, :] = dec_ref[...].astype(F32)
    token = lax.broadcasted_iota(jnp.int32, (TOK, NT * SH), 1)
    place = lax.broadcasted_iota(jnp.int32, (TOK, NT * SH), 0)
    inside = (place & (SP - 1)) < SH
    spread = ((place - (place >> 6) * (SP - SH) == token) & inside).astype(F32).astype(BF)
    ids = jnp.broadcast_to(doc_ref[...].astype(F32) + 1.0, (HD, NT * SH)).astype(BF)
    docr_ref[...] = dot_t(ids[:16], spread)
    docc_ref[...] = dot_t(spread, ids)

    lane = lax.broadcasted_iota(jnp.int32, (RP, NG * RP), 1)
    slot_row = lax.broadcasted_iota(jnp.int32, (RP, NG * RP), 0)

    def wanted(e, c):
        want, span = c
        for r in range(R):
            here = jnp.where(dest_ref[e * R + r] == g, slot_ref[e * R + r], -1)
            spot = lane == e * RP + r
            want = jnp.where(spot, here, want)
            span = jnp.where(spot, len_ref[e * R + r], span)
        return want, span

    none = jnp.full((RP, NG * RP), -1, jnp.int32)
    want, span = lax.fori_loop(0, NG, wanted, (none, jnp.zeros_like(none)))
    pick[...] = (want == slot_row).astype(F32).astype(BF)
    source = jnp.sum(jnp.where(want == slot_row, lane >> 4, 0), axis=-1, keepdims=True)
    length = jnp.sum(jnp.where(want == slot_row, span, 0), axis=-1, keepdims=True)
    plan_lane = lax.broadcasted_iota(jnp.int32, (RP, HD), 1)
    plan_ref[...] = jnp.where(plan_lane == 0, source, length)

    row_of = lax.broadcasted_iota(jnp.int32, (4 * RP, HD), 0) & (RP - 1)
    column_row = lax.broadcasted_iota(jnp.int32, (HD, 4 * RP), 1) & (RP - 1)
    lens = jnp.ones((4 * RP, HD), jnp.int32)
    for r in range(R):
        lens = jnp.where(row_of == r, len_ref[g * R + r], lens)
    cached = lax.broadcasted_iota(jnp.int32, (4 * RP, CTX), 1) < lens[:, 0:1]

    def stack4(v):
        return jnp.concatenate([v] * 4, axis=0)

    def dec_project(step, x):
        wide = x.astype(F32)
        scale = lax.rsqrt(jnp.mean(wide * wide, axis=-1, keepdims=True) + EPS)
        nx[...] = (wide * gain_ref[...]).astype(BF)

        def chunk(k, acc):
            cols = pl.ds(pl.multiple_of(k * 1024, 1024), 1024)
            return acc + dot(nx[:, cols], wqkv[cols, :])

        proj = lax.fori_loop(0, 5, chunk, jnp.zeros((RP, 768), F32)) * scale
        q = jnp.concatenate([proj[:, i * HD : (i + 1) * HD] for i in range(4)], axis=0)
        q = head_norm(q, qgain_ref[...])
        return q, (head_norm(proj[:, 512:640], kgain_ref[...]), proj[:, 640:768].astype(BF))

    def dec_weights(q, new):
        qf = q.astype(F32)
        qt = qf.T.astype(BF)

        def chunk(n, c):
            spots = pl.ds(pl.multiple_of(n * HD, HD), HD)
            acc = jnp.zeros((HD, 4 * RP), F32)
            for r in range(R):
                acc = jnp.where(column_row == r, dot(cache[r, 0, spots, :], qt), acc)
            scores[:, spots] = acc.T
            return c

        lax.fori_loop(0, CTX // HD, chunk, 0)
        s = jnp.where(cached, scores[...] * INV, LOW)
        fresh = [
            jnp.sum(qf * stack4(k.astype(F32)), axis=-1, keepdims=True) * INV for k, _ in new
        ]
        top = functools.reduce(jnp.maximum, fresh, jnp.max(s, axis=-1, keepdims=True))
        e = jnp.exp(s - top)
        ef = [jnp.exp(f - top) for f in fresh]
        total = functools.reduce(jnp.add, ef, jnp.sum(e, axis=-1, keepdims=True))
        inv = 1.0 / total
        return (e * inv).astype(BF), [(f * inv).astype(BF).astype(F32) for f in ef]

    def dec_out(step, w, wf, new):
        def value_row(r, acc):
            return acc + jnp.where(row_of == r, dot(w, cache[r, 1]), 0.0)

        o = lax.fori_loop(0, R, value_row, jnp.zeros((4 * RP, HD), F32), unroll=True)
        for f, (_, v) in zip(wf, new):
            o = o + f * stack4(v.astype(F32))
        o = o.astype(BF)
        o = jnp.concatenate([o[i * RP : (i + 1) * RP] for i in range(4)], axis=1)

        def out_slice(p, c):
            part[step, p] = dot(o, wo[:, pl.ds(pl.multiple_of(p * SL, SL), SL)])
            return c

        lax.fori_loop(0, NT, out_slice, 0)
        lax.fori_loop(1, NT, lambda k, c: (part_copy(step, k).start(), c)[1], 0)

    def part_copy(step, k):
        peer = (t + k) % NT
        return remote(
            part.at[step, peer], gather_part.at[step, t],
            dp_send.at[step, k], dp_recv.at[step, k], {"tp": peer},
        )

    def reduce_parts(step, base):
        lax.fori_loop(1, NT, lambda k, c: (part_copy(step, k).wait_recv(), c)[1], 0)
        total = lax.fori_loop(
            1, NT, lambda k, acc: acc + gather_part[step, (t + k) % NT], part[step, t]
        )
        return (base.astype(F32) + total).astype(BF)

    def x_copy(k):
        return remote(xbuf.at[t], xbuf.at[t], dx_send.at[k], dx_recv.at[k], {"tp": (t + k) % NT})

    loads[2].wait()
    to_row = lax.broadcasted_iota(jnp.int32, (256, 256), 0)
    from_row = lax.broadcasted_iota(jnp.int32, (256, 256), 1)
    parting = (from_row == 2 * (to_row & (HD - 1)) + (to_row >= HD).astype(jnp.int32)).astype(F32).astype(BF)

    def part_rows(b, c):
        both = dot(parting, wkv[pl.ds(pl.multiple_of(b * 256, 256), 256), :]).astype(BF)
        rows = pl.ds(pl.multiple_of(b * HD, HD), HD)
        wqkv[rows, 512:640] = both[:HD]
        wqkv[rows, 640:768] = both[HD:]
        return c

    lax.fori_loop(0, D // HD, part_rows, 0, unroll=8)

    def prepare(p, c):
        total = jnp.zeros((SH, 1), F32)
        rows = pl.ds(pl.multiple_of(p * SP, SP), SP)
        for a in range(2):
            both = xg[p, a].astype(F32)
            for i in range(2):
                x = both[i * SH : (i + 1) * SH]
                total = total + jnp.sum(x * x, axis=-1, keepdims=True)
                start = a * HALF + i * QUART
                n = x * gain_ref[:, start : start + QUART]
                n = jnp.concatenate([n, jnp.zeros((SP - SH, QUART), F32)], axis=0)
                xn[rows, start : start + QUART] = n.astype(BF)
        scale = lax.rsqrt(total / D + EPS)
        scale = jnp.concatenate([scale, jnp.zeros((SP - SH, 1), F32)], axis=0)
        sc[rows, :] = jnp.broadcast_to(scale, (SP, HD))
        return c

    def project(block):
        rows = pl.ds(pl.multiple_of(block * 2 * SP, 2 * SP), 2 * SP)

        def tile(j):
            return dot(xn[rows, :], wqkv[:, j * 256 : (j + 1) * 256]) * sc[rows, 0:1]

        for j in range(2):
            v = tile(j)
            for i in range(2):
                qs[2 * j + i, rows, :] = head_norm(v[:, i * HD : (i + 1) * HD], qgain_ref[...])
        v = tile(2)
        k = head_norm(v[:, :HD], kgain_ref[...])
        kt[:, rows] = k.astype(F32).T.astype(BF)
        vs[rows, :] = v[:, HD:].astype(BF)

    loads[1].wait()
    q0, new0 = dec_project(0, xin[...])
    over_x.wait_recv()
    second_up.start()
    second_down.start()
    first_up.wait_recv()
    fwd_up[0].start()
    first_down.wait_recv()
    fwd_down[0].start()
    send_caches((3, 7), (0, 1))
    w0, wf0 = dec_weights(q0, [new0])
    loads[3].wait()
    dec_out(0, w0, wf0, [new0])
    prepare(mine, 0)
    prepare(partner, 0)
    project(y)
    prepare(down * 2 + h, 0)
    prepare(up * 2 + h, 0)

    base0 = xin[:, pl.ds(pl.multiple_of(t * SL, SL), SL)]
    xbuf[t] = reduce_parts(0, base0)
    lax.fori_loop(1, NT, lambda k, c: (x_copy(k).start(), c)[1], 0)

    second_up.wait_recv()
    fwd_up[1].start()
    second_down.wait_recv()
    fwd_down[1].start()
    send_caches((4,), (2, 3))
    prepare(down * 2 + oh, 0)
    project(down)
    prepare(up * 2 + oh, 0)
    project(up)
    lax.fori_loop(1, NT, lambda k, c: (x_copy(k).wait_recv(), c)[1], 0)
    q1, new1 = dec_project(1, jnp.concatenate([xbuf[p] for p in range(NT)], axis=1))
    fwd_up[0].wait_recv()
    fwd_down[0].wait_recv()
    prepare(far * 2 + h, 0)
    fwd_up[1].wait_recv()
    fwd_down[1].wait_recv()
    prepare(far * 2 + oh, 0)
    project(far)
    send_caches((5,), (4, 5))

    later_col = lax.broadcasted_iota(jnp.int32, (2 * SP, TOK), 1)
    later_row = lax.broadcasted_iota(jnp.int32, (2 * SP, TOK), 0)

    def attend(block):
        rows = pl.ds(pl.multiple_of(block * 2 * SP, 2 * SP), 2 * SP)
        live = (docc_ref[rows, 0:1] == docr_ref[0:1, :]) & (later_col <= later_row + block * (2 * SP))
        heads = []
        for i in range(4):
            s = jnp.where(live, dot(qs[i, rows, :], kt[...]) * INV, LOW)
            e = jnp.exp(s - jnp.max(s, axis=-1, keepdims=True))
            inv = 1.0 / jnp.sum(e, axis=-1, keepdims=True)
            heads.append(dot((e * inv).astype(BF), vs[...]).astype(BF))
        attn = jnp.concatenate(heads, axis=1)
        for a in range(2):
            lo, hi = [
                dot(attn, wo[:, a * HALF + i * QUART : a * HALF + (i + 1) * QUART]) for i in range(2)
            ]
            for i in range(2):
                pair = [v[i * SP : i * SP + SH] for v in (lo, hi)]
                terms[block * 2 + i, a] = jnp.concatenate(pair, axis=0).astype(BF)

    order = (oh, h)

    def rs(n, src, dst, device):
        return Several(pieces(SUM_CUTS, src, dst, rs_send, rs_recv, 3 * n, device))

    far_up = [rs(i, terms.at[far * 2 + order[i], 0], relay.at[0, i], to_up) for i in range(2)]
    far_down = [rs(2 + i, terms.at[far * 2 + order[i], 1], relay.at[1, i], to_down) for i in range(2)]
    near_up = [
        [rs(4 + 2 * i + a, terms.at[up * 2 + order[i], a], arrive.at[0, i, a], to_up) for a in range(2)]
        for i in range(2)
    ]
    near_down = [
        [rs(8 + 2 * i + a, terms.at[down * 2 + order[i], a], arrive.at[1, i, a], to_down) for a in range(2)]
        for i in range(2)
    ]
    over = [rs(12 + a, cross.at[0, a], cross.at[1, a], to_x) for a in range(2)]

    def relay_up(i):
        far_up[i].wait_recv()
        spot = up * 2 + order[i]
        terms[spot, 0] = (terms[spot, 0].astype(F32) + relay[0, i].astype(F32)).astype(BF)
        near_up[i][0].start()

    def relay_down(i):
        far_down[i].wait_recv()
        spot = down * 2 + order[i]
        terms[spot, 1] = (terms[spot, 1].astype(F32) + relay[1, i].astype(F32)).astype(BF)
        near_down[i][1].start()

    def summed(i, a):
        near_up[i][a].wait_recv()
        near_down[i][a].wait_recv()
        return (
            terms[y * 2 + order[i], a].astype(F32)
            + arrive[0, i, a].astype(F32)
            + arrive[1, i, a].astype(F32)
        )

    attend(far)
    far_up[0].start()
    far_down[0].start()
    attend(up)
    attend(down)
    far_up[0].wait_send()
    near_up[0][1].start()
    far_down[0].wait_send()
    near_down[0][0].start()
    relay_up(0)
    relay_down(0)
    send_caches((), (6, 7))
    w1, wf1 = dec_weights(q1, [new0, new1])
    dec_out(1, w1, wf1, [new0, new1])
    attend(y)
    near_up[0][0].wait_send()
    far_up[1].start()
    near_down[0][1].wait_send()
    far_down[1].start()
    for a in range(2):
        cross[0, a] = summed(0, a).astype(BF)
        over[a].start()

    mine_rows = pl.ds(pl.multiple_of(g * RP, RP), RP)
    fin[mine_rows, 0:SL] = reduce_parts(1, xbuf[t])
    for i, (k, v) in enumerate([new0, new1]):
        start = SL + 2 * i * HD
        fin[mine_rows, start : start + HD] = k
        fin[mine_rows, start + HD : start + 2 * HD] = v

    def fin_copy(k):
        where = fin.at[mine_rows]
        return remote(where, where, fin_send.at[k], fin_recv.at[k], {"group": (g + k) % NG})

    lax.fori_loop(1, NG, lambda k, c: (fin_copy(k).start(), c)[1], 0)

    far_up[1].wait_send()
    near_up[1][1].start()
    far_down[1].wait_send()
    near_down[1][0].start()
    relay_up(1)
    relay_down(1)

    for a in range(2):
        near = summed(1, a)
        for i in range(2):
            cols = slice(a * HALF + i * QUART, a * HALF + (i + 1) * QUART)
            add = near[i * SH : (i + 1) * SH]
            score_sum[:, cols] = score_ref[:, cols].astype(F32) + add

    lax.fori_loop(1, NG, lambda k, c: (fin_copy(k).wait_recv(), c)[1], 0)
    placed = dot(pick[...], fin[...])
    obuf[t] = placed[:, :SL].astype(BF)
    patch_ref[...] = placed[:, SL:]

    def o_copy(k):
        return remote(obuf.at[t], obuf.at[t], o_send.at[k], o_recv.at[k], {"tp": (t + k) % NT})

    lax.fori_loop(1, NT, lambda k, c: (o_copy(k).start(), c)[1], 0)

    for a in range(2):
        over[a].wait_recv()
        far_half = cross[1, a].astype(F32)
        for i in range(2):
            cols = slice(a * HALF + i * QUART, a * HALF + (i + 1) * QUART)
            add = far_half[i * SH : (i + 1) * SH]
            score_out_ref[:, cols] = (score_sum[:, cols] + add).astype(BF)

    lax.fori_loop(1, NT, lambda k, c: (o_copy(k).wait_recv(), c)[1], 0)
    for p in range(NT):
        dec_out_ref[:, p * SL : (p + 1) * SL] = obuf[p]

    def end_a2a(j, c):
        a2a(j)[1].wait()
        return c

    lax.fori_loop(1, NG, end_a2a, 0)
    own_copy.wait()
    ended = [over_x, first_up, first_down, second_up, second_down] + fwd_up + fwd_down + over
    ended += near_up[1] + near_down[1] + [near_up[0][1], near_down[0][0]]
    for c in ended:
        c.wait_send()

    def end_tp(k, c):
        part_copy(0, k).wait_send()
        part_copy(1, k).wait_send()
        x_copy(k).wait_send()
        o_copy(k).wait_send()
        return c

    lax.fori_loop(1, NT, end_tp, 0)
    lax.fori_loop(1, NG, lambda k, c: (fin_copy(k).wait_send(), c)[1], 0)


def place_kernel(
    plan_ref, patch_ref, dec_ref, got_hbm, score_hbm,
    dec_out_ref, cache_out, score_out, rows, score_rows, in_sem, out_sem, score_sem,
):
    score_in = pltpu.make_async_copy(score_hbm, score_rows, score_sem.at[0])
    score_end = pltpu.make_async_copy(score_rows, score_out, score_sem.at[1])
    score_in.start()

    def get(s, c):
        pltpu.make_async_copy(got_hbm.at[plan_ref[s, 0]], rows.at[s], in_sem.at[s]).start()
        return c

    lax.fori_loop(0, R, get, 0)
    dec_out_ref[...] = dec_ref[:R, :]
    score_in.wait()
    score_end.start()

    def put(s, c):
        pltpu.make_async_copy(got_hbm.at[0], rows.at[s], in_sem.at[s]).wait()
        entry = patch_ref[pl.ds(s, 1), :]
        for step in range(2):
            pos = plan_ref[s, 1] + step
            base = pl.multiple_of((pos // 16) * 16, 16)
            here = lax.broadcasted_iota(jnp.int32, (16, HD), 0) == pos - base
            for kv in range(2):
                start = (2 * step + kv) * HD
                old = rows[s, kv, pl.ds(base, 16), :].astype(F32)
                both = jnp.where(here, entry[:, start : start + HD], old)
                rows[s, kv, pl.ds(base, 16), :] = both.astype(BF)
        pltpu.make_async_copy(rows.at[s], cache_out.at[s], out_sem.at[s]).start()
        return c

    lax.fori_loop(0, R, put, 0)

    def end(s, c):
        pltpu.make_async_copy(rows.at[s], cache_out.at[s], out_sem.at[s]).wait()
        return c

    lax.fori_loop(0, R, end, 0)
    score_end.wait()


def per_device(
    dec_rows, kv_cache, lengths, dest_group, dest_slot, score_rows, doc_ids,
    norm_gain, query_gain, key_gain, w_query, w_keyval, w_out,
):
    smem = pl.BlockSpec(memory_space=pltpu.SMEM)
    vmem = pl.BlockSpec(memory_space=pltpu.VMEM)
    hbm = pl.BlockSpec(memory_space=pl.ANY)
    dma = pltpu.SemaphoreType.DMA
    got, patch, plan, dec_out16, score_sum = pl.pallas_call(
        main_kernel,
        name="decode_and_score",
        out_shape=(
            jax.ShapeDtypeStruct((NG, 2, CTX, HD), BF),
            jax.ShapeDtypeStruct((RP, 4 * HD), F32),
            jax.ShapeDtypeStruct((RP, HD), jnp.int32),
            jax.ShapeDtypeStruct((RP, D), BF),
            jax.ShapeDtypeStruct((SH, D), BF),
        ),
        in_specs=[smem] * 3 + [vmem] * 6 + [hbm] * 4,
        out_specs=(hbm, vmem, vmem, vmem, vmem),
        scratch_shapes=[
            pltpu.VMEM((R, 2, CTX, HD), BF),
            pltpu.VMEM((2 * D, HD), BF),
            pltpu.VMEM((D, 768), BF),
            pltpu.VMEM((512, D), BF),
            pltpu.VMEM((RP, D), F32),
            pltpu.VMEM((16, TOK), F32),
            pltpu.VMEM((TOK, HD), F32),
            pltpu.VMEM((NG, 2, CTX, HD), BF),
            pltpu.VMEM((NT, 2, 2 * SH, QUART), BF),
            pltpu.VMEM((TOK, D), BF),
            pltpu.VMEM((TOK, HD), F32),
            pltpu.VMEM((4, TOK, HD), BF),
            pltpu.VMEM((HD, TOK), BF),
            pltpu.VMEM((TOK, HD), BF),
            pltpu.VMEM((NT, 2, 2 * SH, QUART), BF),
            pltpu.VMEM((2, 2, 2 * SH, QUART), BF),
            pltpu.VMEM((2, 2, 2, 2 * SH, QUART), BF),
            pltpu.VMEM((2, 2, 2 * SH, QUART), BF),
            pltpu.VMEM((SH, D), F32),
            pltpu.VMEM((2, NT, RP, SL), F32),
            pltpu.VMEM((2, NT, RP, SL), F32),
            pltpu.VMEM((NT, RP, SL), BF),
            pltpu.VMEM((RP, D), BF),
            pltpu.VMEM((4 * RP, CTX), F32),
            pltpu.VMEM((RP, NG * RP), BF),
            pltpu.VMEM((NG * RP, MSG), BF),
            pltpu.VMEM((NT, RP, SL), BF),
            dma((4,)), dma((NG,)), dma((NG,)), dma((28,)), dma((28,)), dma((42,)), dma((42,)),
            dma((2, NT)), dma((2, NT)), dma((NT,)), dma((NT,)), dma((NG,)), dma((NG,)),
            dma((NT,)), dma((NT,)),
        ],
        compiler_params=pltpu.CompilerParams(
            collective_id=0, has_side_effects=True, vmem_limit_bytes=60 * 1024 * 1024
        ),
        cost_estimate=pl.CostEstimate(flops=8 * 10**9, bytes_accessed=30 * 10**6, transcendentals=10**6),
    )(
        dest_group, dest_slot, lengths, dec_rows, score_rows, norm_gain.reshape(1, D),
        query_gain.reshape(1, HD), key_gain.reshape(1, HD), doc_ids,
        kv_cache, w_query, w_keyval.reshape(2 * D, HD), w_out,
    )
    return pl.pallas_call(
        place_kernel,
        name="place_rows",
        out_shape=(
            jax.ShapeDtypeStruct((R, D), BF),
            jax.ShapeDtypeStruct((R, 2, CTX, HD), BF),
            jax.ShapeDtypeStruct((SH, D), BF),
        ),
        in_specs=[smem] + [vmem] * 2 + [hbm] * 2,
        out_specs=(vmem, hbm, hbm),
        scratch_shapes=[
            pltpu.VMEM((R, 2, CTX, HD), BF),
            pltpu.VMEM((SH, D), BF),
            dma((R,)), dma((R,)), dma((2,)),
        ],
        compiler_params=pltpu.CompilerParams(vmem_limit_bytes=60 * 1024 * 1024),
        cost_estimate=pl.CostEstimate(flops=10**6, bytes_accessed=12 * 10**6, transcendentals=0),
    )(plan, patch, dec_out16, got, score_sum)


def solution(mesh):
    placed = (
        P("group", None),
        P("group", None, None, "tp"),
        P(),
        P(),
        P(),
        P(("group", "tp"), None),
        P("group", None),
        P(),
        P(),
        P(),
        P(None, "tp"),
        P(None, None, "tp"),
        P("tp", None),
    )
    return jax.shard_map(
        per_device,
        mesh=mesh,
        in_specs=placed,
        out_specs=(P("group", None), P("group", None, None, "tp"), P(("group", "tp"), None)),
        check_vma=False,
    )
```

```python
import functools
import math

import jax
import jax.numpy as jnp
from jax import lax
from jax.experimental import pallas as pl
from jax.experimental.pallas import tpu as pltpu
from jax.sharding import PartitionSpec as P

HD = 128
EPS = 1e-06
MESH = pl.DeviceIdType.MESH
BF = jnp.bfloat16
F32 = jnp.float32
LOW = -1e30
INV = 1.0 / math.sqrt(HD)

D = 5120
CTX = 768
NG = 16
NT = 8
R = 14
RP = 16
SH = 56
SP = 64
TOK = NT * SP
HALF = D // 2
QUART = D // 4
SL = D // NT
MSG = SL + 4 * HD
GATHER_CUTS = ((0, 112),)
SUM_CUTS = ((0, 112),)


def head_norm(vectors, gain):
    mean = jnp.mean(vectors * vectors, axis=-1, keepdims=True)
    return (vectors * lax.rsqrt(mean + EPS) * gain).astype(BF)


def dot(a, b):
    return jnp.dot(a, b, preferred_element_type=F32)


class Several:
    def __init__(self, copies):
        self.copies = copies

    def start(self):
        for copy in self.copies:
            copy.start()

    def wait_recv(self):
        for copy in self.copies:
            copy.wait_recv()

    def wait_send(self):
        for copy in self.copies:
            copy.wait_send()


def dot_t(a, b):
    return lax.dot_general(a, b, (((1,), (1,)), ((), ())), preferred_element_type=F32)


def main_kernel(
    dest_ref, slot_ref, len_ref,
    dec_ref, score_ref, gain_ref, qgain_ref, kgain_ref, doc_ref,
    cache_hbm, wq_hbm, wkv_hbm, wo_hbm,
    got_ref, patch_ref, plan_ref, dec_out_ref, score_out_ref,
    cache, wkv, wqkv, wo, xin, docr_ref, docc_ref, packed, xg, xn, sc, qs, kt, vs, terms,
    relay, arrive, cross, through_x, through_z, through_cross, score_sum, part, gather_part, xbuf, nx, scores, pick, fin, obuf,
    load_sem, a2a_send, a2a_recv, ex_send, ex_recv, zi_send, zi_recv, zo_send, zo_recv, ag_send, ag_recv, rs_send, rs_recv,
    dp_send, dp_recv, dx_send, dx_recv, fin_send, fin_recv, o_send, o_recv,
):
    g = lax.axis_index("group")
    t = lax.axis_index("tp")
    y, h = t // 2, t % 2
    z, xl, core = g // 4, (g // 2) % 2, g % 2
    oh = 1 - h
    up, down, far = (y + 1) % 4, (y + 3) % 4, (y + 2) % 4
    mine, partner = t, y * 2 + oh
    g_x = z * 4 + (1 - xl) * 2 + core
    to_up, to_down = {"tp": up * 2 + h}, {"tp": down * 2 + h}
    via_same, via_other = (g_x, t), (g_x, partner)

    def remote(src, dst, send, recv, device):
        return pltpu.make_async_remote_copy(
            src_ref=src, dst_ref=dst, send_sem=send, recv_sem=recv,
            device_id=device, device_id_type=MESH,
        )

    loads = [
        pltpu.make_async_copy(cache_hbm, cache, load_sem.at[0]),
        pltpu.make_async_copy(wq_hbm, wqkv.at[:, pl.ds(0, 512)], load_sem.at[1]),
        pltpu.make_async_copy(wkv_hbm, wkv, load_sem.at[2]),
        pltpu.make_async_copy(wo_hbm, wo, load_sem.at[3]),
    ]
    for load in loads:
        load.start()

    barrier = pltpu.get_barrier_semaphore()

    def greet_tp(k, c):
        pl.semaphore_signal(barrier, inc=1, device_id={"tp": (t + k) % NT}, device_id_type=MESH)
        return c

    def greet_group(k, c):
        pl.semaphore_signal(barrier, inc=1, device_id={"group": (g + k) % NG}, device_id_type=MESH)
        return c

    lax.fori_loop(1, NT, greet_tp, 0)
    lax.fori_loop(1, NG, greet_group, 0)
    pl.semaphore_signal(barrier, inc=1, device_id=(g_x, partner), device_id_type=MESH)

    for a in range(2):
        lo = score_ref[:, a * HALF : a * HALF + QUART].astype(F32)
        hi = score_ref[:, a * HALF + QUART : (a + 1) * HALF].astype(F32)
        xg[mine, a] = jnp.concatenate([lo, hi], axis=0).astype(BF)

    pl.semaphore_wait(barrier, NT + NG - 1)

    def pieces(cuts, src, dst, send, recv, base, device):
        return [
            remote(
                src.at[pl.ds(lo, n), :], dst.at[pl.ds(lo, n), :],
                send.at[base + i], recv.at[base + i], device,
            )
            for i, (lo, n) in enumerate(cuts)
        ]

    def ag(base, shard, halves, device):
        copies = []
        for i, a in enumerate(halves):
            where = xg.at[shard, a]
            copies += pieces(GATHER_CUTS, where, where, ag_send, ag_recv, base + 2 * i, device)
        return Several(copies)

    def exchange(src, through, dst, send, recv):
        ins = [
            remote(src.at[a], through.at[a], send.at[a], recv.at[a], device)
            for a, device in enumerate((via_same, via_other))
        ]
        outs = [
            remote(through.at[a], dst(a), send.at[2 + a], recv.at[2 + a], device)
            for a, device in enumerate((via_other, via_same))
        ]
        return ins, outs

    x_in, x_out = exchange(
        xg.at[mine], through_x, lambda a: xg.at[(mine, partner)[a], a], ex_send.at[0], ex_recv.at[0]
    )
    first_up, first_down = ag(4, mine, (0, 1), to_up), ag(8, mine, (0, 1), to_down)
    for c in (*x_in, first_up, first_down):
        c.start()
    second_up, second_down = ag(12, partner, (0, 1), to_up), ag(16, partner, (0, 1), to_down)
    fwd_up = [ag(20 + 2 * i, down * 2 + hh, (0,), to_up) for i, hh in enumerate((h, oh))]
    fwd_down = [ag(24 + 2 * i, up * 2 + hh, (1,), to_down) for i, hh in enumerate((h, oh))]

    def target_of(j):
        dz, dx, dc = j // 4, (j // 2) % 2, j % 2
        return ((z + dz) % 4) * 4 + ((xl + dx) % 2) * 2 + (core + dc) % 2

    def a2a(j):
        device = {"group": target_of(j)}
        return remote(packed.at[j], got_ref.at[g], a2a_send.at[j], a2a_recv.at[j], device)

    def fill(j, target):
        row = 0
        for r in range(1, R):
            row = jnp.where(dest_ref[g * R + r] == target, r, row)
        for kv in range(2):
            packed[j, kv] = cache[row, kv]

    def send_caches(*rows):
        for j in rows:
            fill(j, target_of(j))
            a2a(j).start()

    z_next, z_last = ((z + 1) % 4) * 4 + xl * 2 + core, ((z + 3) % 4) * 4 + xl * 2 + core

    def z_in(m, kv):
        return remote(
            packed.at[8 + m, kv], through_z.at[kv, m], zi_send.at[kv, m], zi_recv.at[kv, m],
            {"group": (z_next, z_last)[kv]},
        )

    def z_out(m, kv):
        onward, source = ((z_next // 4, z_last), (z_last // 4, z_next))[kv]
        target = onward * 4 + ((xl + m // 2) % 2) * 2 + (core + m % 2) % 2
        return remote(
            through_z.at[kv, m], got_ref.at[source, kv], zo_send.at[kv, m], zo_recv.at[kv, m],
            {"group": target},
        )

    halves_z = [(m, kv) for m in range(4) for kv in range(2)]

    loads[0].wait()
    for m in range(4):
        fill(8 + m, target_of(8 + m))
        z_in(m, 0).start()
        z_in(m, 1).start()
    send_caches(1)
    fill(0, g)
    own_copy = pltpu.make_async_copy(packed.at[0], got_ref.at[g], a2a_send.at[0])
    own_copy.start()

    xin[...] = jnp.zeros_like(xin)
    xin[0:R, :] = dec_ref[...].astype(F32)
    token = lax.broadcasted_iota(jnp.int32, (TOK, NT * SH), 1)
    place = lax.broadcasted_iota(jnp.int32, (TOK, NT * SH), 0)
    inside = (place & (SP - 1)) < SH
    spread = ((place - (place >> 6) * (SP - SH) == token) & inside).astype(F32).astype(BF)
    ids = jnp.broadcast_to(doc_ref[...].astype(F32) + 1.0, (HD, NT * SH)).astype(BF)
    docr_ref[...] = dot_t(ids[:16], spread)
    docc_ref[...] = dot_t(spread, ids)

    lane = lax.broadcasted_iota(jnp.int32, (RP, NG * RP), 1)
    slot_row = lax.broadcasted_iota(jnp.int32, (RP, NG * RP), 0)

    def wanted(e, c):
        want, span = c
        for r in range(R):
            here = jnp.where(dest_ref[e * R + r] == g, slot_ref[e * R + r], -1)
            spot = lane == e * RP + r
            want = jnp.where(spot, here, want)
            span = jnp.where(spot, len_ref[e * R + r], span)
        return want, span

    none = jnp.full((RP, NG * RP), -1, jnp.int32)
    want, span = lax.fori_loop(0, NG, wanted, (none, jnp.zeros_like(none)))
    pick[...] = (want == slot_row).astype(F32).astype(BF)
    source = jnp.sum(jnp.where(want == slot_row, lane >> 4, 0), axis=-1, keepdims=True)
    length = jnp.sum(jnp.where(want == slot_row, span, 0), axis=-1, keepdims=True)
    plan_lane = lax.broadcasted_iota(jnp.int32, (RP, HD), 1)
    plan_ref[...] = jnp.where(plan_lane == 0, source, length)

    row_of = lax.broadcasted_iota(jnp.int32, (4 * RP, HD), 0) & (RP - 1)
    column_row = lax.broadcasted_iota(jnp.int32, (HD, 4 * RP), 1) & (RP - 1)
    lens = jnp.ones((4 * RP, HD), jnp.int32)
    for r in range(R):
        lens = jnp.where(row_of == r, len_ref[g * R + r], lens)
    cached = lax.broadcasted_iota(jnp.int32, (4 * RP, CTX), 1) < lens[:, 0:1]

    def stack4(v):
        return jnp.concatenate([v] * 4, axis=0)

    def dec_project(step, x):
        wide = x.astype(F32)
        scale = lax.rsqrt(jnp.mean(wide * wide, axis=-1, keepdims=True) + EPS)
        nx[...] = (wide * gain_ref[...]).astype(BF)

        def chunk(k, acc):
            cols = pl.ds(pl.multiple_of(k * 1024, 1024), 1024)
            return acc + dot(nx[:, cols], wqkv[cols, :])

        proj = lax.fori_loop(0, 5, chunk, jnp.zeros((RP, 768), F32)) * scale
        q = jnp.concatenate([proj[:, i * HD : (i + 1) * HD] for i in range(4)], axis=0)
        q = head_norm(q, qgain_ref[...])
        return q, (head_norm(proj[:, 512:640], kgain_ref[...]), proj[:, 640:768].astype(BF))

    def dec_weights(q, new):
        qf = q.astype(F32)
        qt = qf.T.astype(BF)

        def chunk(n, c):
            spots = pl.ds(pl.multiple_of(n * HD, HD), HD)
            acc = jnp.zeros((HD, 4 * RP), F32)
            for r in range(R):
                acc = jnp.where(column_row == r, dot(cache[r, 0, spots, :], qt), acc)
            scores[:, spots] = acc.T
            return c

        lax.fori_loop(0, CTX // HD, chunk, 0)
        s = jnp.where(cached, scores[...] * INV, LOW)
        fresh = [
            jnp.sum(qf * stack4(k.astype(F32)), axis=-1, keepdims=True) * INV for k, _ in new
        ]
        top = functools.reduce(jnp.maximum, fresh, jnp.max(s, axis=-1, keepdims=True))
        e = jnp.exp(s - top)
        ef = [jnp.exp(f - top) for f in fresh]
        total = functools.reduce(jnp.add, ef, jnp.sum(e, axis=-1, keepdims=True))
        inv = 1.0 / total
        return (e * inv).astype(BF), [(f * inv).astype(BF).astype(F32) for f in ef]

    def dec_out(step, w, wf, new):
        def value_row(r, acc):
            return acc + jnp.where(row_of == r, dot(w, cache[r, 1]), 0.0)

        o = lax.fori_loop(0, R, value_row, jnp.zeros((4 * RP, HD), F32), unroll=True)
        for f, (_, v) in zip(wf, new):
            o = o + f * stack4(v.astype(F32))
        o = o.astype(BF)
        o = jnp.concatenate([o[i * RP : (i + 1) * RP] for i in range(4)], axis=1)

        def out_slice(p, c):
            part[step, p] = dot(o, wo[:, pl.ds(pl.multiple_of(p * SL, SL), SL)])
            return c

        lax.fori_loop(0, NT, out_slice, 0)
        lax.fori_loop(1, NT, lambda k, c: (part_copy(step, k).start(), c)[1], 0)

    def part_copy(step, k):
        peer = (t + k) % NT
        return remote(
            part.at[step, peer], gather_part.at[step, t],
            dp_send.at[step, k], dp_recv.at[step, k], {"tp": peer},
        )

    def reduce_parts(step, base):
        lax.fori_loop(1, NT, lambda k, c: (part_copy(step, k).wait_recv(), c)[1], 0)
        total = lax.fori_loop(
            1, NT, lambda k, acc: acc + gather_part[step, (t + k) % NT], part[step, t]
        )
        return (base.astype(F32) + total).astype(BF)

    def x_copy(k):
        return remote(xbuf.at[t], xbuf.at[t], dx_send.at[k], dx_recv.at[k], {"tp": (t + k) % NT})

    loads[2].wait()
    to_row = lax.broadcasted_iota(jnp.int32, (256, 256), 0)
    from_row = lax.broadcasted_iota(jnp.int32, (256, 256), 1)
    parting = (from_row == 2 * (to_row & (HD - 1)) + (to_row >= HD).astype(jnp.int32)).astype(F32).astype(BF)

    def part_rows(b, c):
        both = dot(parting, wkv[pl.ds(pl.multiple_of(b * 256, 256), 256), :]).astype(BF)
        rows = pl.ds(pl.multiple_of(b * HD, HD), HD)
        wqkv[rows, 512:640] = both[:HD]
        wqkv[rows, 640:768] = both[HD:]
        return c

    lax.fori_loop(0, D // HD, part_rows, 0, unroll=8)

    def prepare(p, c):
        total = jnp.zeros((SH, 1), F32)
        rows = pl.ds(pl.multiple_of(p * SP, SP), SP)
        for a in range(2):
            both = xg[p, a].astype(F32)
            for i in range(2):
                x = both[i * SH : (i + 1) * SH]
                total = total + jnp.sum(x * x, axis=-1, keepdims=True)
                start = a * HALF + i * QUART
                n = x * gain_ref[:, start : start + QUART]
                n = jnp.concatenate([n, jnp.zeros((SP - SH, QUART), F32)], axis=0)
                xn[rows, start : start + QUART] = n.astype(BF)
        scale = lax.rsqrt(total / D + EPS)
        scale = jnp.concatenate([scale, jnp.zeros((SP - SH, 1), F32)], axis=0)
        sc[rows, :] = jnp.broadcast_to(scale, (SP, HD))
        return c

    def project(block):
        rows = pl.ds(pl.multiple_of(block * 2 * SP, 2 * SP), 2 * SP)

        def tile(j):
            return dot(xn[rows, :], wqkv[:, j * 256 : (j + 1) * 256]) * sc[rows, 0:1]

        for j in range(2):
            v = tile(j)
            for i in range(2):
                qs[2 * j + i, rows, :] = head_norm(v[:, i * HD : (i + 1) * HD], qgain_ref[...])
        v = tile(2)
        k = head_norm(v[:, :HD], kgain_ref[...])
        kt[:, rows] = k.astype(F32).T.astype(BF)
        vs[rows, :] = v[:, HD:].astype(BF)

    for a in range(2):
        x_in[a].wait_recv()
        x_out[a].start()
    loads[1].wait()
    q0, new0 = dec_project(0, xin[...])
    for a in range(2):
        x_out[a].wait_recv()
    second_up.start()
    second_down.start()
    first_up.wait_recv()
    fwd_up[0].start()
    first_down.wait_recv()
    fwd_down[0].start()
    send_caches(2, 3)
    w0, wf0 = dec_weights(q0, [new0])
    loads[3].wait()
    dec_out(0, w0, wf0, [new0])
    for m, kv in halves_z:
        z_in(m, kv).wait_recv()
        z_out(m, kv).start()
    prepare(mine, 0)
    prepare(partner, 0)
    project(y)
    prepare(down * 2 + h, 0)
    prepare(up * 2 + h, 0)

    base0 = xin[:, pl.ds(pl.multiple_of(t * SL, SL), SL)]
    xbuf[t] = reduce_parts(0, base0)
    lax.fori_loop(1, NT, lambda k, c: (x_copy(k).start(), c)[1], 0)

    second_up.wait_recv()
    fwd_up[1].start()
    second_down.wait_recv()
    fwd_down[1].start()
    send_caches(6, 14, 4, 12)
    prepare(down * 2 + oh, 0)
    project(down)
    prepare(up * 2 + oh, 0)
    project(up)
    lax.fori_loop(1, NT, lambda k, c: (x_copy(k).wait_recv(), c)[1], 0)
    q1, new1 = dec_project(1, jnp.concatenate([xbuf[p] for p in range(NT)], axis=1))
    fwd_up[0].wait_recv()
    fwd_down[0].wait_recv()
    prepare(far * 2 + h, 0)
    fwd_up[1].wait_recv()
    fwd_down[1].wait_recv()
    prepare(far * 2 + oh, 0)
    project(far)
    send_caches(7, 15)

    later_col = lax.broadcasted_iota(jnp.int32, (2 * SP, TOK), 1)
    later_row = lax.broadcasted_iota(jnp.int32, (2 * SP, TOK), 0)

    def attend(block):
        rows = pl.ds(pl.multiple_of(block * 2 * SP, 2 * SP), 2 * SP)
        live = (docc_ref[rows, 0:1] == docr_ref[0:1, :]) & (later_col <= later_row + block * (2 * SP))
        heads = []
        for i in range(4):
            s = jnp.where(live, dot(qs[i, rows, :], kt[...]) * INV, LOW)
            e = jnp.exp(s - jnp.max(s, axis=-1, keepdims=True))
            inv = 1.0 / jnp.sum(e, axis=-1, keepdims=True)
            heads.append(dot((e * inv).astype(BF), vs[...]).astype(BF))
        attn = jnp.concatenate(heads, axis=1)
        for a in range(2):
            lo, hi = [
                dot(attn, wo[:, a * HALF + i * QUART : a * HALF + (i + 1) * QUART]) for i in range(2)
            ]
            for i in range(2):
                pair = [v[i * SP : i * SP + SH] for v in (lo, hi)]
                terms[block * 2 + i, a] = jnp.concatenate(pair, axis=0).astype(BF)

    order = (oh, h)

    def rs(n, src, dst, device):
        return Several(pieces(SUM_CUTS, src, dst, rs_send, rs_recv, 3 * n, device))

    far_up = [rs(i, terms.at[far * 2 + order[i], 0], relay.at[0, i], to_up) for i in range(2)]
    far_down = [rs(2 + i, terms.at[far * 2 + order[i], 1], relay.at[1, i], to_down) for i in range(2)]
    near_up = [
        [rs(4 + 2 * i + a, terms.at[up * 2 + order[i], a], arrive.at[0, i, a], to_up) for a in range(2)]
        for i in range(2)
    ]
    near_down = [
        [rs(8 + 2 * i + a, terms.at[down * 2 + order[i], a], arrive.at[1, i, a], to_down) for a in range(2)]
        for i in range(2)
    ]
    over_in, over = exchange(
        cross.at[0], through_cross, lambda a: cross.at[1, a], ex_send.at[1], ex_recv.at[1]
    )

    def relay_up(i):
        far_up[i].wait_recv()
        spot = up * 2 + order[i]
        terms[spot, 0] = (terms[spot, 0].astype(F32) + relay[0, i].astype(F32)).astype(BF)
        near_up[i][0].start()

    def relay_down(i):
        far_down[i].wait_recv()
        spot = down * 2 + order[i]
        terms[spot, 1] = (terms[spot, 1].astype(F32) + relay[1, i].astype(F32)).astype(BF)
        near_down[i][1].start()

    def summed(i, a):
        near_up[i][a].wait_recv()
        near_down[i][a].wait_recv()
        return (
            terms[y * 2 + order[i], a].astype(F32)
            + arrive[0, i, a].astype(F32)
            + arrive[1, i, a].astype(F32)
        )

    attend(far)
    far_up[0].start()
    far_down[0].start()
    attend(up)
    attend(down)
    far_up[0].wait_send()
    near_up[0][1].start()
    far_down[0].wait_send()
    near_down[0][0].start()
    relay_up(0)
    relay_down(0)
    send_caches(5, 13)
    w1, wf1 = dec_weights(q1, [new0, new1])
    dec_out(1, w1, wf1, [new0, new1])
    attend(y)
    near_up[0][0].wait_send()
    far_up[1].start()
    near_down[0][1].wait_send()
    far_down[1].start()
    for a in range(2):
        cross[0, a] = summed(0, a).astype(BF)
        over_in[a].start()

    mine_rows = pl.ds(pl.multiple_of(g * RP, RP), RP)
    fin[mine_rows, 0:SL] = reduce_parts(1, xbuf[t])
    for i, (k, v) in enumerate([new0, new1]):
        start = SL + 2 * i * HD
        fin[mine_rows, start : start + HD] = k
        fin[mine_rows, start + HD : start + 2 * HD] = v

    def fin_copy(k):
        where = fin.at[mine_rows]
        return remote(where, where, fin_send.at[k], fin_recv.at[k], {"group": (g + k) % NG})

    lax.fori_loop(1, NG, lambda k, c: (fin_copy(k).start(), c)[1], 0)

    far_up[1].wait_send()
    near_up[1][1].start()
    far_down[1].wait_send()
    near_down[1][0].start()
    for a in range(2):
        over_in[a].wait_recv()
        over[a].start()
    relay_up(1)
    relay_down(1)

    for a in range(2):
        near = summed(1, a)
        for i in range(2):
            cols = slice(a * HALF + i * QUART, a * HALF + (i + 1) * QUART)
            add = near[i * SH : (i + 1) * SH]
            score_sum[:, cols] = score_ref[:, cols].astype(F32) + add

    lax.fori_loop(1, NG, lambda k, c: (fin_copy(k).wait_recv(), c)[1], 0)
    placed = dot(pick[...], fin[...])
    obuf[t] = placed[:, :SL].astype(BF)
    patch_ref[...] = placed[:, SL:]

    def o_copy(k):
        return remote(obuf.at[t], obuf.at[t], o_send.at[k], o_recv.at[k], {"tp": (t + k) % NT})

    lax.fori_loop(1, NT, lambda k, c: (o_copy(k).start(), c)[1], 0)

    for a in range(2):
        over[a].wait_recv()
        far_half = cross[1, a].astype(F32)
        for i in range(2):
            cols = slice(a * HALF + i * QUART, a * HALF + (i + 1) * QUART)
            add = far_half[i * SH : (i + 1) * SH]
            score_out_ref[:, cols] = (score_sum[:, cols] + add).astype(BF)

    lax.fori_loop(1, NT, lambda k, c: (o_copy(k).wait_recv(), c)[1], 0)
    for p in range(NT):
        dec_out_ref[:, p * SL : (p + 1) * SL] = obuf[p]

    def end_a2a(j, c):
        a2a(j).wait()
        return c

    lax.fori_loop(1, 8, end_a2a, 0)
    lax.fori_loop(12, NG, end_a2a, 0)
    for m, kv in halves_z:
        z_out(m, kv).wait()
    own_copy.wait()
    ended = [first_up, first_down, second_up, second_down] + fwd_up + fwd_down
    ended += x_in + x_out + over_in + over + [z_in(m, kv) for m, kv in halves_z]
    ended += near_up[1] + near_down[1] + [near_up[0][1], near_down[0][0]]
    for c in ended:
        c.wait_send()

    def end_tp(k, c):
        part_copy(0, k).wait_send()
        part_copy(1, k).wait_send()
        x_copy(k).wait_send()
        o_copy(k).wait_send()
        return c

    lax.fori_loop(1, NT, end_tp, 0)
    lax.fori_loop(1, NG, lambda k, c: (fin_copy(k).wait_send(), c)[1], 0)


def place_kernel(
    plan_ref, patch_ref, dec_ref, got_hbm, score_hbm,
    dec_out_ref, cache_out, score_out, rows, score_rows, in_sem, out_sem, score_sem,
):
    score_in = pltpu.make_async_copy(score_hbm, score_rows, score_sem.at[0])
    score_end = pltpu.make_async_copy(score_rows, score_out, score_sem.at[1])
    score_in.start()

    def get(s, c):
        pltpu.make_async_copy(got_hbm.at[plan_ref[s, 0]], rows.at[s], in_sem.at[s]).start()
        return c

    lax.fori_loop(0, R, get, 0)
    dec_out_ref[...] = dec_ref[:R, :]
    score_in.wait()
    score_end.start()

    def put(s, c):
        pltpu.make_async_copy(got_hbm.at[0], rows.at[s], in_sem.at[s]).wait()
        entry = patch_ref[pl.ds(s, 1), :]
        for step in range(2):
            pos = plan_ref[s, 1] + step
            base = pl.multiple_of((pos // 16) * 16, 16)
            here = lax.broadcasted_iota(jnp.int32, (16, HD), 0) == pos - base
            for kv in range(2):
                start = (2 * step + kv) * HD
                old = rows[s, kv, pl.ds(base, 16), :].astype(F32)
                both = jnp.where(here, entry[:, start : start + HD], old)
                rows[s, kv, pl.ds(base, 16), :] = both.astype(BF)
        pltpu.make_async_copy(rows.at[s], cache_out.at[s], out_sem.at[s]).start()
        return c

    lax.fori_loop(0, R, put, 0)

    def end(s, c):
        pltpu.make_async_copy(rows.at[s], cache_out.at[s], out_sem.at[s]).wait()
        return c

    lax.fori_loop(0, R, end, 0)
    score_end.wait()


def per_device(
    dec_rows, kv_cache, lengths, dest_group, dest_slot, score_rows, doc_ids,
    norm_gain, query_gain, key_gain, w_query, w_keyval, w_out,
):
    smem = pl.BlockSpec(memory_space=pltpu.SMEM)
    vmem = pl.BlockSpec(memory_space=pltpu.VMEM)
    hbm = pl.BlockSpec(memory_space=pl.ANY)
    dma = pltpu.SemaphoreType.DMA
    got, patch, plan, dec_out16, score_sum = pl.pallas_call(
        main_kernel,
        name="decode_and_score",
        out_shape=(
            jax.ShapeDtypeStruct((NG, 2, CTX, HD), BF),
            jax.ShapeDtypeStruct((RP, 4 * HD), F32),
            jax.ShapeDtypeStruct((RP, HD), jnp.int32),
            jax.ShapeDtypeStruct((RP, D), BF),
            jax.ShapeDtypeStruct((SH, D), BF),
        ),
        in_specs=[smem] * 3 + [vmem] * 6 + [hbm] * 4,
        out_specs=(hbm, vmem, vmem, vmem, vmem),
        scratch_shapes=[
            pltpu.VMEM((R, 2, CTX, HD), BF),
            pltpu.VMEM((2 * D, HD), BF),
            pltpu.VMEM((D, 768), BF),
            pltpu.VMEM((512, D), BF),
            pltpu.VMEM((RP, D), F32),
            pltpu.VMEM((16, TOK), F32),
            pltpu.VMEM((TOK, HD), F32),
            pltpu.VMEM((NG, 2, CTX, HD), BF),
            pltpu.VMEM((NT, 2, 2 * SH, QUART), BF),
            pltpu.VMEM((TOK, D), BF),
            pltpu.VMEM((TOK, HD), F32),
            pltpu.VMEM((4, TOK, HD), BF),
            pltpu.VMEM((HD, TOK), BF),
            pltpu.VMEM((TOK, HD), BF),
            pltpu.VMEM((NT, 2, 2 * SH, QUART), BF),
            pltpu.VMEM((2, 2, 2 * SH, QUART), BF),
            pltpu.VMEM((2, 2, 2, 2 * SH, QUART), BF),
            pltpu.VMEM((2, 2, 2 * SH, QUART), BF),
            pltpu.VMEM((2, 2 * SH, QUART), BF),
            pltpu.VMEM((2, 4, CTX, HD), BF),
            pltpu.VMEM((2, 2 * SH, QUART), BF),
            pltpu.VMEM((SH, D), F32),
            pltpu.VMEM((2, NT, RP, SL), F32),
            pltpu.VMEM((2, NT, RP, SL), F32),
            pltpu.VMEM((NT, RP, SL), BF),
            pltpu.VMEM((RP, D), BF),
            pltpu.VMEM((4 * RP, CTX), F32),
            pltpu.VMEM((RP, NG * RP), BF),
            pltpu.VMEM((NG * RP, MSG), BF),
            pltpu.VMEM((NT, RP, SL), BF),
            dma((4,)), dma((NG,)), dma((NG,)), dma((2, 4)), dma((2, 4)), dma((2, 4)), dma((2, 4)), dma((2, 4)), dma((2, 4)), dma((28,)), dma((28,)), dma((42,)), dma((42,)),
            dma((2, NT)), dma((2, NT)), dma((NT,)), dma((NT,)), dma((NG,)), dma((NG,)),
            dma((NT,)), dma((NT,)),
        ],
        compiler_params=pltpu.CompilerParams(
            collective_id=0, has_side_effects=True, vmem_limit_bytes=60 * 1024 * 1024
        ),
        cost_estimate=pl.CostEstimate(flops=8 * 10**9, bytes_accessed=30 * 10**6, transcendentals=10**6),
    )(
        dest_group, dest_slot, lengths, dec_rows, score_rows, norm_gain.reshape(1, D),
        query_gain.reshape(1, HD), key_gain.reshape(1, HD), doc_ids,
        kv_cache, w_query, w_keyval.reshape(2 * D, HD), w_out,
    )
    return pl.pallas_call(
        place_kernel,
        name="place_rows",
        out_shape=(
            jax.ShapeDtypeStruct((R, D), BF),
            jax.ShapeDtypeStruct((R, 2, CTX, HD), BF),
            jax.ShapeDtypeStruct((SH, D), BF),
        ),
        in_specs=[smem] + [vmem] * 2 + [hbm] * 2,
        out_specs=(vmem, hbm, hbm),
        scratch_shapes=[
            pltpu.VMEM((R, 2, CTX, HD), BF),
            pltpu.VMEM((SH, D), BF),
            dma((R,)), dma((R,)), dma((2,)),
        ],
        compiler_params=pltpu.CompilerParams(vmem_limit_bytes=60 * 1024 * 1024),
        cost_estimate=pl.CostEstimate(flops=10**6, bytes_accessed=12 * 10**6, transcendentals=0),
    )(plan, patch, dec_out16, got, score_sum)


def solution(mesh):
    placed = (
        P("group", None),
        P("group", None, None, "tp"),
        P(),
        P(),
        P(),
        P(("group", "tp"), None),
        P("group", None),
        P(),
        P(),
        P(),
        P(None, "tp"),
        P(None, None, "tp"),
        P("tp", None),
    )
    return jax.shard_map(
        per_device,
        mesh=mesh,
        in_specs=placed,
        out_specs=(P("group", None), P("group", None, None, "tp"), P(("group", "tp"), None)),
        check_vma=False,
    )
```

```python
import functools
import math

import jax
import jax.numpy as jnp
from jax import lax
from jax.experimental import pallas as pl
from jax.experimental.pallas import tpu as pltpu
from jax.sharding import PartitionSpec as P

HD = 128
EPS = 1e-06
MESH = pl.DeviceIdType.MESH
BF = jnp.bfloat16
F32 = jnp.float32
LOW = -1e30
INV = 1.0 / math.sqrt(HD)

D = 5120
CTX = 768
NG = 16
NT = 8
R = 14
RP = 16
SH = 56
SP = 64
TOK = NT * SP
HALF = D // 2
QUART = D // 4
SL = D // NT
MSG = SL + 4 * HD
WAVE = 5
GATHER_CUTS = ((0, 112),)
SUM_CUTS = ((0, 112),)


def head_norm(vectors, gain):
    mean = jnp.mean(vectors * vectors, axis=-1, keepdims=True)
    return (vectors * lax.rsqrt(mean + EPS) * gain).astype(BF)


def dot(a, b):
    return jnp.dot(a, b, preferred_element_type=F32)


class Several:
    def __init__(self, copies):
        self.copies = copies

    def start(self):
        for copy in self.copies:
            copy.start()

    def wait_recv(self):
        for copy in self.copies:
            copy.wait_recv()

    def wait_send(self):
        for copy in self.copies:
            copy.wait_send()


def dot_t(a, b):
    return lax.dot_general(a, b, (((1,), (1,)), ((), ())), preferred_element_type=F32)


def main_kernel(
    dest_ref, slot_ref, len_ref,
    gain_ref, qgain_ref, kgain_ref, doc_ref,
    cache_hbm, wq_hbm, wkv_hbm, wo_hbm, score_hbm, dec_hbm,
    got_ref, patch_ref, plan_ref, dec_out_ref, score_out_ref,
    score_ref, dec_ref, cache, wkv, wqkv, wo, xin, docr_ref, docc_ref, packed, xg, xn, sc, qs, kt, vs, terms,
    relay, arrive, cross, through_x, through_z, through_cross, score_sum, part, gather_part, xbuf, nx, scores, pick, fin, obuf,
    load_sem, a2a_send, a2a_recv, ex_send, ex_recv, zi_send, zi_recv, zo_send, zo_recv, ag_send, ag_recv, rs_send, rs_recv,
    dp_send, dp_recv, dx_send, dx_recv, fin_send, fin_recv, o_send, o_recv,
):
    g = lax.axis_index("group")
    t = lax.axis_index("tp")
    y, h = t // 2, t % 2
    z, xl, core = g // 4, (g // 2) % 2, g % 2
    oh = 1 - h
    up, down, far = (y + 1) % 4, (y + 3) % 4, (y + 2) % 4
    mine, partner = t, y * 2 + oh
    g_x = z * 4 + (1 - xl) * 2 + core
    to_up, to_down = {"tp": up * 2 + h}, {"tp": down * 2 + h}
    via_same, via_other = (g_x, t), (g_x, partner)

    def remote(src, dst, send, recv, device):
        return pltpu.make_async_remote_copy(
            src_ref=src, dst_ref=dst, send_sem=send, recv_sem=recv,
            device_id=device, device_id_type=MESH,
        )

    barrier = pltpu.get_barrier_semaphore()

    def greet_tp(k, c):
        pl.semaphore_signal(barrier, inc=1, device_id={"tp": (t + k) % NT}, device_id_type=MESH)
        return c

    def greet_group(k, c):
        pl.semaphore_signal(barrier, inc=1, device_id={"group": (g + k) % NG}, device_id_type=MESH)
        return c

    lax.fori_loop(1, NT, greet_tp, 0)
    lax.fori_loop(1, NG, greet_group, 0)
    pl.semaphore_signal(barrier, inc=1, device_id=(g_x, partner), device_id_type=MESH)

    loads = [
        pltpu.make_async_copy(cache_hbm, cache, load_sem.at[0]),
        pltpu.make_async_copy(wq_hbm, wqkv.at[:, pl.ds(0, 512)], load_sem.at[1]),
        pltpu.make_async_copy(wkv_hbm, wkv, load_sem.at[2]),
        pltpu.make_async_copy(wo_hbm, wo, load_sem.at[3]),
        pltpu.make_async_copy(score_hbm, score_ref, load_sem.at[4]),
        pltpu.make_async_copy(dec_hbm, dec_ref, load_sem.at[5]),
    ]
    for i in (4, 0, 5, 2, 1, 3):
        loads[i].start()

    loads[4].wait()
    for a in range(2):
        lo = score_ref[:, a * HALF : a * HALF + QUART].astype(F32)
        hi = score_ref[:, a * HALF + QUART : (a + 1) * HALF].astype(F32)
        xg[mine, a] = jnp.concatenate([lo, hi], axis=0).astype(BF)

    pl.semaphore_wait(barrier, NT + NG - 1)

    def pieces(cuts, src, dst, send, recv, base, device):
        return [
            remote(
                src.at[pl.ds(lo, n), :], dst.at[pl.ds(lo, n), :],
                send.at[base + i], recv.at[base + i], device,
            )
            for i, (lo, n) in enumerate(cuts)
        ]

    def ag(base, shard, halves, device):
        copies = []
        for i, a in enumerate(halves):
            where = xg.at[shard, a]
            copies += pieces(GATHER_CUTS, where, where, ag_send, ag_recv, base + 2 * i, device)
        return Several(copies)

    def exchange(src, through, dst, send, recv):
        ins = [
            remote(src.at[a], through.at[a], send.at[a], recv.at[a], device)
            for a, device in enumerate((via_same, via_other))
        ]
        outs = [
            remote(through.at[a], dst(a), send.at[2 + a], recv.at[2 + a], device)
            for a, device in enumerate((via_other, via_same))
        ]
        return ins, outs

    x_in, x_out = exchange(
        xg.at[mine], through_x, lambda a: xg.at[(mine, partner)[a], a], ex_send.at[0], ex_recv.at[0]
    )
    first_up, first_down = ag(4, mine, (0, 1), to_up), ag(8, mine, (0, 1), to_down)
    for c in (*x_in, first_up, first_down):
        c.start()
    second_up, second_down = ag(12, partner, (0, 1), to_up), ag(16, partner, (0, 1), to_down)
    fwd_up = [ag(20 + 2 * i, down * 2 + hh, (0,), to_up) for i, hh in enumerate((h, oh))]
    fwd_down = [ag(24 + 2 * i, up * 2 + hh, (1,), to_down) for i, hh in enumerate((h, oh))]

    def target_of(j):
        dz, dx, dc = j // 4, (j // 2) % 2, j % 2
        return ((z + dz) % 4) * 4 + ((xl + dx) % 2) * 2 + (core + dc) % 2

    def a2a(j):
        device = {"group": target_of(j)}
        return remote(packed.at[j], got_ref.at[g], a2a_send.at[j], a2a_recv.at[j], device)

    def fill(j, target):
        row = 0
        for r in range(1, R):
            row = jnp.where(dest_ref[g * R + r] == target, r, row)
        for kv in range(2):
            packed[j, kv] = cache[row, kv]

    def send_caches(*rows):
        for j in rows:
            fill(j, target_of(j))
            a2a(j).start()

    z_next, z_last = ((z + 1) % 4) * 4 + xl * 2 + core, ((z + 3) % 4) * 4 + xl * 2 + core

    def z_in(m, kv):
        return remote(
            packed.at[8 + m, kv], through_z.at[kv, m], zi_send.at[kv, m], zi_recv.at[kv, m],
            {"group": (z_next, z_last)[kv]},
        )

    def z_out(m, kv):
        onward, source = ((z_next // 4, z_last), (z_last // 4, z_next))[kv]
        target = onward * 4 + ((xl + m // 2) % 2) * 2 + (core + m % 2) % 2
        return remote(
            through_z.at[kv, m], got_ref.at[source, kv], zo_send.at[kv, m], zo_recv.at[kv, m],
            {"group": target},
        )

    halves_z = [(m, kv) for m in range(4) for kv in range(2)]

    loads[0].wait()
    for m in range(4):
        fill(8 + m, target_of(8 + m))
        z_in(m, 0).start()
        z_in(m, 1).start()
    send_caches(1)
    fill(0, g)
    own_copy = pltpu.make_async_copy(packed.at[0], got_ref.at[g], a2a_send.at[0])
    own_copy.start()

    loads[5].wait()
    xin[...] = jnp.zeros_like(xin)
    xin[0:R, :] = dec_ref[...].astype(F32)
    token = lax.broadcasted_iota(jnp.int32, (TOK, NT * SH), 1)
    place = lax.broadcasted_iota(jnp.int32, (TOK, NT * SH), 0)
    inside = (place & (SP - 1)) < SH
    spread = ((place - (place >> 6) * (SP - SH) == token) & inside).astype(F32).astype(BF)
    ids = jnp.broadcast_to(doc_ref[...].astype(F32) + 1.0, (HD, NT * SH)).astype(BF)
    docr_ref[...] = dot_t(ids[:16], spread)
    docc_ref[...] = dot_t(spread, ids)

    lane = lax.broadcasted_iota(jnp.int32, (RP, NG * RP), 1)
    slot_row = lax.broadcasted_iota(jnp.int32, (RP, NG * RP), 0)

    def wanted(e, c):
        want, span = c
        for r in range(R):
            here = jnp.where(dest_ref[e * R + r] == g, slot_ref[e * R + r], -1)
            spot = lane == e * RP + r
            want = jnp.where(spot, here, want)
            span = jnp.where(spot, len_ref[e * R + r], span)
        return want, span

    none = jnp.full((RP, NG * RP), -1, jnp.int32)
    want, span = lax.fori_loop(0, NG, wanted, (none, jnp.zeros_like(none)))
    pick[...] = (want == slot_row).astype(F32).astype(BF)
    source = jnp.sum(jnp.where(want == slot_row, lane >> 4, 0), axis=-1, keepdims=True)
    length = jnp.sum(jnp.where(want == slot_row, span, 0), axis=-1, keepdims=True)
    plan_lane = lax.broadcasted_iota(jnp.int32, (RP, HD), 1)
    plan_ref[...] = jnp.where(plan_lane == 0, source, length)

    row_of = lax.broadcasted_iota(jnp.int32, (4 * RP, HD), 0) & (RP - 1)
    column_row = lax.broadcasted_iota(jnp.int32, (HD, 4 * RP), 1) & (RP - 1)
    lens = jnp.ones((4 * RP, HD), jnp.int32)
    for r in range(R):
        lens = jnp.where(row_of == r, len_ref[g * R + r], lens)
    cached = lax.broadcasted_iota(jnp.int32, (4 * RP, CTX), 1) < lens[:, 0:1]

    def stack4(v):
        return jnp.concatenate([v] * 4, axis=0)

    def dec_project(step, x):
        wide = x.astype(F32)
        scale = lax.rsqrt(jnp.mean(wide * wide, axis=-1, keepdims=True) + EPS)
        nx[...] = (wide * gain_ref[...]).astype(BF)

        def chunk(k, acc):
            cols = pl.ds(pl.multiple_of(k * 1024, 1024), 1024)
            return acc + dot(nx[:, cols], wqkv[cols, :])

        proj = lax.fori_loop(0, 5, chunk, jnp.zeros((RP, 768), F32)) * scale
        q = jnp.concatenate([proj[:, i * HD : (i + 1) * HD] for i in range(4)], axis=0)
        q = head_norm(q, qgain_ref[...])
        return q, (head_norm(proj[:, 512:640], kgain_ref[...]), proj[:, 640:768].astype(BF))

    def dec_weights(q, new):
        qf = q.astype(F32)
        qt = qf.T.astype(BF)

        def chunk(n, c):
            spots = pl.ds(pl.multiple_of(n * HD, HD), HD)
            acc = jnp.zeros((HD, 4 * RP), F32)
            for r in range(R):
                acc = jnp.where(column_row == r, dot(cache[r, 0, spots, :], qt), acc)
            scores[:, spots] = acc.T
            return c

        lax.fori_loop(0, CTX // HD, chunk, 0)
        s = jnp.where(cached, scores[...] * INV, LOW)
        fresh = [
            jnp.sum(qf * stack4(k.astype(F32)), axis=-1, keepdims=True) * INV for k, _ in new
        ]
        top = functools.reduce(jnp.maximum, fresh, jnp.max(s, axis=-1, keepdims=True))
        e = jnp.exp(s - top)
        ef = [jnp.exp(f - top) for f in fresh]
        total = functools.reduce(jnp.add, ef, jnp.sum(e, axis=-1, keepdims=True))
        inv = 1.0 / total
        return (e * inv).astype(BF), [(f * inv).astype(BF).astype(F32) for f in ef]

    def dec_out(step, w, wf, new):
        def value_row(r, acc):
            return acc + jnp.where(row_of == r, dot(w, cache[r, 1]), 0.0)

        o = lax.fori_loop(0, R, value_row, jnp.zeros((4 * RP, HD), F32), unroll=True)
        for f, (_, v) in zip(wf, new):
            o = o + f * stack4(v.astype(F32))
        o = o.astype(BF)
        o = jnp.concatenate([o[i * RP : (i + 1) * RP] for i in range(4)], axis=1)

        def out_slice(p, c):
            part[step, p] = dot(o, wo[:, pl.ds(pl.multiple_of(p * SL, SL), SL)])
            return c

        lax.fori_loop(0, NT, out_slice, 0)
        lax.fori_loop(1, NT, lambda k, c: (part_copy(step, k).start(), c)[1], 0)

    def part_copy(step, k):
        peer = (t + k) % NT
        return remote(
            part.at[step, peer], gather_part.at[step, t],
            dp_send.at[step, k], dp_recv.at[step, k], {"tp": peer},
        )

    def reduce_parts(step, base):
        lax.fori_loop(1, NT, lambda k, c: (part_copy(step, k).wait_recv(), c)[1], 0)
        total = lax.fori_loop(
            1, NT, lambda k, acc: acc + gather_part[step, (t + k) % NT], part[step, t]
        )
        return (base.astype(F32) + total).astype(BF)

    def x_copy(k):
        return remote(xbuf.at[t], xbuf.at[t], dx_send.at[k], dx_recv.at[k], {"tp": (t + k) % NT})

    loads[2].wait()
    to_row = lax.broadcasted_iota(jnp.int32, (256, 256), 0)
    from_row = lax.broadcasted_iota(jnp.int32, (256, 256), 1)
    parting = (from_row == 2 * (to_row & (HD - 1)) + (to_row >= HD).astype(jnp.int32)).astype(F32).astype(BF)

    def part_rows(b, c):
        both = dot(parting, wkv[pl.ds(pl.multiple_of(b * 256, 256), 256), :]).astype(BF)
        rows = pl.ds(pl.multiple_of(b * HD, HD), HD)
        wqkv[rows, 512:640] = both[:HD]
        wqkv[rows, 640:768] = both[HD:]
        return c

    lax.fori_loop(0, D // HD, part_rows, 0, unroll=8)

    def prepare(p, c):
        total = jnp.zeros((SH, 1), F32)
        rows = pl.ds(pl.multiple_of(p * SP, SP), SP)
        for a in range(2):
            both = xg[p, a].astype(F32)
            for i in range(2):
                x = both[i * SH : (i + 1) * SH]
                total = total + jnp.sum(x * x, axis=-1, keepdims=True)
                start = a * HALF + i * QUART
                n = x * gain_ref[:, start : start + QUART]
                n = jnp.concatenate([n, jnp.zeros((SP - SH, QUART), F32)], axis=0)
                xn[rows, start : start + QUART] = n.astype(BF)
        scale = lax.rsqrt(total / D + EPS)
        scale = jnp.concatenate([scale, jnp.zeros((SP - SH, 1), F32)], axis=0)
        sc[rows, :] = jnp.broadcast_to(scale, (SP, HD))
        return c

    def project(block):
        rows = pl.ds(pl.multiple_of(block * 2 * SP, 2 * SP), 2 * SP)

        def tile(j):
            return dot(xn[rows, :], wqkv[:, j * 256 : (j + 1) * 256]) * sc[rows, 0:1]

        for j in range(2):
            v = tile(j)
            for i in range(2):
                qs[2 * j + i, rows, :] = head_norm(v[:, i * HD : (i + 1) * HD], qgain_ref[...])
        v = tile(2)
        k = head_norm(v[:, :HD], kgain_ref[...])
        kt[:, rows] = k.astype(F32).T.astype(BF)
        vs[rows, :] = v[:, HD:].astype(BF)

    for a in range(2):
        x_in[a].wait_recv()
        x_out[a].start()
    loads[1].wait()
    q0, new0 = dec_project(0, xin[...])
    for a in range(2):
        x_out[a].wait_recv()
    second_up.start()
    second_down.start()
    first_up.wait_recv()
    fwd_up[0].start()
    first_down.wait_recv()
    fwd_down[0].start()
    send_caches(2)
    for m, kv in halves_z[:4]:
        z_in(m, kv).wait_recv()
        z_out(m, kv).start()
    w0, wf0 = dec_weights(q0, [new0])
    loads[3].wait()
    dec_out(0, w0, wf0, [new0])
    for m, kv in halves_z[4:]:
        z_in(m, kv).wait_recv()
        z_out(m, kv).start()
    prepare(mine, 0)
    prepare(partner, 0)
    project(y)
    prepare(down * 2 + h, 0)
    prepare(up * 2 + h, 0)

    base0 = xin[:, pl.ds(pl.multiple_of(t * SL, SL), SL)]
    xbuf[t] = reduce_parts(0, base0)
    lax.fori_loop(1, NT, lambda k, c: (x_copy(k).start(), c)[1], 0)

    second_up.wait_recv()
    fwd_up[1].start()
    second_down.wait_recv()
    fwd_down[1].start()
    send_caches(3, 6)
    prepare(down * 2 + oh, 0)
    project(down)
    prepare(up * 2 + oh, 0)
    project(up)
    send_caches(14, 4)
    lax.fori_loop(1, NT, lambda k, c: (x_copy(k).wait_recv(), c)[1], 0)
    q1, new1 = dec_project(1, jnp.concatenate([xbuf[p] for p in range(NT)], axis=1))
    fwd_up[0].wait_recv()
    fwd_down[0].wait_recv()
    prepare(far * 2 + h, 0)
    fwd_up[1].wait_recv()
    fwd_down[1].wait_recv()
    prepare(far * 2 + oh, 0)
    project(far)
    send_caches(7, 12)

    later_col = lax.broadcasted_iota(jnp.int32, (2 * SP, TOK), 1)
    later_row = lax.broadcasted_iota(jnp.int32, (2 * SP, TOK), 0)

    def attend(block):
        rows = pl.ds(pl.multiple_of(block * 2 * SP, 2 * SP), 2 * SP)
        live = (docc_ref[rows, 0:1] == docr_ref[0:1, :]) & (later_col <= later_row + block * (2 * SP))
        heads = []
        for i in range(4):
            s = jnp.where(live, dot(qs[i, rows, :], kt[...]) * INV, LOW)
            e = jnp.exp(s - jnp.max(s, axis=-1, keepdims=True))
            inv = 1.0 / jnp.sum(e, axis=-1, keepdims=True)
            heads.append(dot((e * inv).astype(BF), vs[...]).astype(BF))
        attn = jnp.concatenate(heads, axis=1)
        for a in range(2):
            lo, hi = [
                dot(attn, wo[:, a * HALF + i * QUART : a * HALF + (i + 1) * QUART]) for i in range(2)
            ]
            for i in range(2):
                pair = [v[i * SP : i * SP + SH] for v in (lo, hi)]
                terms[block * 2 + i, a] = jnp.concatenate(pair, axis=0).astype(BF)

    order = (oh, h)

    def rs(n, src, dst, device):
        return Several(pieces(SUM_CUTS, src, dst, rs_send, rs_recv, 3 * n, device))

    far_up = [rs(i, terms.at[far * 2 + order[i], 0], relay.at[0, i], to_up) for i in range(2)]
    far_down = [rs(2 + i, terms.at[far * 2 + order[i], 1], relay.at[1, i], to_down) for i in range(2)]
    near_up = [
        [rs(4 + 2 * i + a, terms.at[up * 2 + order[i], a], arrive.at[0, i, a], to_up) for a in range(2)]
        for i in range(2)
    ]
    near_down = [
        [rs(8 + 2 * i + a, terms.at[down * 2 + order[i], a], arrive.at[1, i, a], to_down) for a in range(2)]
        for i in range(2)
    ]
    over_in, over = exchange(
        cross.at[0], through_cross, lambda a: cross.at[1, a], ex_send.at[1], ex_recv.at[1]
    )

    def relay_up(i):
        far_up[i].wait_recv()
        spot = up * 2 + order[i]
        terms[spot, 0] = (terms[spot, 0].astype(F32) + relay[0, i].astype(F32)).astype(BF)
        near_up[i][0].start()

    def relay_down(i):
        far_down[i].wait_recv()
        spot = down * 2 + order[i]
        terms[spot, 1] = (terms[spot, 1].astype(F32) + relay[1, i].astype(F32)).astype(BF)
        near_down[i][1].start()

    def summed(i, a):
        near_up[i][a].wait_recv()
        near_down[i][a].wait_recv()
        return (
            terms[y * 2 + order[i], a].astype(F32)
            + arrive[0, i, a].astype(F32)
            + arrive[1, i, a].astype(F32)
        )

    attend(far)
    far_up[0].start()
    far_down[0].start()
    attend(up)
    send_caches(15)
    attend(down)
    far_up[0].wait_send()
    near_up[0][1].start()
    far_down[0].wait_send()
    near_down[0][0].start()
    relay_up(0)
    relay_down(0)
    send_caches(5, 13)
    w1, wf1 = dec_weights(q1, [new0, new1])
    dec_out(1, w1, wf1, [new0, new1])
    attend(y)
    near_up[0][0].wait_send()
    far_up[1].start()
    near_down[0][1].wait_send()
    far_down[1].start()
    for a in range(2):
        cross[0, a] = summed(0, a).astype(BF)
        over_in[a].start()

    mine_rows = pl.ds(pl.multiple_of(g * RP, RP), RP)
    fin[mine_rows, 0:SL] = reduce_parts(1, xbuf[t])
    for i, (k, v) in enumerate([new0, new1]):
        start = SL + 2 * i * HD
        fin[mine_rows, start : start + HD] = k
        fin[mine_rows, start + HD : start + 2 * HD] = v

    def fin_copy(k):
        where = fin.at[mine_rows]
        return remote(where, where, fin_send.at[k], fin_recv.at[k], {"group": (g + k) % NG})

    lax.fori_loop(1, NG, lambda k, c: (fin_copy(k).start(), c)[1], 0)

    far_up[1].wait_send()
    near_up[1][1].start()
    far_down[1].wait_send()
    near_down[1][0].start()
    for a in range(2):
        over_in[a].wait_recv()
        over[a].start()
    relay_up(1)
    relay_down(1)

    for a in range(2):
        near = summed(1, a)
        for i in range(2):
            cols = slice(a * HALF + i * QUART, a * HALF + (i + 1) * QUART)
            add = near[i * SH : (i + 1) * SH]
            score_sum[:, cols] = score_ref[:, cols].astype(F32) + add

    lax.fori_loop(1, NG, lambda k, c: (fin_copy(k).wait_recv(), c)[1], 0)
    placed = dot(pick[...], fin[...])
    obuf[t] = placed[:, :SL].astype(BF)
    patch_ref[...] = placed[:, SL:]

    def o_copy(k):
        return remote(obuf.at[t], obuf.at[t], o_send.at[k], o_recv.at[k], {"tp": (t + k) % NT})

    lax.fori_loop(1, NT, lambda k, c: (o_copy(k).start(), c)[1], 0)

    for a in range(2):
        over[a].wait_recv()
        far_half = cross[1, a].astype(F32)
        for i in range(2):
            cols = slice(a * HALF + i * QUART, a * HALF + (i + 1) * QUART)
            add = far_half[i * SH : (i + 1) * SH]
            score_out_ref[:, cols] = (score_sum[:, cols] + add).astype(BF)

    lax.fori_loop(1, NT, lambda k, c: (o_copy(k).wait_recv(), c)[1], 0)
    for p in range(NT):
        dec_out_ref[:, p * SL : (p + 1) * SL] = obuf[p]

    def end_a2a(j, c):
        a2a(j).wait()
        return c

    lax.fori_loop(1, 8, end_a2a, 0)
    lax.fori_loop(12, NG, end_a2a, 0)
    for m, kv in halves_z:
        z_out(m, kv).wait()
    own_copy.wait()
    ended = [first_up, first_down, second_up, second_down] + fwd_up + fwd_down
    ended += x_in + x_out + over_in + over + [z_in(m, kv) for m, kv in halves_z]
    ended += near_up[1] + near_down[1] + [near_up[0][1], near_down[0][0]]
    for c in ended:
        c.wait_send()

    def end_tp(k, c):
        part_copy(0, k).wait_send()
        part_copy(1, k).wait_send()
        x_copy(k).wait_send()
        o_copy(k).wait_send()
        return c

    lax.fori_loop(1, NT, end_tp, 0)
    lax.fori_loop(1, NG, lambda k, c: (fin_copy(k).wait_send(), c)[1], 0)


def place_kernel(
    plan_ref, patch_ref, dec_ref, got_hbm, score_hbm,
    dec_out_ref, cache_out, score_out, rows, score_rows, in_sem, out_sem, score_sem,
):
    score_in = pltpu.make_async_copy(score_hbm, score_rows, score_sem.at[0])
    score_end = pltpu.make_async_copy(score_rows, score_out, score_sem.at[1])
    score_in.start()

    def get(s, c):
        pltpu.make_async_copy(got_hbm.at[plan_ref[s, 0]], rows.at[s], in_sem.at[s]).start()
        return c

    lax.fori_loop(0, WAVE, get, 0)
    dec_out_ref[...] = dec_ref[:R, :]
    score_in.wait()
    score_end.start()

    def put(s, c):
        pltpu.make_async_copy(got_hbm.at[0], rows.at[s], in_sem.at[s]).wait()

        @pl.when(s + WAVE < R)
        def _():
            get(s + WAVE, 0)

        entry = patch_ref[pl.ds(s, 1), :]
        for step in range(2):
            pos = plan_ref[s, 1] + step
            base = pl.multiple_of((pos // 16) * 16, 16)
            here = lax.broadcasted_iota(jnp.int32, (16, HD), 0) == pos - base
            for kv in range(2):
                start = (2 * step + kv) * HD
                old = rows[s, kv, pl.ds(base, 16), :].astype(F32)
                both = jnp.where(here, entry[:, start : start + HD], old)
                rows[s, kv, pl.ds(base, 16), :] = both.astype(BF)
        pltpu.make_async_copy(rows.at[s], cache_out.at[s], out_sem.at[s]).start()
        return c

    lax.fori_loop(0, R, put, 0)

    def end(s, c):
        pltpu.make_async_copy(rows.at[s], cache_out.at[s], out_sem.at[s]).wait()
        return c

    lax.fori_loop(0, R, end, 0)
    score_end.wait()


def per_device(
    dec_rows, kv_cache, lengths, dest_group, dest_slot, score_rows, doc_ids,
    norm_gain, query_gain, key_gain, w_query, w_keyval, w_out,
):
    smem = pl.BlockSpec(memory_space=pltpu.SMEM)
    vmem = pl.BlockSpec(memory_space=pltpu.VMEM)
    hbm = pl.BlockSpec(memory_space=pl.ANY)
    dma = pltpu.SemaphoreType.DMA
    got, patch, plan, dec_out16, score_sum = pl.pallas_call(
        main_kernel,
        name="decode_and_score",
        out_shape=(
            jax.ShapeDtypeStruct((NG, 2, CTX, HD), BF),
            jax.ShapeDtypeStruct((RP, 4 * HD), F32),
            jax.ShapeDtypeStruct((RP, HD), jnp.int32),
            jax.ShapeDtypeStruct((RP, D), BF),
            jax.ShapeDtypeStruct((SH, D), BF),
        ),
        in_specs=[smem] * 3 + [vmem] * 4 + [hbm] * 6,
        out_specs=(hbm, vmem, vmem, vmem, vmem),
        scratch_shapes=[
            pltpu.VMEM((SH, D), BF),
            pltpu.VMEM((R, D), BF),
            pltpu.VMEM((R, 2, CTX, HD), BF),
            pltpu.VMEM((2 * D, HD), BF),
            pltpu.VMEM((D, 768), BF),
            pltpu.VMEM((512, D), BF),
            pltpu.VMEM((RP, D), F32),
            pltpu.VMEM((16, TOK), F32),
            pltpu.VMEM((TOK, HD), F32),
            pltpu.VMEM((NG, 2, CTX, HD), BF),
            pltpu.VMEM((NT, 2, 2 * SH, QUART), BF),
            pltpu.VMEM((TOK, D), BF),
            pltpu.VMEM((TOK, HD), F32),
            pltpu.VMEM((4, TOK, HD), BF),
            pltpu.VMEM((HD, TOK), BF),
            pltpu.VMEM((TOK, HD), BF),
            pltpu.VMEM((NT, 2, 2 * SH, QUART), BF),
            pltpu.VMEM((2, 2, 2 * SH, QUART), BF),
            pltpu.VMEM((2, 2, 2, 2 * SH, QUART), BF),
            pltpu.VMEM((2, 2, 2 * SH, QUART), BF),
            pltpu.VMEM((2, 2 * SH, QUART), BF),
            pltpu.VMEM((2, 4, CTX, HD), BF),
            pltpu.VMEM((2, 2 * SH, QUART), BF),
            pltpu.VMEM((SH, D), F32),
            pltpu.VMEM((2, NT, RP, SL), F32),
            pltpu.VMEM((2, NT, RP, SL), F32),
            pltpu.VMEM((NT, RP, SL), BF),
            pltpu.VMEM((RP, D), BF),
            pltpu.VMEM((4 * RP, CTX), F32),
            pltpu.VMEM((RP, NG * RP), BF),
            pltpu.VMEM((NG * RP, MSG), BF),
            pltpu.VMEM((NT, RP, SL), BF),
            dma((6,)), dma((NG,)), dma((NG,)), dma((2, 4)), dma((2, 4)), dma((2, 4)), dma((2, 4)), dma((2, 4)), dma((2, 4)), dma((28,)), dma((28,)), dma((42,)), dma((42,)),
            dma((2, NT)), dma((2, NT)), dma((NT,)), dma((NT,)), dma((NG,)), dma((NG,)),
            dma((NT,)), dma((NT,)),
        ],
        compiler_params=pltpu.CompilerParams(
            collective_id=0, has_side_effects=True, vmem_limit_bytes=60 * 1024 * 1024
        ),
        cost_estimate=pl.CostEstimate(flops=8 * 10**9, bytes_accessed=30 * 10**6, transcendentals=10**6),
    )(
        dest_group, dest_slot, lengths, norm_gain.reshape(1, D),
        query_gain.reshape(1, HD), key_gain.reshape(1, HD), doc_ids,
        kv_cache, w_query, w_keyval.reshape(2 * D, HD), w_out, score_rows, dec_rows,
    )
    return pl.pallas_call(
        place_kernel,
        name="place_rows",
        out_shape=(
            jax.ShapeDtypeStruct((R, D), BF),
            jax.ShapeDtypeStruct((R, 2, CTX, HD), BF),
            jax.ShapeDtypeStruct((SH, D), BF),
        ),
        in_specs=[smem] + [vmem] * 2 + [hbm] * 2,
        out_specs=(vmem, hbm, hbm),
        scratch_shapes=[
            pltpu.VMEM((R, 2, CTX, HD), BF),
            pltpu.VMEM((SH, D), BF),
            dma((R,)), dma((R,)), dma((2,)),
        ],
        compiler_params=pltpu.CompilerParams(vmem_limit_bytes=60 * 1024 * 1024),
        cost_estimate=pl.CostEstimate(flops=10**6, bytes_accessed=12 * 10**6, transcendentals=0),
    )(plan, patch, dec_out16, got, score_sum)


def solution(mesh):
    placed = (
        P("group", None),
        P("group", None, None, "tp"),
        P(),
        P(),
        P(),
        P(("group", "tp"), None),
        P("group", None),
        P(),
        P(),
        P(),
        P(None, "tp"),
        P(None, None, "tp"),
        P("tp", None),
    )
    return jax.shard_map(
        per_device,
        mesh=mesh,
        in_specs=placed,
        out_specs=(P("group", None), P("group", None, None, "tp"), P(("group", "tp"), None)),
        check_vma=False,
    )
```

```python
import functools
import math

import jax
import jax.numpy as jnp
from jax import lax
from jax.experimental import pallas as pl
from jax.experimental.pallas import tpu as pltpu
from jax.sharding import PartitionSpec as P

HD = 128
EPS = 1e-06
MESH = pl.DeviceIdType.MESH
BF = jnp.bfloat16
F32 = jnp.float32
LOW = -1e30
INV = 1.0 / math.sqrt(HD)

D = 5120
CTX = 768
NG = 16
NT = 8
R = 14
RP = 16
SH = 56
SP = 64
TOK = NT * SP
HALF = D // 2
QUART = D // 4
SL = D // NT
MSG = SL + 4 * HD
GATHER_CUTS = ((0, 112),)
SUM_CUTS = ((0, 112),)


def head_norm(vectors, gain):
    mean = jnp.mean(vectors * vectors, axis=-1, keepdims=True)
    return (vectors * lax.rsqrt(mean + EPS) * gain).astype(BF)


def dot(a, b):
    return jnp.dot(a, b, preferred_element_type=F32)


class Several:
    def __init__(self, copies):
        self.copies = copies

    def start(self):
        for copy in self.copies:
            copy.start()

    def wait_recv(self):
        for copy in self.copies:
            copy.wait_recv()

    def wait_send(self):
        for copy in self.copies:
            copy.wait_send()


def dot_t(a, b):
    return lax.dot_general(a, b, (((1,), (1,)), ((), ())), preferred_element_type=F32)


def main_kernel(
    dest_ref, slot_ref, len_ref,
    gain_ref, qgain_ref, kgain_ref, doc_ref,
    cache_hbm, wq_hbm, wkv_hbm, wo_hbm, score_hbm, dec_hbm,
    got_ref, patch_ref, plan_ref, dec_out_ref, score_out_ref,
    score_ref, dec_ref, cache, wkv, wqkv, wo, xin, docr_ref, docc_ref, packed, xg, xn, sc, qs, ks, kt, vs, terms,
    relay, arrive, cross, through_x, through_z, through_cross, score_sum, part, gather_part, xbuf, nx, scores, pick, fin, obuf,
    load_sem, a2a_send, a2a_recv, ex_send, ex_recv, zi_send, zi_recv, zo_send, zo_recv, ag_send, ag_recv, rs_send, rs_recv,
    dp_send, dp_recv, dx_send, dx_recv, fin_send, fin_recv, o_send, o_recv,
):
    g = lax.axis_index("group")
    t = lax.axis_index("tp")
    y, h = t // 2, t % 2
    z, xl, core = g // 4, (g // 2) % 2, g % 2
    oh = 1 - h
    up, down, far = (y + 1) % 4, (y + 3) % 4, (y + 2) % 4
    mine, partner = t, y * 2 + oh
    g_x = z * 4 + (1 - xl) * 2 + core
    to_up, to_down = {"tp": up * 2 + h}, {"tp": down * 2 + h}
    via_same, via_other = (g_x, t), (g_x, partner)

    def remote(src, dst, send, recv, device):
        return pltpu.make_async_remote_copy(
            src_ref=src, dst_ref=dst, send_sem=send, recv_sem=recv,
            device_id=device, device_id_type=MESH,
        )

    barrier = pltpu.get_barrier_semaphore()

    def greet_tp(k, c):
        pl.semaphore_signal(barrier, inc=1, device_id={"tp": (t + k) % NT}, device_id_type=MESH)
        return c

    def greet_group(k, c):
        pl.semaphore_signal(barrier, inc=1, device_id={"group": (g + k) % NG}, device_id_type=MESH)
        return c

    lax.fori_loop(1, NT, greet_tp, 0)
    lax.fori_loop(1, NG, greet_group, 0)
    pl.semaphore_signal(barrier, inc=1, device_id=(g_x, partner), device_id_type=MESH)

    loads = [
        pltpu.make_async_copy(cache_hbm, cache, load_sem.at[0]),
        pltpu.make_async_copy(wq_hbm, wqkv.at[:, pl.ds(0, 512)], load_sem.at[1]),
        pltpu.make_async_copy(wkv_hbm, wkv, load_sem.at[2]),
        pltpu.make_async_copy(wo_hbm, wo, load_sem.at[3]),
        pltpu.make_async_copy(score_hbm, score_ref, load_sem.at[4]),
        pltpu.make_async_copy(dec_hbm, dec_ref, load_sem.at[5]),
    ]
    for i in (4, 0, 5, 2, 1, 3):
        loads[i].start()

    loads[4].wait()
    for a in range(2):
        lo = score_ref[:, a * HALF : a * HALF + QUART].astype(F32)
        hi = score_ref[:, a * HALF + QUART : (a + 1) * HALF].astype(F32)
        xg[mine, a] = jnp.concatenate([lo, hi], axis=0).astype(BF)

    pl.semaphore_wait(barrier, NT + NG - 1)

    def pieces(cuts, src, dst, send, recv, base, device):
        return [
            remote(
                src.at[pl.ds(lo, n), :], dst.at[pl.ds(lo, n), :],
                send.at[base + i], recv.at[base + i], device,
            )
            for i, (lo, n) in enumerate(cuts)
        ]

    def ag(base, shard, halves, device):
        copies = []
        for i, a in enumerate(halves):
            where = xg.at[shard, a]
            copies += pieces(GATHER_CUTS, where, where, ag_send, ag_recv, base + 2 * i, device)
        return Several(copies)

    def exchange(src, through, dst, send, recv):
        ins = [
            remote(src.at[a], through.at[a], send.at[a], recv.at[a], device)
            for a, device in enumerate((via_same, via_other))
        ]
        outs = [
            remote(through.at[a], dst(a), send.at[2 + a], recv.at[2 + a], device)
            for a, device in enumerate((via_other, via_same))
        ]
        return ins, outs

    x_in, x_out = exchange(
        xg.at[mine], through_x, lambda a: xg.at[(mine, partner)[a], a], ex_send.at[0], ex_recv.at[0]
    )
    first_up, first_down = ag(4, mine, (0, 1), to_up), ag(8, mine, (0, 1), to_down)
    for c in (*x_in, first_up, first_down):
        c.start()
    second_up, second_down = ag(12, partner, (0, 1), to_up), ag(16, partner, (0, 1), to_down)
    fwd_up = [ag(20 + 2 * i, down * 2 + hh, (0,), to_up) for i, hh in enumerate((h, oh))]
    fwd_down = [ag(24 + 2 * i, up * 2 + hh, (1,), to_down) for i, hh in enumerate((h, oh))]

    def target_of(j):
        dz, dx, dc = j // 4, (j // 2) % 2, j % 2
        return ((z + dz) % 4) * 4 + ((xl + dx) % 2) * 2 + (core + dc) % 2

    def a2a(j):
        device = {"group": target_of(j)}
        return remote(packed.at[j], got_ref.at[g], a2a_send.at[j], a2a_recv.at[j], device)

    def fill(j, target):
        row = 0
        for r in range(1, R):
            row = jnp.where(dest_ref[g * R + r] == target, r, row)
        for kv in range(2):
            packed[j, kv] = cache[row, kv]

    def send_caches(*rows):
        for j in rows:
            fill(j, target_of(j))
            a2a(j).start()

    z_next, z_last = ((z + 1) % 4) * 4 + xl * 2 + core, ((z + 3) % 4) * 4 + xl * 2 + core

    def z_in(m, kv):
        return remote(
            packed.at[8 + m, kv], through_z.at[kv, m], zi_send.at[kv, m], zi_recv.at[kv, m],
            {"group": (z_next, z_last)[kv]},
        )

    def z_out(m, kv):
        onward, source = ((z_next // 4, z_last), (z_last // 4, z_next))[kv]
        target = onward * 4 + ((xl + m // 2) % 2) * 2 + (core + m % 2) % 2
        return remote(
            through_z.at[kv, m], got_ref.at[source, kv], zo_send.at[kv, m], zo_recv.at[kv, m],
            {"group": target},
        )

    halves_z = [(m, kv) for m in range(4) for kv in range(2)]

    loads[0].wait()
    for m in range(4):
        fill(8 + m, target_of(8 + m))
        z_in(m, 0).start()
        z_in(m, 1).start()
    send_caches(1)
    fill(0, g)
    own_copy = pltpu.make_async_copy(packed.at[0], got_ref.at[g], a2a_send.at[0])
    own_copy.start()

    loads[5].wait()
    xin[...] = jnp.zeros_like(xin)
    xin[0:R, :] = dec_ref[...].astype(F32)
    token = lax.broadcasted_iota(jnp.int32, (TOK, NT * SH), 1)
    place = lax.broadcasted_iota(jnp.int32, (TOK, NT * SH), 0)
    inside = (place & (SP - 1)) < SH
    spread = ((place - (place >> 6) * (SP - SH) == token) & inside).astype(F32).astype(BF)
    ids = jnp.broadcast_to(doc_ref[...].astype(F32) + 1.0, (HD, NT * SH)).astype(BF)
    docr_ref[...] = dot_t(ids[:16], spread)
    docc_ref[...] = dot_t(spread, ids)

    lane = lax.broadcasted_iota(jnp.int32, (RP, NG * RP), 1)
    slot_row = lax.broadcasted_iota(jnp.int32, (RP, NG * RP), 0)

    def wanted(e, c):
        want, span = c
        for r in range(R):
            here = jnp.where(dest_ref[e * R + r] == g, slot_ref[e * R + r], -1)
            spot = lane == e * RP + r
            want = jnp.where(spot, here, want)
            span = jnp.where(spot, len_ref[e * R + r], span)
        return want, span

    none = jnp.full((RP, NG * RP), -1, jnp.int32)
    want, span = lax.fori_loop(0, NG, wanted, (none, jnp.zeros_like(none)))
    pick[...] = (want == slot_row).astype(F32).astype(BF)
    source = jnp.sum(jnp.where(want == slot_row, lane >> 4, 0), axis=-1, keepdims=True)
    length = jnp.sum(jnp.where(want == slot_row, span, 0), axis=-1, keepdims=True)
    plan_lane = lax.broadcasted_iota(jnp.int32, (RP, HD), 1)
    plan_ref[...] = jnp.where(plan_lane == 0, source, length)

    row_of = lax.broadcasted_iota(jnp.int32, (4 * RP, HD), 0) & (RP - 1)
    column_row = lax.broadcasted_iota(jnp.int32, (HD, 4 * RP), 1) & (RP - 1)
    lens = jnp.ones((4 * RP, HD), jnp.int32)
    for r in range(R):
        lens = jnp.where(row_of == r, len_ref[g * R + r], lens)
    cached = lax.broadcasted_iota(jnp.int32, (4 * RP, CTX), 1) < lens[:, 0:1]

    def stack4(v):
        return jnp.concatenate([v] * 4, axis=0)

    def dec_norm(x):
        wide = x.astype(F32)
        nx[...] = (wide * gain_ref[...]).astype(BF)
        return lax.rsqrt(jnp.mean(wide * wide, axis=-1, keepdims=True) + EPS)

    def dec_heads(proj):
        q = jnp.concatenate([proj[:, i * HD : (i + 1) * HD] for i in range(4)], axis=0)
        q = head_norm(q, qgain_ref[...])
        return q, (head_norm(proj[:, 512:640], kgain_ref[...]), proj[:, 640:768].astype(BF))

    def dec_weights(q, new):
        qf = q.astype(F32)
        qt = qf.T.astype(BF)

        def chunk(n, c):
            spots = pl.ds(pl.multiple_of(n * HD, HD), HD)
            acc = jnp.zeros((HD, 4 * RP), F32)
            for r in range(R):
                acc = jnp.where(column_row == r, dot(cache[r, 0, spots, :], qt), acc)
            scores[:, spots] = acc.T
            return c

        lax.fori_loop(0, CTX // HD, chunk, 0)
        s = jnp.where(cached, scores[...] * INV, LOW)
        fresh = [
            jnp.sum(qf * stack4(k.astype(F32)), axis=-1, keepdims=True) * INV for k, _ in new
        ]
        top = functools.reduce(jnp.maximum, fresh, jnp.max(s, axis=-1, keepdims=True))
        e = jnp.exp(s - top)
        ef = [jnp.exp(f - top) for f in fresh]
        total = functools.reduce(jnp.add, ef, jnp.sum(e, axis=-1, keepdims=True))
        inv = 1.0 / total
        return (e * inv).astype(BF), [(f * inv).astype(BF).astype(F32) for f in ef]

    def dec_attn(w, wf, new):
        def value_row(r, acc):
            return acc + jnp.where(row_of == r, dot(w, cache[r, 1]), 0.0)

        o = lax.fori_loop(0, R, value_row, jnp.zeros((4 * RP, HD), F32), unroll=True)
        for f, (_, v) in zip(wf, new):
            o = o + f * stack4(v.astype(F32))
        o = o.astype(BF)
        return jnp.concatenate([o[i * RP : (i + 1) * RP] for i in range(4)], axis=1)

    def dec_out(step, o):
        for p in range(NT):
            part[step, p] = dot(o, wo[:, p * SL : (p + 1) * SL])
        send_parts(step)

    def send_parts(step):
        lax.fori_loop(1, NT, lambda k, c: (part_copy(step, k).start(), c)[1], 0)

    def part_copy(step, k):
        peer = (t + k) % NT
        return remote(
            part.at[step, peer], gather_part.at[step, t],
            dp_send.at[step, k], dp_recv.at[step, k], {"tp": peer},
        )

    def reduce_parts(step, base):
        lax.fori_loop(1, NT, lambda k, c: (part_copy(step, k).wait_recv(), c)[1], 0)
        total = lax.fori_loop(
            1, NT, lambda k, acc: acc + gather_part[step, (t + k) % NT], part[step, t]
        )
        return (base.astype(F32) + total).astype(BF)

    def x_copy(k):
        return remote(xbuf.at[t], xbuf.at[t], dx_send.at[k], dx_recv.at[k], {"tp": (t + k) % NT})

    loads[2].wait()
    to_row = lax.broadcasted_iota(jnp.int32, (256, 256), 0)
    from_row = lax.broadcasted_iota(jnp.int32, (256, 256), 1)
    parting = (from_row == 2 * (to_row & (HD - 1)) + (to_row >= HD).astype(jnp.int32)).astype(F32).astype(BF)

    def part_rows(b, c):
        both = dot(parting, wkv[pl.ds(pl.multiple_of(b * 256, 256), 256), :]).astype(BF)
        rows = pl.ds(pl.multiple_of(b * HD, HD), HD)
        wqkv[rows, 512:640] = both[:HD]
        wqkv[rows, 640:768] = both[HD:]
        return c

    lax.fori_loop(0, D // HD, part_rows, 0, unroll=8)

    def prepare(p, c):
        total = jnp.zeros((SH, 1), F32)
        rows = pl.ds(pl.multiple_of(p * SP, SP), SP)
        for a in range(2):
            both = xg[p, a].astype(F32)
            for i in range(2):
                x = both[i * SH : (i + 1) * SH]
                total = total + jnp.sum(x * x, axis=-1, keepdims=True)
                start = a * HALF + i * QUART
                n = x * gain_ref[:, start : start + QUART]
                n = jnp.concatenate([n, jnp.zeros((SP - SH, QUART), F32)], axis=0)
                xn[rows, start : start + QUART] = n.astype(BF)
        scale = lax.rsqrt(total / D + EPS)
        scale = jnp.concatenate([scale, jnp.zeros((SP - SH, 1), F32)], axis=0)
        sc[rows, :] = jnp.broadcast_to(scale, (SP, HD))
        return c

    def project(shards, dec_scale=None):
        spots = [pl.ds(pl.multiple_of(p * SP, SP), SP) for p in shards]
        lhs = [xn[rows, :] for rows in spots]
        scale = [sc[rows, 0:1] for rows in spots]
        if dec_scale is not None:
            lhs.append(nx[...])
            scale.append(dec_scale)
        lhs = jnp.concatenate(lhs, axis=0)
        scale = jnp.concatenate(scale, axis=0)
        extra = []
        for j in range(3):
            v = dot(lhs, wqkv[:, j * 256 : (j + 1) * 256]) * scale
            extra.append(v[len(shards) * SP :])
            for n, rows in enumerate(spots):
                mine_v = v[n * SP : (n + 1) * SP]
                if j < 2:
                    for i in range(2):
                        head = mine_v[:, i * HD : (i + 1) * HD]
                        qs[2 * j + i, rows, :] = head_norm(head, qgain_ref[...])
                else:
                    ks[rows, :] = head_norm(mine_v[:, :HD], kgain_ref[...]).astype(F32)
                    vs[rows, :] = mine_v[:, HD:].astype(BF)
        if dec_scale is not None:
            return dec_heads(jnp.concatenate(extra, axis=1))

    prepare(mine, 0)
    scale0 = dec_norm(xin[...])
    for a in range(2):
        x_in[a].wait_recv()
        x_out[a].start()
    loads[1].wait()
    q0, new0 = project((mine,), scale0)
    for a in range(2):
        x_out[a].wait_recv()
    second_up.start()
    second_down.start()
    first_up.wait_recv()
    fwd_up[0].start()
    first_down.wait_recv()
    fwd_down[0].start()
    send_caches(2)
    for m, kv in halves_z[:4]:
        z_in(m, kv).wait_recv()
        z_out(m, kv).start()
    w0, wf0 = dec_weights(q0, [new0])
    loads[3].wait()
    dec_out(0, dec_attn(w0, wf0, [new0]))
    for m, kv in halves_z[4:]:
        z_in(m, kv).wait_recv()
        z_out(m, kv).start()
    prepare(partner, 0)
    prepare(down * 2 + h, 0)
    prepare(up * 2 + h, 0)
    project((partner, down * 2 + h, up * 2 + h))

    base0 = xin[:, pl.ds(pl.multiple_of(t * SL, SL), SL)]
    xbuf[t] = reduce_parts(0, base0)
    lax.fori_loop(1, NT, lambda k, c: (x_copy(k).start(), c)[1], 0)

    second_up.wait_recv()
    fwd_up[1].start()
    second_down.wait_recv()
    fwd_down[1].start()
    send_caches(3, 6)
    prepare(down * 2 + oh, 0)
    prepare(up * 2 + oh, 0)
    lax.fori_loop(1, NT, lambda k, c: (x_copy(k).wait_recv(), c)[1], 0)
    scale1 = dec_norm(jnp.concatenate([xbuf[p] for p in range(NT)], axis=1))
    q1, new1 = project((down * 2 + oh, up * 2 + oh), scale1)
    send_caches(14, 4)
    fwd_up[0].wait_recv()
    fwd_down[0].wait_recv()
    prepare(far * 2 + h, 0)
    fwd_up[1].wait_recv()
    fwd_down[1].wait_recv()
    prepare(far * 2 + oh, 0)
    project((far * 2 + h, far * 2 + oh))
    kt[...] = ks[...].T.astype(BF)
    send_caches(7, 12)

    later_col = lax.broadcasted_iota(jnp.int32, (2 * SP, TOK), 1)
    later_row = lax.broadcasted_iota(jnp.int32, (2 * SP, TOK), 0)

    def heads_of(block):
        rows = pl.ds(pl.multiple_of(block * 2 * SP, 2 * SP), 2 * SP)
        live = (docc_ref[rows, 0:1] == docr_ref[0:1, :]) & (later_col <= later_row + block * (2 * SP))
        heads = []
        for i in range(4):
            s = jnp.where(live, dot(qs[i, rows, :], kt[...]) * INV, LOW)
            e = jnp.exp(s - jnp.max(s, axis=-1, keepdims=True))
            inv = 1.0 / jnp.sum(e, axis=-1, keepdims=True)
            heads.append(dot((e * inv).astype(BF), vs[...]).astype(BF))
        return jnp.concatenate(heads, axis=1)

    def attend(blocks, dec=None):
        attn = [heads_of(block) for block in blocks]
        if dec is not None:
            attn.append(dec)
        attn = jnp.concatenate(attn, axis=0)
        for a in range(2):
            lo, hi = [
                dot(attn, wo[:, a * HALF + i * QUART : a * HALF + (i + 1) * QUART]) for i in range(2)
            ]
            for n, block in enumerate(blocks):
                for i in range(2):
                    start = (2 * n + i) * SP
                    pair = [v[start : start + SH] for v in (lo, hi)]
                    terms[block * 2 + i, a] = jnp.concatenate(pair, axis=0).astype(BF)
            if dec is not None:
                start = len(blocks) * 2 * SP
                for i, v in enumerate((lo, hi)):
                    for k in range(2):
                        part[1, 4 * a + 2 * i + k] = v[start:, k * SL : (k + 1) * SL]

    order = (oh, h)

    def rs(n, src, dst, device):
        return Several(pieces(SUM_CUTS, src, dst, rs_send, rs_recv, 3 * n, device))

    far_up = [rs(i, terms.at[far * 2 + order[i], 0], relay.at[0, i], to_up) for i in range(2)]
    far_down = [rs(2 + i, terms.at[far * 2 + order[i], 1], relay.at[1, i], to_down) for i in range(2)]
    near_up = [
        [rs(4 + 2 * i + a, terms.at[up * 2 + order[i], a], arrive.at[0, i, a], to_up) for a in range(2)]
        for i in range(2)
    ]
    near_down = [
        [rs(8 + 2 * i + a, terms.at[down * 2 + order[i], a], arrive.at[1, i, a], to_down) for a in range(2)]
        for i in range(2)
    ]
    over_in, over = exchange(
        cross.at[0], through_cross, lambda a: cross.at[1, a], ex_send.at[1], ex_recv.at[1]
    )

    def relay_up(i):
        far_up[i].wait_recv()
        spot = up * 2 + order[i]
        terms[spot, 0] = (terms[spot, 0].astype(F32) + relay[0, i].astype(F32)).astype(BF)
        near_up[i][0].start()

    def relay_down(i):
        far_down[i].wait_recv()
        spot = down * 2 + order[i]
        terms[spot, 1] = (terms[spot, 1].astype(F32) + relay[1, i].astype(F32)).astype(BF)
        near_down[i][1].start()

    def summed(i, a):
        near_up[i][a].wait_recv()
        near_down[i][a].wait_recv()
        return (
            terms[y * 2 + order[i], a].astype(F32)
            + arrive[0, i, a].astype(F32)
            + arrive[1, i, a].astype(F32)
        )

    attend((far,))
    far_up[0].start()
    far_down[0].start()
    attend((up, down))
    send_caches(15)
    far_up[0].wait_send()
    near_up[0][1].start()
    far_down[0].wait_send()
    near_down[0][0].start()
    relay_up(0)
    relay_down(0)
    send_caches(5, 13)
    w1, wf1 = dec_weights(q1, [new0, new1])
    attend((y,), dec_attn(w1, wf1, [new0, new1]))
    send_parts(1)
    near_up[0][0].wait_send()
    far_up[1].start()
    near_down[0][1].wait_send()
    far_down[1].start()
    for a in range(2):
        cross[0, a] = summed(0, a).astype(BF)
        over_in[a].start()

    mine_rows = pl.ds(pl.multiple_of(g * RP, RP), RP)
    fin[mine_rows, 0:SL] = reduce_parts(1, xbuf[t])
    for i, (k, v) in enumerate([new0, new1]):
        start = SL + 2 * i * HD
        fin[mine_rows, start : start + HD] = k
        fin[mine_rows, start + HD : start + 2 * HD] = v

    def fin_copy(k):
        where = fin.at[mine_rows]
        return remote(where, where, fin_send.at[k], fin_recv.at[k], {"group": (g + k) % NG})

    lax.fori_loop(1, NG, lambda k, c: (fin_copy(k).start(), c)[1], 0)

    far_up[1].wait_send()
    near_up[1][1].start()
    far_down[1].wait_send()
    near_down[1][0].start()
    for a in range(2):
        over_in[a].wait_recv()
        over[a].start()
    relay_up(1)
    relay_down(1)

    for a in range(2):
        near = summed(1, a)
        for i in range(2):
            cols = slice(a * HALF + i * QUART, a * HALF + (i + 1) * QUART)
            add = near[i * SH : (i + 1) * SH]
            score_sum[:, cols] = score_ref[:, cols].astype(F32) + add

    lax.fori_loop(1, NG, lambda k, c: (fin_copy(k).wait_recv(), c)[1], 0)
    placed = dot(pick[...], fin[...])
    obuf[t] = placed[:, :SL].astype(BF)
    patch_ref[...] = placed[:, SL:]

    def o_copy(k):
        return remote(obuf.at[t], obuf.at[t], o_send.at[k], o_recv.at[k], {"tp": (t + k) % NT})

    lax.fori_loop(1, NT, lambda k, c: (o_copy(k).start(), c)[1], 0)

    for a in range(2):
        over[a].wait_recv()
        far_half = cross[1, a].astype(F32)
        for i in range(2):
            cols = slice(a * HALF + i * QUART, a * HALF + (i + 1) * QUART)
            add = far_half[i * SH : (i + 1) * SH]
            score_out_ref[:, cols] = (score_sum[:, cols] + add).astype(BF)

    lax.fori_loop(1, NT, lambda k, c: (o_copy(k).wait_recv(), c)[1], 0)
    for p in range(NT):
        dec_out_ref[:, p * SL : (p + 1) * SL] = obuf[p]

    def end_a2a(j, c):
        a2a(j).wait()
        return c

    lax.fori_loop(1, 8, end_a2a, 0)
    lax.fori_loop(12, NG, end_a2a, 0)
    for m, kv in halves_z:
        z_out(m, kv).wait()
    own_copy.wait()
    ended = [first_up, first_down, second_up, second_down] + fwd_up + fwd_down
    ended += x_in + x_out + over_in + over + [z_in(m, kv) for m, kv in halves_z]
    ended += near_up[1] + near_down[1] + [near_up[0][1], near_down[0][0]]
    for c in ended:
        c.wait_send()

    def end_tp(k, c):
        part_copy(0, k).wait_send()
        part_copy(1, k).wait_send()
        x_copy(k).wait_send()
        o_copy(k).wait_send()
        return c

    lax.fori_loop(1, NT, end_tp, 0)
    lax.fori_loop(1, NG, lambda k, c: (fin_copy(k).wait_send(), c)[1], 0)


def place_kernel(
    plan_ref, patch_ref, dec_ref, got_hbm, score_hbm,
    dec_out_ref, cache_out, score_out, rows, score_rows, in_sem, out_sem, score_sem,
):
    score_in = pltpu.make_async_copy(score_hbm, score_rows, score_sem.at[0])
    score_end = pltpu.make_async_copy(score_rows, score_out, score_sem.at[1])
    score_in.start()

    def get(s, c):
        pltpu.make_async_copy(got_hbm.at[plan_ref[s, 0]], rows.at[s], in_sem.at[s]).start()
        return c

    lax.fori_loop(0, R, get, 0)
    dec_out_ref[...] = dec_ref[:R, :]
    score_in.wait()
    score_end.start()

    def put(s, c):
        pltpu.make_async_copy(got_hbm.at[0], rows.at[s], in_sem.at[s]).wait()
        entry = patch_ref[pl.ds(s, 1), :]
        for step in range(2):
            pos = plan_ref[s, 1] + step
            base = pl.multiple_of((pos // 16) * 16, 16)
            here = lax.broadcasted_iota(jnp.int32, (16, HD), 0) == pos - base
            for kv in range(2):
                start = (2 * step + kv) * HD
                old = rows[s, kv, pl.ds(base, 16), :].astype(F32)
                both = jnp.where(here, entry[:, start : start + HD], old)
                rows[s, kv, pl.ds(base, 16), :] = both.astype(BF)
        pltpu.make_async_copy(rows.at[s], cache_out.at[s], out_sem.at[s]).start()
        return c

    lax.fori_loop(0, R, put, 0)

    def end(s, c):
        pltpu.make_async_copy(rows.at[s], cache_out.at[s], out_sem.at[s]).wait()
        return c

    lax.fori_loop(0, R, end, 0)
    score_end.wait()


def per_device(
    dec_rows, kv_cache, lengths, dest_group, dest_slot, score_rows, doc_ids,
    norm_gain, query_gain, key_gain, w_query, w_keyval, w_out,
):
    smem = pl.BlockSpec(memory_space=pltpu.SMEM)
    vmem = pl.BlockSpec(memory_space=pltpu.VMEM)
    hbm = pl.BlockSpec(memory_space=pl.ANY)
    dma = pltpu.SemaphoreType.DMA
    got, patch, plan, dec_out16, score_sum = pl.pallas_call(
        main_kernel,
        name="decode_and_score",
        out_shape=(
            jax.ShapeDtypeStruct((NG, 2, CTX, HD), BF),
            jax.ShapeDtypeStruct((RP, 4 * HD), F32),
            jax.ShapeDtypeStruct((RP, HD), jnp.int32),
            jax.ShapeDtypeStruct((RP, D), BF),
            jax.ShapeDtypeStruct((SH, D), BF),
        ),
        in_specs=[smem] * 3 + [vmem] * 4 + [hbm] * 6,
        out_specs=(hbm, vmem, vmem, vmem, vmem),
        scratch_shapes=[
            pltpu.VMEM((SH, D), BF),
            pltpu.VMEM((R, D), BF),
            pltpu.VMEM((R, 2, CTX, HD), BF),
            pltpu.VMEM((2 * D, HD), BF),
            pltpu.VMEM((D, 768), BF),
            pltpu.VMEM((512, D), BF),
            pltpu.VMEM((RP, D), F32),
            pltpu.VMEM((16, TOK), F32),
            pltpu.VMEM((TOK, HD), F32),
            pltpu.VMEM((NG, 2, CTX, HD), BF),
            pltpu.VMEM((NT, 2, 2 * SH, QUART), BF),
            pltpu.VMEM((TOK, D), BF),
            pltpu.VMEM((TOK, HD), F32),
            pltpu.VMEM((4, TOK, HD), BF),
            pltpu.VMEM((TOK, HD), F32),
            pltpu.VMEM((HD, TOK), BF),
            pltpu.VMEM((TOK, HD), BF),
            pltpu.VMEM((NT, 2, 2 * SH, QUART), BF),
            pltpu.VMEM((2, 2, 2 * SH, QUART), BF),
            pltpu.VMEM((2, 2, 2, 2 * SH, QUART), BF),
            pltpu.VMEM((2, 2, 2 * SH, QUART), BF),
            pltpu.VMEM((2, 2 * SH, QUART), BF),
            pltpu.VMEM((2, 4, CTX, HD), BF),
            pltpu.VMEM((2, 2 * SH, QUART), BF),
            pltpu.VMEM((SH, D), F32),
            pltpu.VMEM((2, NT, RP, SL), F32),
            pltpu.VMEM((2, NT, RP, SL), F32),
            pltpu.VMEM((NT, RP, SL), BF),
            pltpu.VMEM((RP, D), BF),
            pltpu.VMEM((4 * RP, CTX), F32),
            pltpu.VMEM((RP, NG * RP), BF),
            pltpu.VMEM((NG * RP, MSG), BF),
            pltpu.VMEM((NT, RP, SL), BF),
            dma((6,)), dma((NG,)), dma((NG,)), dma((2, 4)), dma((2, 4)), dma((2, 4)), dma((2, 4)), dma((2, 4)), dma((2, 4)), dma((28,)), dma((28,)), dma((42,)), dma((42,)),
            dma((2, NT)), dma((2, NT)), dma((NT,)), dma((NT,)), dma((NG,)), dma((NG,)),
            dma((NT,)), dma((NT,)),
        ],
        compiler_params=pltpu.CompilerParams(
            collective_id=0, has_side_effects=True, vmem_limit_bytes=60 * 1024 * 1024
        ),
        cost_estimate=pl.CostEstimate(flops=8 * 10**9, bytes_accessed=30 * 10**6, transcendentals=10**6),
    )(
        dest_group, dest_slot, lengths, norm_gain.reshape(1, D),
        query_gain.reshape(1, HD), key_gain.reshape(1, HD), doc_ids,
        kv_cache, w_query, w_keyval.reshape(2 * D, HD), w_out, score_rows, dec_rows,
    )
    return pl.pallas_call(
        place_kernel,
        name="place_rows",
        out_shape=(
            jax.ShapeDtypeStruct((R, D), BF),
            jax.ShapeDtypeStruct((R, 2, CTX, HD), BF),
            jax.ShapeDtypeStruct((SH, D), BF),
        ),
        in_specs=[smem] + [vmem] * 2 + [hbm] * 2,
        out_specs=(vmem, hbm, hbm),
        scratch_shapes=[
            pltpu.VMEM((R, 2, CTX, HD), BF),
            pltpu.VMEM((SH, D), BF),
            dma((R,)), dma((R,)), dma((2,)),
        ],
        compiler_params=pltpu.CompilerParams(vmem_limit_bytes=60 * 1024 * 1024),
        cost_estimate=pl.CostEstimate(flops=10**6, bytes_accessed=12 * 10**6, transcendentals=0),
    )(plan, patch, dec_out16, got, score_sum)


def solution(mesh):
    placed = (
        P("group", None),
        P("group", None, None, "tp"),
        P(),
        P(),
        P(),
        P(("group", "tp"), None),
        P("group", None),
        P(),
        P(),
        P(),
        P(None, "tp"),
        P(None, None, "tp"),
        P("tp", None),
    )
    return jax.shard_map(
        per_device,
        mesh=mesh,
        in_specs=placed,
        out_specs=(P("group", None), P("group", None, None, "tp"), P(("group", "tp"), None)),
        check_vma=False,
    )
```

```python
import functools
import math

import jax
import jax.numpy as jnp
from jax import lax
from jax.experimental import pallas as pl
from jax.experimental.pallas import tpu as pltpu
from jax.sharding import PartitionSpec as P

HD = 128
EPS = 1e-06
MESH = pl.DeviceIdType.MESH
BF = jnp.bfloat16
F32 = jnp.float32
LOW = -1e30
INV = 1.0 / math.sqrt(HD)

D = 5120
CTX = 768
NG = 16
NT = 8
R = 14
RP = 16
SH = 56
SP = 64
TOK = NT * SP
HALF = D // 2
QUART = D // 4
SL = D // NT
MSG = SL + 4 * HD
GATHER_CUTS = ((0, 112),)
SUM_CUTS = ((0, 112),)


def head_norm(vectors, gain):
    mean = jnp.mean(vectors * vectors, axis=-1, keepdims=True)
    return (vectors * lax.rsqrt(mean + EPS) * gain).astype(BF)


def dot(a, b):
    return jnp.dot(a, b, preferred_element_type=F32)


class Several:
    def __init__(self, copies):
        self.copies = copies

    def start(self):
        for copy in self.copies:
            copy.start()

    def wait_recv(self):
        for copy in self.copies:
            copy.wait_recv()

    def wait_send(self):
        for copy in self.copies:
            copy.wait_send()


def dot_t(a, b):
    return lax.dot_general(a, b, (((1,), (1,)), ((), ())), preferred_element_type=F32)


def main_kernel(
    dest_ref, slot_ref, len_ref,
    gain_ref, qgain_ref, kgain_ref, doc_ref,
    cache_hbm, wq_hbm, wkv_hbm, wo_hbm, score_hbm, dec_hbm,
    got_ref, patch_ref, plan_ref, dec_out_ref, score_out_ref,
    score_ref, dec_ref, cache, wkv, wqkv, wo, xin, docr_ref, docc_ref, packed, xg, xn, sc, qs, ks, kt, vs, terms,
    relay, arrive, cross, through_x, through_z, through_cross, score_sum, part, gather_part, xbuf, nx, scores, pick, drop, fin, arrived, obuf,
    load_sem, a2a_send, a2a_recv, ex_send, ex_recv, zi_send, zi_recv, zo_send, zo_recv, ag_send, ag_recv, rs_send, rs_recv,
    dp_send, dp_recv, dx_send, dx_recv, fin_send, fin_recv, o_send, o_recv,
):
    g = lax.axis_index("group")
    t = lax.axis_index("tp")
    y, h = t // 2, t % 2
    z, xl, core = g // 4, (g // 2) % 2, g % 2
    oh = 1 - h
    up, down, far = (y + 1) % 4, (y + 3) % 4, (y + 2) % 4
    mine, partner = t, y * 2 + oh
    g_x = z * 4 + (1 - xl) * 2 + core
    to_up, to_down = {"tp": up * 2 + h}, {"tp": down * 2 + h}
    via_same, via_other = (g_x, t), (g_x, partner)

    def remote(src, dst, send, recv, device):
        return pltpu.make_async_remote_copy(
            src_ref=src, dst_ref=dst, send_sem=send, recv_sem=recv,
            device_id=device, device_id_type=MESH,
        )

    barrier = pltpu.get_barrier_semaphore()

    def greet_tp(k, c):
        pl.semaphore_signal(barrier, inc=1, device_id={"tp": (t + k) % NT}, device_id_type=MESH)
        return c

    def greet_group(k, c):
        pl.semaphore_signal(barrier, inc=1, device_id={"group": (g + k) % NG}, device_id_type=MESH)
        return c

    lax.fori_loop(1, NT, greet_tp, 0)
    lax.fori_loop(1, NG, greet_group, 0)
    pl.semaphore_signal(barrier, inc=1, device_id=(g_x, partner), device_id_type=MESH)

    loads = [
        pltpu.make_async_copy(cache_hbm, cache, load_sem.at[0]),
        pltpu.make_async_copy(wq_hbm, wqkv.at[:, pl.ds(0, 512)], load_sem.at[1]),
        pltpu.make_async_copy(wkv_hbm, wkv, load_sem.at[2]),
        pltpu.make_async_copy(wo_hbm, wo, load_sem.at[3]),
        pltpu.make_async_copy(score_hbm, score_ref, load_sem.at[4]),
        pltpu.make_async_copy(dec_hbm, dec_ref, load_sem.at[5]),
    ]
    for i in (4, 0, 5, 2, 1, 3):
        loads[i].start()

    loads[4].wait()
    for a in range(2):
        lo = score_ref[:, a * HALF : a * HALF + QUART].astype(F32)
        hi = score_ref[:, a * HALF + QUART : (a + 1) * HALF].astype(F32)
        xg[mine, a] = jnp.concatenate([lo, hi], axis=0).astype(BF)

    pl.semaphore_wait(barrier, NT + NG - 1)

    def pieces(cuts, src, dst, send, recv, base, device):
        return [
            remote(
                src.at[pl.ds(lo, n), :], dst.at[pl.ds(lo, n), :],
                send.at[base + i], recv.at[base + i], device,
            )
            for i, (lo, n) in enumerate(cuts)
        ]

    def ag(base, shard, halves, device):
        copies = []
        for i, a in enumerate(halves):
            where = xg.at[shard, a]
            copies += pieces(GATHER_CUTS, where, where, ag_send, ag_recv, base + 2 * i, device)
        return Several(copies)

    def exchange(src, through, dst, send, recv):
        ins = [
            remote(src.at[a], through.at[a], send.at[a], recv.at[a], device)
            for a, device in enumerate((via_same, via_other))
        ]
        outs = [
            remote(through.at[a], dst(a), send.at[2 + a], recv.at[2 + a], device)
            for a, device in enumerate((via_other, via_same))
        ]
        return ins, outs

    x_in, x_out = exchange(
        xg.at[mine], through_x, lambda a: xg.at[(mine, partner)[a], a], ex_send.at[0], ex_recv.at[0]
    )
    first_up, first_down = ag(4, mine, (0, 1), to_up), ag(8, mine, (0, 1), to_down)
    for c in (*x_in, first_up, first_down):
        c.start()
    second_up, second_down = ag(12, partner, (0, 1), to_up), ag(16, partner, (0, 1), to_down)
    fwd_up = [ag(20 + 2 * i, down * 2 + hh, (0,), to_up) for i, hh in enumerate((h, oh))]
    fwd_down = [ag(24 + 2 * i, up * 2 + hh, (1,), to_down) for i, hh in enumerate((h, oh))]

    def target_of(j):
        dz, dx, dc = j // 4, (j // 2) % 2, j % 2
        return ((z + dz) % 4) * 4 + ((xl + dx) % 2) * 2 + (core + dc) % 2

    def a2a(j):
        device = {"group": target_of(j)}
        return remote(packed.at[j], got_ref.at[g], a2a_send.at[j], a2a_recv.at[j], device)

    def fill(j, target):
        row = 0
        for r in range(1, R):
            row = jnp.where(dest_ref[g * R + r] == target, r, row)
        for kv in range(2):
            packed[j, kv] = cache[row, kv]

    def send_caches(*rows):
        for j in rows:
            fill(j, target_of(j))
            a2a(j).start()

    z_next, z_last = ((z + 1) % 4) * 4 + xl * 2 + core, ((z + 3) % 4) * 4 + xl * 2 + core

    def z_in(m, kv):
        return remote(
            packed.at[8 + m, kv], through_z.at[kv, m], zi_send.at[kv, m], zi_recv.at[kv, m],
            {"group": (z_next, z_last)[kv]},
        )

    def z_out(m, kv):
        onward, source = ((z_next // 4, z_last), (z_last // 4, z_next))[kv]
        target = onward * 4 + ((xl + m // 2) % 2) * 2 + (core + m % 2) % 2
        return remote(
            through_z.at[kv, m], got_ref.at[source, kv], zo_send.at[kv, m], zo_recv.at[kv, m],
            {"group": target},
        )

    halves_z = [(m, kv) for m in range(4) for kv in range(2)]

    loads[0].wait()
    for m in range(4):
        fill(8 + m, target_of(8 + m))
        z_in(m, 0).start()
        z_in(m, 1).start()
    send_caches(1)
    fill(0, g)
    own_copy = pltpu.make_async_copy(packed.at[0], got_ref.at[g], a2a_send.at[0])
    own_copy.start()

    loads[5].wait()
    xin[...] = jnp.zeros_like(xin)
    xin[0:R, :] = dec_ref[...].astype(F32)
    token = lax.broadcasted_iota(jnp.int32, (TOK, NT * SH), 1)
    place = lax.broadcasted_iota(jnp.int32, (TOK, NT * SH), 0)
    inside = (place & (SP - 1)) < SH
    spread = ((place - (place >> 6) * (SP - SH) == token) & inside).astype(F32).astype(BF)
    ids = jnp.broadcast_to(doc_ref[...].astype(F32) + 1.0, (HD, NT * SH)).astype(BF)
    docr_ref[...] = dot_t(ids[:16], spread)
    docc_ref[...] = dot_t(spread, ids)

    fin[...] = jnp.zeros_like(fin)

    lane = lax.broadcasted_iota(jnp.int32, (RP, NG * RP), 1)
    slot_row = lax.broadcasted_iota(jnp.int32, (RP, NG * RP), 0)

    def wanted(e, c):
        want, span = c
        for r in range(R):
            here = jnp.where(dest_ref[e * R + r] == g, slot_ref[e * R + r], -1)
            spot = lane == e * RP + r
            want = jnp.where(spot, here, want)
            span = jnp.where(spot, len_ref[e * R + r], span)
        return want, span

    none = jnp.full((RP, NG * RP), -1, jnp.int32)
    want, span = lax.fori_loop(0, NG, wanted, (none, jnp.zeros_like(none)))
    source = jnp.sum(jnp.where(want == slot_row, lane >> 4, 0), axis=-1, keepdims=True)
    length = jnp.sum(jnp.where(want == slot_row, span, 0), axis=-1, keepdims=True)
    plan_lane = lax.broadcasted_iota(jnp.int32, (RP, HD), 1)
    pick[...] = (source == plan_lane).astype(F32).astype(BF)
    row_dest = jnp.full((RP, HD), -1, jnp.int32)
    for r in range(R):
        row_dest = jnp.where(plan_lane == r, dest_ref[g * R + r], row_dest)
    outward = row_dest == lax.broadcasted_iota(jnp.int32, (RP, HD), 0)
    drop[...] = outward.astype(F32).astype(BF)
    plan_ref[...] = jnp.where(plan_lane == 0, source, length)

    row_of = lax.broadcasted_iota(jnp.int32, (4 * RP, HD), 0) & (RP - 1)
    column_row = lax.broadcasted_iota(jnp.int32, (HD, 4 * RP), 1) & (RP - 1)
    lens = jnp.ones((4 * RP, HD), jnp.int32)
    for r in range(R):
        lens = jnp.where(row_of == r, len_ref[g * R + r], lens)
    cached = lax.broadcasted_iota(jnp.int32, (4 * RP, CTX), 1) < lens[:, 0:1]

    def stack4(v):
        return jnp.concatenate([v] * 4, axis=0)

    def dec_norm(x):
        wide = x.astype(F32)
        nx[...] = (wide * gain_ref[...]).astype(BF)
        return lax.rsqrt(jnp.mean(wide * wide, axis=-1, keepdims=True) + EPS)

    def dec_heads(proj):
        q = jnp.concatenate([proj[:, i * HD : (i + 1) * HD] for i in range(4)], axis=0)
        q = head_norm(q, qgain_ref[...])
        return q, (head_norm(proj[:, 512:640], kgain_ref[...]), proj[:, 640:768].astype(BF))

    def dec_weights(q, new):
        qf = q.astype(F32)
        qt = qf.T.astype(BF)

        def chunk(n, c):
            spots = pl.ds(pl.multiple_of(n * HD, HD), HD)
            acc = jnp.zeros((HD, 4 * RP), F32)
            for r in range(R):
                acc = jnp.where(column_row == r, dot(cache[r, 0, spots, :], qt), acc)
            scores[:, spots] = acc.T
            return c

        lax.fori_loop(0, CTX // HD, chunk, 0)
        s = jnp.where(cached, scores[...] * INV, LOW)
        fresh = [
            jnp.sum(qf * stack4(k.astype(F32)), axis=-1, keepdims=True) * INV for k, _ in new
        ]
        top = functools.reduce(jnp.maximum, fresh, jnp.max(s, axis=-1, keepdims=True))
        e = jnp.exp(s - top)
        ef = [jnp.exp(f - top) for f in fresh]
        total = functools.reduce(jnp.add, ef, jnp.sum(e, axis=-1, keepdims=True))
        inv = 1.0 / total
        return (e * inv).astype(BF), [(f * inv).astype(BF).astype(F32) for f in ef]

    def dec_attn(w, wf, new):
        def value_row(r, acc):
            return acc + jnp.where(row_of == r, dot(w, cache[r, 1]), 0.0)

        o = lax.fori_loop(0, R, value_row, jnp.zeros((4 * RP, HD), F32), unroll=True)
        for f, (_, v) in zip(wf, new):
            o = o + f * stack4(v.astype(F32))
        o = o.astype(BF)
        return jnp.concatenate([o[i * RP : (i + 1) * RP] for i in range(4)], axis=1)

    def dec_out(step, o):
        for p in range(NT):
            part[step, p] = dot(o, wo[:, p * SL : (p + 1) * SL])
        send_parts(step)

    def send_parts(step):
        lax.fori_loop(1, NT, lambda k, c: (part_copy(step, k).start(), c)[1], 0)

    def part_copy(step, k):
        peer = (t + k) % NT
        return remote(
            part.at[step, peer], gather_part.at[step, t],
            dp_send.at[step, k], dp_recv.at[step, k], {"tp": peer},
        )

    def reduce_parts(step, base):
        lax.fori_loop(1, NT, lambda k, c: (part_copy(step, k).wait_recv(), c)[1], 0)
        total = lax.fori_loop(
            1, NT, lambda k, acc: acc + gather_part[step, (t + k) % NT], part[step, t]
        )
        return (base.astype(F32) + total).astype(BF)

    def x_copy(k):
        return remote(xbuf.at[t], xbuf.at[t], dx_send.at[k], dx_recv.at[k], {"tp": (t + k) % NT})

    loads[2].wait()
    to_row = lax.broadcasted_iota(jnp.int32, (256, 256), 0)
    from_row = lax.broadcasted_iota(jnp.int32, (256, 256), 1)
    parting = (from_row == 2 * (to_row & (HD - 1)) + (to_row >= HD).astype(jnp.int32)).astype(F32).astype(BF)

    def part_rows(b, c):
        both = dot(parting, wkv[pl.ds(pl.multiple_of(b * 256, 256), 256), :]).astype(BF)
        rows = pl.ds(pl.multiple_of(b * HD, HD), HD)
        wqkv[rows, 512:640] = both[:HD]
        wqkv[rows, 640:768] = both[HD:]
        return c

    lax.fori_loop(0, D // HD, part_rows, 0, unroll=8)

    def prepare(p, c):
        total = jnp.zeros((SH, 1), F32)
        rows = pl.ds(pl.multiple_of(p * SP, SP), SP)
        for a in range(2):
            both = xg[p, a].astype(F32)
            for i in range(2):
                x = both[i * SH : (i + 1) * SH]
                total = total + jnp.sum(x * x, axis=-1, keepdims=True)
                start = a * HALF + i * QUART
                n = x * gain_ref[:, start : start + QUART]
                n = jnp.concatenate([n, jnp.zeros((SP - SH, QUART), F32)], axis=0)
                xn[rows, start : start + QUART] = n.astype(BF)
        scale = lax.rsqrt(total / D + EPS)
        scale = jnp.concatenate([scale, jnp.zeros((SP - SH, 1), F32)], axis=0)
        sc[rows, :] = jnp.broadcast_to(scale, (SP, HD))
        return c

    def project(shards, dec_scale=None):
        spots = [pl.ds(pl.multiple_of(p * SP, SP), SP) for p in shards]
        lhs = [xn[rows, :] for rows in spots]
        scale = [sc[rows, 0:1] for rows in spots]
        if dec_scale is not None:
            lhs.append(nx[...])
            scale.append(dec_scale)
        lhs = jnp.concatenate(lhs, axis=0)
        scale = jnp.concatenate(scale, axis=0)
        extra = []
        for j in range(3):
            v = dot(lhs, wqkv[:, j * 256 : (j + 1) * 256]) * scale
            extra.append(v[len(shards) * SP :])
            for n, rows in enumerate(spots):
                mine_v = v[n * SP : (n + 1) * SP]
                if j < 2:
                    for i in range(2):
                        head = mine_v[:, i * HD : (i + 1) * HD]
                        qs[2 * j + i, rows, :] = head_norm(head, qgain_ref[...])
                else:
                    ks[rows, :] = head_norm(mine_v[:, :HD], kgain_ref[...]).astype(F32)
                    vs[rows, :] = mine_v[:, HD:].astype(BF)
        if dec_scale is not None:
            return dec_heads(jnp.concatenate(extra, axis=1))

    prepare(mine, 0)
    scale0 = dec_norm(xin[...])
    for a in range(2):
        x_in[a].wait_recv()
        x_out[a].start()
    loads[1].wait()
    q0, new0 = project((mine,), scale0)
    for a in range(2):
        x_out[a].wait_recv()
    second_up.start()
    second_down.start()
    first_up.wait_recv()
    fwd_up[0].start()
    first_down.wait_recv()
    fwd_down[0].start()
    send_caches(2)
    for m, kv in halves_z[:4]:
        z_in(m, kv).wait_recv()
        z_out(m, kv).start()
    w0, wf0 = dec_weights(q0, [new0])
    loads[3].wait()
    dec_out(0, dec_attn(w0, wf0, [new0]))
    for m, kv in halves_z[4:]:
        z_in(m, kv).wait_recv()
        z_out(m, kv).start()
    prepare(partner, 0)
    prepare(down * 2 + h, 0)
    prepare(up * 2 + h, 0)
    project((partner, down * 2 + h, up * 2 + h))

    base0 = xin[:, pl.ds(pl.multiple_of(t * SL, SL), SL)]
    xbuf[t] = reduce_parts(0, base0)
    lax.fori_loop(1, NT, lambda k, c: (x_copy(k).start(), c)[1], 0)

    second_up.wait_recv()
    fwd_up[1].start()
    second_down.wait_recv()
    fwd_down[1].start()
    send_caches(3, 6)
    prepare(down * 2 + oh, 0)
    prepare(up * 2 + oh, 0)
    lax.fori_loop(1, NT, lambda k, c: (x_copy(k).wait_recv(), c)[1], 0)
    scale1 = dec_norm(jnp.concatenate([xbuf[p] for p in range(NT)], axis=1))
    q1, new1 = project((down * 2 + oh, up * 2 + oh), scale1)
    send_caches(14, 4)
    fwd_up[0].wait_recv()
    fwd_down[0].wait_recv()
    prepare(far * 2 + h, 0)
    fwd_up[1].wait_recv()
    fwd_down[1].wait_recv()
    prepare(far * 2 + oh, 0)
    project((far * 2 + h, far * 2 + oh))
    kt[...] = ks[...].T.astype(BF)
    send_caches(7, 12)

    later_col = lax.broadcasted_iota(jnp.int32, (2 * SP, TOK), 1)
    later_row = lax.broadcasted_iota(jnp.int32, (2 * SP, TOK), 0)

    def heads_of(block):
        rows = pl.ds(pl.multiple_of(block * 2 * SP, 2 * SP), 2 * SP)
        live = (docc_ref[rows, 0:1] == docr_ref[0:1, :]) & (later_col <= later_row + block * (2 * SP))
        heads = []
        for i in range(4):
            s = jnp.where(live, dot(qs[i, rows, :], kt[...]) * INV, LOW)
            e = jnp.exp(s - jnp.max(s, axis=-1, keepdims=True))
            inv = 1.0 / jnp.sum(e, axis=-1, keepdims=True)
            heads.append(dot((e * inv).astype(BF), vs[...]).astype(BF))
        return jnp.concatenate(heads, axis=1)

    def attend(blocks, dec=None):
        attn = [heads_of(block) for block in blocks]
        if dec is not None:
            attn.append(dec)
        attn = jnp.concatenate(attn, axis=0)
        for a in range(2):
            lo, hi = [
                dot(attn, wo[:, a * HALF + i * QUART : a * HALF + (i + 1) * QUART]) for i in range(2)
            ]
            for n, block in enumerate(blocks):
                for i in range(2):
                    start = (2 * n + i) * SP
                    pair = [v[start : start + SH] for v in (lo, hi)]
                    terms[block * 2 + i, a] = jnp.concatenate(pair, axis=0).astype(BF)
            if dec is not None:
                start = len(blocks) * 2 * SP
                for i, v in enumerate((lo, hi)):
                    for k in range(2):
                        part[1, 4 * a + 2 * i + k] = v[start:, k * SL : (k + 1) * SL]

    order = (oh, h)

    def rs(n, src, dst, device):
        return Several(pieces(SUM_CUTS, src, dst, rs_send, rs_recv, 3 * n, device))

    far_up = [rs(i, terms.at[far * 2 + order[i], 0], relay.at[0, i], to_up) for i in range(2)]
    far_down = [rs(2 + i, terms.at[far * 2 + order[i], 1], relay.at[1, i], to_down) for i in range(2)]
    near_up = [
        [rs(4 + 2 * i + a, terms.at[up * 2 + order[i], a], arrive.at[0, i, a], to_up) for a in range(2)]
        for i in range(2)
    ]
    near_down = [
        [rs(8 + 2 * i + a, terms.at[down * 2 + order[i], a], arrive.at[1, i, a], to_down) for a in range(2)]
        for i in range(2)
    ]
    over_in, over = exchange(
        cross.at[0], through_cross, lambda a: cross.at[1, a], ex_send.at[1], ex_recv.at[1]
    )

    def relay_up(i):
        far_up[i].wait_recv()
        spot = up * 2 + order[i]
        terms[spot, 0] = (terms[spot, 0].astype(F32) + relay[0, i].astype(F32)).astype(BF)
        near_up[i][0].start()

    def relay_down(i):
        far_down[i].wait_recv()
        spot = down * 2 + order[i]
        terms[spot, 1] = (terms[spot, 1].astype(F32) + relay[1, i].astype(F32)).astype(BF)
        near_down[i][1].start()

    def summed(i, a):
        near_up[i][a].wait_recv()
        near_down[i][a].wait_recv()
        return (
            terms[y * 2 + order[i], a].astype(F32)
            + arrive[0, i, a].astype(F32)
            + arrive[1, i, a].astype(F32)
        )

    attend((far,))
    far_up[0].start()
    far_down[0].start()
    attend((up, down))
    send_caches(15)
    far_up[0].wait_send()
    near_up[0][1].start()
    far_down[0].wait_send()
    near_down[0][0].start()
    relay_up(0)
    relay_down(0)
    send_caches(5, 13)
    w1, wf1 = dec_weights(q1, [new0, new1])
    attend((y,), dec_attn(w1, wf1, [new0, new1]))
    send_parts(1)
    near_up[0][0].wait_send()
    far_up[1].start()
    near_down[0][1].wait_send()
    far_down[1].start()
    for a in range(2):
        cross[0, a] = summed(0, a).astype(BF)
        over_in[a].start()

    columns = [reduce_parts(1, xbuf[t])]
    for k, v in (new0, new1):
        columns += [k, v]
    leaving = dot(drop[:, :RP], jnp.concatenate(columns, axis=1))
    for i in range(MSG // HD):
        fin[:, i, :] = leaving[:, i * HD : (i + 1) * HD]
    arrived[g] = fin[g]

    def fin_copy(k):
        target = (g + k) % NG
        return remote(fin.at[target], arrived.at[g], fin_send.at[k], fin_recv.at[k], {"group": target})

    lax.fori_loop(1, NG, lambda k, c: (fin_copy(k).start(), c)[1], 0)

    far_up[1].wait_send()
    near_up[1][1].start()
    far_down[1].wait_send()
    near_down[1][0].start()
    for a in range(2):
        over_in[a].wait_recv()
        over[a].start()
    relay_up(1)
    relay_down(1)

    for a in range(2):
        near = summed(1, a)
        for i in range(2):
            cols = slice(a * HALF + i * QUART, a * HALF + (i + 1) * QUART)
            add = near[i * SH : (i + 1) * SH]
            score_sum[:, cols] = score_ref[:, cols].astype(F32) + add

    lax.fori_loop(1, NG, lambda k, c: (fin_copy(k).wait_recv(), c)[1], 0)
    placed = [dot(pick[:, :NG], arrived[:, i, :].astype(BF)) for i in range(MSG // HD)]
    obuf[t] = jnp.concatenate(placed[: SL // HD], axis=1).astype(BF)
    patch_ref[...] = jnp.concatenate(placed[SL // HD :], axis=1)

    def o_copy(k):
        return remote(obuf.at[t], obuf.at[t], o_send.at[k], o_recv.at[k], {"tp": (t + k) % NT})

    lax.fori_loop(1, NT, lambda k, c: (o_copy(k).start(), c)[1], 0)

    for a in range(2):
        over[a].wait_recv()
        far_half = cross[1, a].astype(F32)
        for i in range(2):
            cols = slice(a * HALF + i * QUART, a * HALF + (i + 1) * QUART)
            add = far_half[i * SH : (i + 1) * SH]
            score_out_ref[:, cols] = (score_sum[:, cols] + add).astype(BF)

    lax.fori_loop(1, NT, lambda k, c: (o_copy(k).wait_recv(), c)[1], 0)
    for p in range(NT):
        dec_out_ref[:, p * SL : (p + 1) * SL] = obuf[p]

    def end_a2a(j, c):
        a2a(j).wait()
        return c

    lax.fori_loop(1, 8, end_a2a, 0)
    lax.fori_loop(12, NG, end_a2a, 0)
    for m, kv in halves_z:
        z_out(m, kv).wait()
    own_copy.wait()
    ended = [first_up, first_down, second_up, second_down] + fwd_up + fwd_down
    ended += x_in + x_out + over_in + over + [z_in(m, kv) for m, kv in halves_z]
    ended += near_up[1] + near_down[1] + [near_up[0][1], near_down[0][0]]
    for c in ended:
        c.wait_send()

    def end_tp(k, c):
        part_copy(0, k).wait_send()
        part_copy(1, k).wait_send()
        x_copy(k).wait_send()
        o_copy(k).wait_send()
        return c

    lax.fori_loop(1, NT, end_tp, 0)
    lax.fori_loop(1, NG, lambda k, c: (fin_copy(k).wait_send(), c)[1], 0)


def place_kernel(
    plan_ref, patch_ref, dec_ref, got_hbm, score_hbm,
    dec_out_ref, cache_out, score_out, rows, score_rows, in_sem, out_sem, score_sem,
):
    score_in = pltpu.make_async_copy(score_hbm, score_rows, score_sem.at[0])
    score_end = pltpu.make_async_copy(score_rows, score_out, score_sem.at[1])
    score_in.start()

    def get(s, c):
        pltpu.make_async_copy(got_hbm.at[plan_ref[s, 0]], rows.at[s], in_sem.at[s]).start()
        return c

    lax.fori_loop(0, R, get, 0)
    dec_out_ref[...] = dec_ref[:R, :]
    score_in.wait()
    score_end.start()

    def put(s, c):
        pltpu.make_async_copy(got_hbm.at[0], rows.at[s], in_sem.at[s]).wait()
        entry = patch_ref[pl.ds(s, 1), :]
        for step in range(2):
            pos = plan_ref[s, 1] + step
            base = pl.multiple_of((pos // 16) * 16, 16)
            here = lax.broadcasted_iota(jnp.int32, (16, HD), 0) == pos - base
            for kv in range(2):
                start = (2 * step + kv) * HD
                old = rows[s, kv, pl.ds(base, 16), :].astype(F32)
                both = jnp.where(here, entry[:, start : start + HD], old)
                rows[s, kv, pl.ds(base, 16), :] = both.astype(BF)
        pltpu.make_async_copy(rows.at[s], cache_out.at[s], out_sem.at[s]).start()
        return c

    lax.fori_loop(0, R, put, 0)

    def end(s, c):
        pltpu.make_async_copy(rows.at[s], cache_out.at[s], out_sem.at[s]).wait()
        return c

    lax.fori_loop(0, R, end, 0)
    score_end.wait()


def per_device(
    dec_rows, kv_cache, lengths, dest_group, dest_slot, score_rows, doc_ids,
    norm_gain, query_gain, key_gain, w_query, w_keyval, w_out,
):
    smem = pl.BlockSpec(memory_space=pltpu.SMEM)
    vmem = pl.BlockSpec(memory_space=pltpu.VMEM)
    hbm = pl.BlockSpec(memory_space=pl.ANY)
    dma = pltpu.SemaphoreType.DMA
    got, patch, plan, dec_out16, score_sum = pl.pallas_call(
        main_kernel,
        name="decode_and_score",
        out_shape=(
            jax.ShapeDtypeStruct((NG, 2, CTX, HD), BF),
            jax.ShapeDtypeStruct((RP, 4 * HD), F32),
            jax.ShapeDtypeStruct((RP, HD), jnp.int32),
            jax.ShapeDtypeStruct((RP, D), BF),
            jax.ShapeDtypeStruct((SH, D), BF),
        ),
        in_specs=[smem] * 3 + [vmem] * 4 + [hbm] * 6,
        out_specs=(hbm, vmem, vmem, vmem, vmem),
        scratch_shapes=[
            pltpu.VMEM((SH, D), BF),
            pltpu.VMEM((R, D), BF),
            pltpu.VMEM((R, 2, CTX, HD), BF),
            pltpu.VMEM((2 * D, HD), BF),
            pltpu.VMEM((D, 768), BF),
            pltpu.VMEM((512, D), BF),
            pltpu.VMEM((RP, D), F32),
            pltpu.VMEM((16, TOK), F32),
            pltpu.VMEM((TOK, HD), F32),
            pltpu.VMEM((NG, 2, CTX, HD), BF),
            pltpu.VMEM((NT, 2, 2 * SH, QUART), BF),
            pltpu.VMEM((TOK, D), BF),
            pltpu.VMEM((TOK, HD), F32),
            pltpu.VMEM((4, TOK, HD), BF),
            pltpu.VMEM((TOK, HD), F32),
            pltpu.VMEM((HD, TOK), BF),
            pltpu.VMEM((TOK, HD), BF),
            pltpu.VMEM((NT, 2, 2 * SH, QUART), BF),
            pltpu.VMEM((2, 2, 2 * SH, QUART), BF),
            pltpu.VMEM((2, 2, 2, 2 * SH, QUART), BF),
            pltpu.VMEM((2, 2, 2 * SH, QUART), BF),
            pltpu.VMEM((2, 2 * SH, QUART), BF),
            pltpu.VMEM((2, 4, CTX, HD), BF),
            pltpu.VMEM((2, 2 * SH, QUART), BF),
            pltpu.VMEM((SH, D), F32),
            pltpu.VMEM((2, NT, RP, SL), F32),
            pltpu.VMEM((2, NT, RP, SL), F32),
            pltpu.VMEM((NT, RP, SL), BF),
            pltpu.VMEM((RP, D), BF),
            pltpu.VMEM((4 * RP, CTX), F32),
            pltpu.VMEM((RP, HD), BF),
            pltpu.VMEM((RP, HD), BF),
            pltpu.VMEM((NG, RP, HD), F32),
            pltpu.VMEM((NG, RP, HD), F32),
            pltpu.VMEM((NT, RP, SL), BF),
            dma((6,)), dma((NG,)), dma((NG,)), dma((2, 4)), dma((2, 4)), dma((2, 4)), dma((2, 4)), dma((2, 4)), dma((2, 4)), dma((28,)), dma((28,)), dma((42,)), dma((42,)),
            dma((2, NT)), dma((2, NT)), dma((NT,)), dma((NT,)), dma((NG,)), dma((NG,)),
            dma((NT,)), dma((NT,)),
        ],
        compiler_params=pltpu.CompilerParams(
            collective_id=0, has_side_effects=True, vmem_limit_bytes=60 * 1024 * 1024
        ),
        cost_estimate=pl.CostEstimate(flops=8 * 10**9, bytes_accessed=30 * 10**6, transcendentals=10**6),
    )(
        dest_group, dest_slot, lengths, norm_gain.reshape(1, D),
        query_gain.reshape(1, HD), key_gain.reshape(1, HD), doc_ids,
        kv_cache, w_query, w_keyval.reshape(2 * D, HD), w_out, score_rows, dec_rows,
    )
    return pl.pallas_call(
        place_kernel,
        name="place_rows",
        out_shape=(
            jax.ShapeDtypeStruct((R, D), BF),
            jax.ShapeDtypeStruct((R, 2, CTX, HD), BF),
            jax.ShapeDtypeStruct((SH, D), BF),
        ),
        in_specs=[smem] + [vmem] * 2 + [hbm] * 2,
        out_specs=(vmem, hbm, hbm),
        scratch_shapes=[
            pltpu.VMEM((R, 2, CTX, HD), BF),
            pltpu.VMEM((SH, D), BF),
            dma((R,)), dma((R,)), dma((2,)),
        ],
        compiler_params=pltpu.CompilerParams(vmem_limit_bytes=60 * 1024 * 1024),
        cost_estimate=pl.CostEstimate(flops=10**6, bytes_accessed=12 * 10**6, transcendentals=0),
    )(plan, patch, dec_out16, got, score_sum)


def solution(mesh):
    placed = (
        P("group", None),
        P("group", None, None, "tp"),
        P(),
        P(),
        P(),
        P(("group", "tp"), None),
        P("group", None),
        P(),
        P(),
        P(),
        P(None, "tp"),
        P(None, None, "tp"),
        P("tp", None),
    )
    return jax.shard_map(
        per_device,
        mesh=mesh,
        in_specs=placed,
        out_specs=(P("group", None), P("group", None, None, "tp"), P(("group", "tp"), None)),
        check_vma=False,
    )
```

```python
import functools
import math

import jax
import jax.numpy as jnp
from jax import lax
from jax.experimental import pallas as pl
from jax.experimental.pallas import tpu as pltpu
from jax.sharding import PartitionSpec as P

HD = 128
EPS = 1e-06
MESH = pl.DeviceIdType.MESH
BF = jnp.bfloat16
F32 = jnp.float32
LOW = -1e30
INV = 1.0 / math.sqrt(HD)

D = 5120
CTX = 768
NG = 16
NT = 8
R = 14
RP = 16
SH = 56
SP = 64
TOK = NT * SP
HALF = D // 2
QUART = D // 4
SL = D // NT
MSG = SL + 4 * HD
GATHER_CUTS = ((0, 112),)
SUM_CUTS = ((0, 112),)


def head_norm(vectors, gain):
    mean = jnp.mean(vectors * vectors, axis=-1, keepdims=True)
    return (vectors * lax.rsqrt(mean + EPS) * gain).astype(BF)


def dot(a, b):
    return jnp.dot(a, b, preferred_element_type=F32)


class Several:
    def __init__(self, copies):
        self.copies = copies

    def start(self):
        for copy in self.copies:
            copy.start()

    def wait_recv(self):
        for copy in self.copies:
            copy.wait_recv()

    def wait_send(self):
        for copy in self.copies:
            copy.wait_send()


def dot_t(a, b):
    return lax.dot_general(a, b, (((1,), (1,)), ((), ())), preferred_element_type=F32)


def main_kernel(
    dest_ref, slot_ref, len_ref,
    gain_ref, qgain_ref, kgain_ref, doc_ref,
    cache_hbm, wq_hbm, wkv_hbm, wo_hbm, score_hbm, dec_hbm,
    got_ref, patch_ref, plan_ref, dec_out_ref, score_out_ref,
    score_ref, dec_ref, cache, wkv, wqkv, wo, xin, docr_ref, docc_ref, packed, xg, xn, sc, qs, ks, kt, vs, terms,
    relay, arrive, cross, through_x, through_z, through_cross, score_sum, part, gather_part, xbuf, nx, scores, pick, drop, fin, arrived, obuf,
    load_sem, a2a_send, a2a_recv, ex_send, ex_recv, zi_send, zi_recv, zo_send, zo_recv, ag_send, ag_recv, rs_send, rs_recv,
    dp_send, dp_recv, dx_send, dx_recv, fin_send, fin_recv, o_send, o_recv,
):
    g = lax.axis_index("group")
    t = lax.axis_index("tp")
    y, h = t // 2, t % 2
    z, xl, core = g // 4, (g // 2) % 2, g % 2
    oh = 1 - h
    up, down, far = (y + 1) % 4, (y + 3) % 4, (y + 2) % 4
    mine, partner = t, y * 2 + oh
    g_x = z * 4 + (1 - xl) * 2 + core
    to_up, to_down = {"tp": up * 2 + h}, {"tp": down * 2 + h}
    via_same, via_other = (g_x, t), (g_x, partner)

    def remote(src, dst, send, recv, device):
        return pltpu.make_async_remote_copy(
            src_ref=src, dst_ref=dst, send_sem=send, recv_sem=recv,
            device_id=device, device_id_type=MESH,
        )

    barrier = pltpu.get_barrier_semaphore()

    def greet_tp(k, c):
        pl.semaphore_signal(barrier, inc=1, device_id={"tp": (t + k) % NT}, device_id_type=MESH)
        return c

    def greet_group(k, c):
        pl.semaphore_signal(barrier, inc=1, device_id={"group": (g + k) % NG}, device_id_type=MESH)
        return c

    lax.fori_loop(1, NT, greet_tp, 0)
    lax.fori_loop(1, NG, greet_group, 0)
    pl.semaphore_signal(barrier, inc=1, device_id=(g_x, partner), device_id_type=MESH)

    loads = [
        pltpu.make_async_copy(cache_hbm, cache, load_sem.at[0]),
        pltpu.make_async_copy(wq_hbm, wqkv.at[:, pl.ds(0, 512)], load_sem.at[1]),
        pltpu.make_async_copy(wkv_hbm, wkv, load_sem.at[2]),
        pltpu.make_async_copy(wo_hbm, wo, load_sem.at[3]),
        pltpu.make_async_copy(score_hbm, score_ref, load_sem.at[4]),
        pltpu.make_async_copy(dec_hbm, dec_ref, load_sem.at[5]),
    ]
    for i in (4, 0, 5, 2, 1, 3):
        loads[i].start()

    loads[4].wait()
    for a in range(2):
        lo = score_ref[:, a * HALF : a * HALF + QUART].astype(F32)
        hi = score_ref[:, a * HALF + QUART : (a + 1) * HALF].astype(F32)
        xg[mine, a] = jnp.concatenate([lo, hi], axis=0).astype(BF)

    pl.semaphore_wait(barrier, NT + NG - 1)

    def pieces(cuts, src, dst, send, recv, base, device):
        return [
            remote(
                src.at[pl.ds(lo, n), :], dst.at[pl.ds(lo, n), :],
                send.at[base + i], recv.at[base + i], device,
            )
            for i, (lo, n) in enumerate(cuts)
        ]

    def ag(base, shard, halves, device):
        copies = []
        for i, a in enumerate(halves):
            where = xg.at[shard, a]
            copies += pieces(GATHER_CUTS, where, where, ag_send, ag_recv, base + 2 * i, device)
        return Several(copies)

    def exchange(src, through, dst, send, recv):
        ins = [
            remote(src.at[a], through.at[a], send.at[a], recv.at[a], device)
            for a, device in enumerate((via_same, via_other))
        ]
        outs = [
            remote(through.at[a], dst(a), send.at[2 + a], recv.at[2 + a], device)
            for a, device in enumerate((via_other, via_same))
        ]
        return ins, outs

    x_in, x_out = exchange(
        xg.at[mine], through_x, lambda a: xg.at[(mine, partner)[a], a], ex_send.at[0], ex_recv.at[0]
    )
    first_up, first_down = ag(4, mine, (0, 1), to_up), ag(8, mine, (0, 1), to_down)
    for c in (*x_in, first_up, first_down):
        c.start()
    second_up, second_down = ag(12, partner, (0, 1), to_up), ag(16, partner, (0, 1), to_down)
    fwd_up = [ag(20 + 2 * i, down * 2 + hh, (0,), to_up) for i, hh in enumerate((h, oh))]
    fwd_down = [ag(24 + 2 * i, up * 2 + hh, (1,), to_down) for i, hh in enumerate((h, oh))]

    def target_of(j):
        dz, dx, dc = j // 4, (j // 2) % 2, j % 2
        return ((z + dz) % 4) * 4 + ((xl + dx) % 2) * 2 + (core + dc) % 2

    def a2a(j):
        device = {"group": target_of(j)}
        return remote(packed.at[j], got_ref.at[g], a2a_send.at[j], a2a_recv.at[j], device)

    def fill(j, target):
        row = 0
        for r in range(1, R):
            row = jnp.where(dest_ref[g * R + r] == target, r, row)
        for kv in range(2):
            packed[j, kv] = cache[row, kv]

    def send_caches(*rows):
        for j in rows:
            fill(j, target_of(j))
            a2a(j).start()

    z_next, z_last = ((z + 1) % 4) * 4 + xl * 2 + core, ((z + 3) % 4) * 4 + xl * 2 + core

    def z_in(m, kv):
        return remote(
            packed.at[8 + m, kv], through_z.at[kv, m], zi_send.at[kv, m], zi_recv.at[kv, m],
            {"group": (z_next, z_last)[kv]},
        )

    def z_out(m, kv):
        onward, source = ((z_next // 4, z_last), (z_last // 4, z_next))[kv]
        target = onward * 4 + ((xl + m // 2) % 2) * 2 + (core + m % 2) % 2
        return remote(
            through_z.at[kv, m], got_ref.at[source, kv], zo_send.at[kv, m], zo_recv.at[kv, m],
            {"group": target},
        )

    halves_z = [(m, kv) for m in range(4) for kv in range(2)]

    loads[0].wait()
    for m in range(4):
        fill(8 + m, target_of(8 + m))
        z_in(m, 0).start()
        z_in(m, 1).start()
    send_caches(1)
    fill(0, g)
    own_copy = pltpu.make_async_copy(packed.at[0], got_ref.at[g], a2a_send.at[0])
    own_copy.start()

    loads[5].wait()
    xin[...] = jnp.zeros_like(xin)
    xin[0:R, :] = dec_ref[...].astype(F32)
    token = lax.broadcasted_iota(jnp.int32, (TOK, NT * SH), 1)
    place = lax.broadcasted_iota(jnp.int32, (TOK, NT * SH), 0)
    inside = (place & (SP - 1)) < SH
    spread = ((place - (place >> 6) * (SP - SH) == token) & inside).astype(F32).astype(BF)
    ids = jnp.broadcast_to(doc_ref[...].astype(F32) + 1.0, (HD, NT * SH)).astype(BF)
    docr_ref[...] = dot_t(ids[:16], spread)
    docc_ref[...] = dot_t(spread, ids)

    fin[...] = jnp.zeros_like(fin)

    lane = lax.broadcasted_iota(jnp.int32, (RP, NG * RP), 1)
    slot_row = lax.broadcasted_iota(jnp.int32, (RP, NG * RP), 0)

    def wanted(e, c):
        want, span = c
        for r in range(R):
            here = jnp.where(dest_ref[e * R + r] == g, slot_ref[e * R + r], -1)
            spot = lane == e * RP + r
            want = jnp.where(spot, here, want)
            span = jnp.where(spot, len_ref[e * R + r], span)
        return want, span

    none = jnp.full((RP, NG * RP), -1, jnp.int32)
    want, span = lax.fori_loop(0, NG, wanted, (none, jnp.zeros_like(none)))
    source = jnp.sum(jnp.where(want == slot_row, lane >> 4, 0), axis=-1, keepdims=True)
    length = jnp.sum(jnp.where(want == slot_row, span, 0), axis=-1, keepdims=True)
    plan_lane = lax.broadcasted_iota(jnp.int32, (RP, HD), 1)
    pick[...] = (source == plan_lane).astype(F32).astype(BF)
    row_dest = jnp.full((RP, HD), -1, jnp.int32)
    for r in range(R):
        row_dest = jnp.where(plan_lane == r, dest_ref[g * R + r], row_dest)
    outward = row_dest == lax.broadcasted_iota(jnp.int32, (RP, HD), 0)
    drop[...] = outward.astype(F32).astype(BF)
    plan_ref[...] = jnp.where(plan_lane == 0, source, length)

    row_of = lax.broadcasted_iota(jnp.int32, (4 * RP, HD), 0) & (RP - 1)
    column_row = lax.broadcasted_iota(jnp.int32, (HD, 4 * RP), 1) & (RP - 1)
    lens = jnp.ones((4 * RP, HD), jnp.int32)
    for r in range(R):
        lens = jnp.where(row_of == r, len_ref[g * R + r], lens)
    cached = lax.broadcasted_iota(jnp.int32, (4 * RP, CTX), 1) < lens[:, 0:1]

    def stack4(v):
        return jnp.concatenate([v] * 4, axis=0)

    def dec_norm(x):
        wide = x.astype(F32)
        nx[...] = (wide * gain_ref[...]).astype(BF)
        return lax.rsqrt(jnp.mean(wide * wide, axis=-1, keepdims=True) + EPS)

    def dec_heads(proj):
        q = jnp.concatenate([proj[:, i * HD : (i + 1) * HD] for i in range(4)], axis=0)
        q = head_norm(q, qgain_ref[...])
        return q, (head_norm(proj[:, 512:640], kgain_ref[...]), proj[:, 640:768].astype(BF))

    def dec_weights(q, new):
        qf = q.astype(F32)
        qt = qf.T.astype(BF)

        def chunk(n, c):
            spots = pl.ds(pl.multiple_of(n * HD, HD), HD)
            acc = jnp.zeros((HD, 4 * RP), F32)
            for r in range(R):
                acc = jnp.where(column_row == r, dot(cache[r, 0, spots, :], qt), acc)
            scores[:, spots] = acc.T
            return c

        lax.fori_loop(0, CTX // HD, chunk, 0)
        s = jnp.where(cached, scores[...] * INV, LOW)
        fresh = [
            jnp.sum(qf * stack4(k.astype(F32)), axis=-1, keepdims=True) * INV for k, _ in new
        ]
        top = functools.reduce(jnp.maximum, fresh, jnp.max(s, axis=-1, keepdims=True))
        e = jnp.exp(s - top)
        ef = [jnp.exp(f - top) for f in fresh]
        total = functools.reduce(jnp.add, ef, jnp.sum(e, axis=-1, keepdims=True))
        inv = 1.0 / total
        return (e * inv).astype(BF), [(f * inv).astype(BF).astype(F32) for f in ef]

    def dec_attn(w, wf, new):
        def value_row(r, acc):
            return acc + jnp.where(row_of == r, dot(w, cache[r, 1]), 0.0)

        o = lax.fori_loop(0, R, value_row, jnp.zeros((4 * RP, HD), F32), unroll=True)
        for f, (_, v) in zip(wf, new):
            o = o + f * stack4(v.astype(F32))
        o = o.astype(BF)
        return jnp.concatenate([o[i * RP : (i + 1) * RP] for i in range(4)], axis=1)

    def dec_out(step, o):
        for p in range(NT):
            part[step, p] = dot(o, wo[:, p * SL : (p + 1) * SL])
        send_parts(step)

    def send_parts(step):
        lax.fori_loop(1, NT, lambda k, c: (part_copy(step, k).start(), c)[1], 0)

    def part_copy(step, k):
        peer = (t + k) % NT
        return remote(
            part.at[step, peer], gather_part.at[step, t],
            dp_send.at[step, k], dp_recv.at[step, k], {"tp": peer},
        )

    def reduce_parts(step, base):
        lax.fori_loop(1, NT, lambda k, c: (part_copy(step, k).wait_recv(), c)[1], 0)
        total = lax.fori_loop(
            1, NT, lambda k, acc: acc + gather_part[step, (t + k) % NT], part[step, t]
        )
        return (base.astype(F32) + total).astype(BF)

    def x_copy(k):
        return remote(xbuf.at[t], xbuf.at[t], dx_send.at[k], dx_recv.at[k], {"tp": (t + k) % NT})

    loads[2].wait()
    to_row = lax.broadcasted_iota(jnp.int32, (256, 256), 0)
    from_row = lax.broadcasted_iota(jnp.int32, (256, 256), 1)
    parting = (from_row == 2 * (to_row & (HD - 1)) + (to_row >= HD).astype(jnp.int32)).astype(F32).astype(BF)

    def part_rows(b, c):
        both = dot(parting, wkv[pl.ds(pl.multiple_of(b * 256, 256), 256), :]).astype(BF)
        rows = pl.ds(pl.multiple_of(b * HD, HD), HD)
        wqkv[rows, 512:640] = both[:HD]
        wqkv[rows, 640:768] = both[HD:]
        return c

    lax.fori_loop(0, D // HD, part_rows, 0, unroll=8)

    def prepare(p, c):
        total = jnp.zeros((SH, 1), F32)
        rows = pl.ds(pl.multiple_of(p * SP, SP), SP)
        for a in range(2):
            both = xg[p, a].astype(F32)
            for i in range(2):
                x = both[i * SH : (i + 1) * SH]
                total = total + jnp.sum(x * x, axis=-1, keepdims=True)
                start = a * HALF + i * QUART
                n = x * gain_ref[:, start : start + QUART]
                n = jnp.concatenate([n, jnp.zeros((SP - SH, QUART), F32)], axis=0)
                xn[rows, start : start + QUART] = n.astype(BF)
        scale = lax.rsqrt(total / D + EPS)
        scale = jnp.concatenate([scale, jnp.zeros((SP - SH, 1), F32)], axis=0)
        sc[rows, :] = jnp.broadcast_to(scale, (SP, HD))
        return c

    def project(shards, dec_scale=None):
        spots = [pl.ds(pl.multiple_of(p * SP, SP), SP) for p in shards]
        lhs = [xn[rows, :] for rows in spots]
        scale = [sc[rows, 0:1] for rows in spots]
        if dec_scale is not None:
            lhs.append(nx[...])
            scale.append(dec_scale)
        lhs = jnp.concatenate(lhs, axis=0)
        scale = jnp.concatenate(scale, axis=0)
        extra = []
        for j in range(3):
            v = dot(lhs, wqkv[:, j * 256 : (j + 1) * 256]) * scale
            extra.append(v[len(shards) * SP :])
            for n, rows in enumerate(spots):
                mine_v = v[n * SP : (n + 1) * SP]
                if j < 2:
                    for i in range(2):
                        head = mine_v[:, i * HD : (i + 1) * HD]
                        qs[2 * j + i, rows, :] = head_norm(head, qgain_ref[...])
                else:
                    ks[rows, :] = head_norm(mine_v[:, :HD], kgain_ref[...]).astype(F32)
                    vs[rows, :] = mine_v[:, HD:].astype(BF)
        if dec_scale is not None:
            return dec_heads(jnp.concatenate(extra, axis=1))

    prepare(mine, 0)
    scale0 = dec_norm(xin[...])
    for a in range(2):
        x_in[a].wait_recv()
        x_out[a].start()
    loads[1].wait()
    q0, new0 = project((mine,), scale0)
    for a in range(2):
        x_out[a].wait_recv()
    second_up.start()
    second_down.start()
    first_up.wait_recv()
    fwd_up[0].start()
    first_down.wait_recv()
    fwd_down[0].start()
    send_caches(2, 4)
    for m, kv in halves_z[:4]:
        z_in(m, kv).wait_recv()
        z_out(m, kv).start()
    w0, wf0 = dec_weights(q0, [new0])
    loads[3].wait()
    dec_out(0, dec_attn(w0, wf0, [new0]))
    for m, kv in halves_z[4:]:
        z_in(m, kv).wait_recv()
        z_out(m, kv).start()
    prepare(partner, 0)
    prepare(down * 2 + h, 0)
    prepare(up * 2 + h, 0)
    project((partner, down * 2 + h, up * 2 + h))

    base0 = xin[:, pl.ds(pl.multiple_of(t * SL, SL), SL)]
    xbuf[t] = reduce_parts(0, base0)
    lax.fori_loop(1, NT, lambda k, c: (x_copy(k).start(), c)[1], 0)

    second_up.wait_recv()
    fwd_up[1].start()
    second_down.wait_recv()
    fwd_down[1].start()
    send_caches(3, 6, 12)
    prepare(down * 2 + oh, 0)
    prepare(up * 2 + oh, 0)
    lax.fori_loop(1, NT, lambda k, c: (x_copy(k).wait_recv(), c)[1], 0)
    scale1 = dec_norm(jnp.concatenate([xbuf[p] for p in range(NT)], axis=1))
    q1, new1 = project((down * 2 + oh, up * 2 + oh), scale1)
    send_caches(14, 5)
    fwd_up[0].wait_recv()
    fwd_down[0].wait_recv()
    prepare(far * 2 + h, 0)
    fwd_up[1].wait_recv()
    fwd_down[1].wait_recv()
    prepare(far * 2 + oh, 0)
    project((far * 2 + h, far * 2 + oh))
    kt[...] = ks[...].T.astype(BF)
    send_caches(7, 13)

    later_col = lax.broadcasted_iota(jnp.int32, (2 * SP, TOK), 1)
    later_row = lax.broadcasted_iota(jnp.int32, (2 * SP, TOK), 0)

    def heads_of(block):
        rows = pl.ds(pl.multiple_of(block * 2 * SP, 2 * SP), 2 * SP)
        live = (docc_ref[rows, 0:1] == docr_ref[0:1, :]) & (later_col <= later_row + block * (2 * SP))
        heads = []
        for i in range(4):
            s = jnp.where(live, dot(qs[i, rows, :], kt[...]) * INV, LOW)
            e = jnp.exp(s - jnp.max(s, axis=-1, keepdims=True))
            inv = 1.0 / jnp.sum(e, axis=-1, keepdims=True)
            heads.append(dot((e * inv).astype(BF), vs[...]).astype(BF))
        return jnp.concatenate(heads, axis=1)

    def attend(blocks, dec=None):
        attn = [heads_of(block) for block in blocks]
        if dec is not None:
            attn.append(dec)
        attn = jnp.concatenate(attn, axis=0)
        for a in range(2):
            lo, hi = [
                dot(attn, wo[:, a * HALF + i * QUART : a * HALF + (i + 1) * QUART]) for i in range(2)
            ]
            for n, block in enumerate(blocks):
                for i in range(2):
                    start = (2 * n + i) * SP
                    pair = [v[start : start + SH] for v in (lo, hi)]
                    terms[block * 2 + i, a] = jnp.concatenate(pair, axis=0).astype(BF)
            if dec is not None:
                start = len(blocks) * 2 * SP
                for i, v in enumerate((lo, hi)):
                    for k in range(2):
                        part[1, 4 * a + 2 * i + k] = v[start:, k * SL : (k + 1) * SL]

    order = (oh, h)

    def rs(n, src, dst, device):
        return Several(pieces(SUM_CUTS, src, dst, rs_send, rs_recv, 3 * n, device))

    far_up = [rs(i, terms.at[far * 2 + order[i], 0], relay.at[0, i], to_up) for i in range(2)]
    far_down = [rs(2 + i, terms.at[far * 2 + order[i], 1], relay.at[1, i], to_down) for i in range(2)]
    near_up = [
        [rs(4 + 2 * i + a, terms.at[up * 2 + order[i], a], arrive.at[0, i, a], to_up) for a in range(2)]
        for i in range(2)
    ]
    near_down = [
        [rs(8 + 2 * i + a, terms.at[down * 2 + order[i], a], arrive.at[1, i, a], to_down) for a in range(2)]
        for i in range(2)
    ]
    over_in, over = exchange(
        cross.at[0], through_cross, lambda a: cross.at[1, a], ex_send.at[1], ex_recv.at[1]
    )

    def relay_up(i):
        far_up[i].wait_recv()
        spot = up * 2 + order[i]
        terms[spot, 0] = (terms[spot, 0].astype(F32) + relay[0, i].astype(F32)).astype(BF)
        near_up[i][0].start()

    def relay_down(i):
        far_down[i].wait_recv()
        spot = down * 2 + order[i]
        terms[spot, 1] = (terms[spot, 1].astype(F32) + relay[1, i].astype(F32)).astype(BF)
        near_down[i][1].start()

    def summed(i, a):
        near_up[i][a].wait_recv()
        near_down[i][a].wait_recv()
        return (
            terms[y * 2 + order[i], a].astype(F32)
            + arrive[0, i, a].astype(F32)
            + arrive[1, i, a].astype(F32)
        )

    attend((far,))
    far_up[0].start()
    far_down[0].start()
    attend((up, down))
    send_caches(15)
    far_up[0].wait_send()
    near_up[0][1].start()
    far_down[0].wait_send()
    near_down[0][0].start()
    relay_up(0)
    relay_down(0)
    w1, wf1 = dec_weights(q1, [new0, new1])
    attend((y,), dec_attn(w1, wf1, [new0, new1]))
    send_parts(1)
    near_up[0][0].wait_send()
    far_up[1].start()
    near_down[0][1].wait_send()
    far_down[1].start()
    for a in range(2):
        cross[0, a] = summed(0, a).astype(BF)
        over_in[a].start()

    columns = [reduce_parts(1, xbuf[t])]
    for k, v in (new0, new1):
        columns += [k, v]
    leaving = dot(drop[:, :RP], jnp.concatenate(columns, axis=1))
    for i in range(MSG // HD):
        fin[:, i, :] = leaving[:, i * HD : (i + 1) * HD]
    arrived[g] = fin[g]

    def fin_copy(k):
        target = (g + k) % NG
        return remote(fin.at[target], arrived.at[g], fin_send.at[k], fin_recv.at[k], {"group": target})

    lax.fori_loop(1, NG, lambda k, c: (fin_copy(k).start(), c)[1], 0)

    far_up[1].wait_send()
    near_up[1][1].start()
    far_down[1].wait_send()
    near_down[1][0].start()
    for a in range(2):
        over_in[a].wait_recv()
        over[a].start()
    relay_up(1)
    relay_down(1)

    for a in range(2):
        near = summed(1, a)
        for i in range(2):
            cols = slice(a * HALF + i * QUART, a * HALF + (i + 1) * QUART)
            add = near[i * SH : (i + 1) * SH]
            score_sum[:, cols] = score_ref[:, cols].astype(F32) + add

    lax.fori_loop(1, NG, lambda k, c: (fin_copy(k).wait_recv(), c)[1], 0)
    placed = [dot(pick[:, :NG], arrived[:, i, :].astype(BF)) for i in range(MSG // HD)]
    obuf[t] = jnp.concatenate(placed[: SL // HD], axis=1).astype(BF)
    patch_ref[...] = jnp.concatenate(placed[SL // HD :], axis=1)

    def o_copy(k):
        return remote(obuf.at[t], obuf.at[t], o_send.at[k], o_recv.at[k], {"tp": (t + k) % NT})

    lax.fori_loop(1, NT, lambda k, c: (o_copy(k).start(), c)[1], 0)

    for a in range(2):
        over[a].wait_recv()
        far_half = cross[1, a].astype(F32)
        for i in range(2):
            cols = slice(a * HALF + i * QUART, a * HALF + (i + 1) * QUART)
            add = far_half[i * SH : (i + 1) * SH]
            score_out_ref[:, cols] = (score_sum[:, cols] + add).astype(BF)

    lax.fori_loop(1, NT, lambda k, c: (o_copy(k).wait_recv(), c)[1], 0)
    for p in range(NT):
        dec_out_ref[:, p * SL : (p + 1) * SL] = obuf[p]

    def end_a2a(j, c):
        a2a(j).wait()
        return c

    lax.fori_loop(1, 8, end_a2a, 0)
    lax.fori_loop(12, NG, end_a2a, 0)
    for m, kv in halves_z:
        z_out(m, kv).wait()
    own_copy.wait()
    ended = [first_up, first_down, second_up, second_down] + fwd_up + fwd_down
    ended += x_in + x_out + over_in + over + [z_in(m, kv) for m, kv in halves_z]
    ended += near_up[1] + near_down[1] + [near_up[0][1], near_down[0][0]]
    for c in ended:
        c.wait_send()

    def end_tp(k, c):
        part_copy(0, k).wait_send()
        part_copy(1, k).wait_send()
        x_copy(k).wait_send()
        o_copy(k).wait_send()
        return c

    lax.fori_loop(1, NT, end_tp, 0)
    lax.fori_loop(1, NG, lambda k, c: (fin_copy(k).wait_send(), c)[1], 0)


def place_kernel(
    plan_ref, patch_ref, dec_ref, got_hbm, score_hbm,
    dec_out_ref, cache_out, score_out, rows, score_rows, in_sem, out_sem, score_sem,
):
    score_in = pltpu.make_async_copy(score_hbm, score_rows, score_sem.at[0])
    score_end = pltpu.make_async_copy(score_rows, score_out, score_sem.at[1])
    score_in.start()

    def get(s, c):
        pltpu.make_async_copy(got_hbm.at[plan_ref[s, 0]], rows.at[s], in_sem.at[s]).start()
        return c

    lax.fori_loop(0, R, get, 0)
    dec_out_ref[...] = dec_ref[:R, :]
    score_in.wait()
    score_end.start()

    def put(s, c):
        pltpu.make_async_copy(got_hbm.at[0], rows.at[s], in_sem.at[s]).wait()
        entry = patch_ref[pl.ds(s, 1), :]
        for step in range(2):
            pos = plan_ref[s, 1] + step
            base = pl.multiple_of((pos // 16) * 16, 16)
            here = lax.broadcasted_iota(jnp.int32, (16, HD), 0) == pos - base
            for kv in range(2):
                start = (2 * step + kv) * HD
                old = rows[s, kv, pl.ds(base, 16), :].astype(F32)
                both = jnp.where(here, entry[:, start : start + HD], old)
                rows[s, kv, pl.ds(base, 16), :] = both.astype(BF)
        pltpu.make_async_copy(rows.at[s], cache_out.at[s], out_sem.at[s]).start()
        return c

    lax.fori_loop(0, R, put, 0)

    def end(s, c):
        pltpu.make_async_copy(rows.at[s], cache_out.at[s], out_sem.at[s]).wait()
        return c

    lax.fori_loop(0, R, end, 0)
    score_end.wait()


def per_device(
    dec_rows, kv_cache, lengths, dest_group, dest_slot, score_rows, doc_ids,
    norm_gain, query_gain, key_gain, w_query, w_keyval, w_out,
):
    smem = pl.BlockSpec(memory_space=pltpu.SMEM)
    vmem = pl.BlockSpec(memory_space=pltpu.VMEM)
    hbm = pl.BlockSpec(memory_space=pl.ANY)
    dma = pltpu.SemaphoreType.DMA
    got, patch, plan, dec_out16, score_sum = pl.pallas_call(
        main_kernel,
        name="decode_and_score",
        out_shape=(
            jax.ShapeDtypeStruct((NG, 2, CTX, HD), BF),
            jax.ShapeDtypeStruct((RP, 4 * HD), F32),
            jax.ShapeDtypeStruct((RP, HD), jnp.int32),
            jax.ShapeDtypeStruct((RP, D), BF),
            jax.ShapeDtypeStruct((SH, D), BF),
        ),
        in_specs=[smem] * 3 + [vmem] * 4 + [hbm] * 6,
        out_specs=(hbm, vmem, vmem, vmem, vmem),
        scratch_shapes=[
            pltpu.VMEM((SH, D), BF),
            pltpu.VMEM((R, D), BF),
            pltpu.VMEM((R, 2, CTX, HD), BF),
            pltpu.VMEM((2 * D, HD), BF),
            pltpu.VMEM((D, 768), BF),
            pltpu.VMEM((512, D), BF),
            pltpu.VMEM((RP, D), F32),
            pltpu.VMEM((16, TOK), F32),
            pltpu.VMEM((TOK, HD), F32),
            pltpu.VMEM((NG, 2, CTX, HD), BF),
            pltpu.VMEM((NT, 2, 2 * SH, QUART), BF),
            pltpu.VMEM((TOK, D), BF),
            pltpu.VMEM((TOK, HD), F32),
            pltpu.VMEM((4, TOK, HD), BF),
            pltpu.VMEM((TOK, HD), F32),
            pltpu.VMEM((HD, TOK), BF),
            pltpu.VMEM((TOK, HD), BF),
            pltpu.VMEM((NT, 2, 2 * SH, QUART), BF),
            pltpu.VMEM((2, 2, 2 * SH, QUART), BF),
            pltpu.VMEM((2, 2, 2, 2 * SH, QUART), BF),
            pltpu.VMEM((2, 2, 2 * SH, QUART), BF),
            pltpu.VMEM((2, 2 * SH, QUART), BF),
            pltpu.VMEM((2, 4, CTX, HD), BF),
            pltpu.VMEM((2, 2 * SH, QUART), BF),
            pltpu.VMEM((SH, D), F32),
            pltpu.VMEM((2, NT, RP, SL), F32),
            pltpu.VMEM((2, NT, RP, SL), F32),
            pltpu.VMEM((NT, RP, SL), BF),
            pltpu.VMEM((RP, D), BF),
            pltpu.VMEM((4 * RP, CTX), F32),
            pltpu.VMEM((RP, HD), BF),
            pltpu.VMEM((RP, HD), BF),
            pltpu.VMEM((NG, RP, HD), F32),
            pltpu.VMEM((NG, RP, HD), F32),
            pltpu.VMEM((NT, RP, SL), BF),
            dma((6,)), dma((NG,)), dma((NG,)), dma((2, 4)), dma((2, 4)), dma((2, 4)), dma((2, 4)), dma((2, 4)), dma((2, 4)), dma((28,)), dma((28,)), dma((42,)), dma((42,)),
            dma((2, NT)), dma((2, NT)), dma((NT,)), dma((NT,)), dma((NG,)), dma((NG,)),
            dma((NT,)), dma((NT,)),
        ],
        compiler_params=pltpu.CompilerParams(
            collective_id=0, has_side_effects=True, vmem_limit_bytes=60 * 1024 * 1024
        ),
        cost_estimate=pl.CostEstimate(flops=8 * 10**9, bytes_accessed=30 * 10**6, transcendentals=10**6),
    )(
        dest_group, dest_slot, lengths, norm_gain.reshape(1, D),
        query_gain.reshape(1, HD), key_gain.reshape(1, HD), doc_ids,
        kv_cache, w_query, w_keyval.reshape(2 * D, HD), w_out, score_rows, dec_rows,
    )
    return pl.pallas_call(
        place_kernel,
        name="place_rows",
        out_shape=(
            jax.ShapeDtypeStruct((R, D), BF),
            jax.ShapeDtypeStruct((R, 2, CTX, HD), BF),
            jax.ShapeDtypeStruct((SH, D), BF),
        ),
        in_specs=[smem] + [vmem] * 2 + [hbm] * 2,
        out_specs=(vmem, hbm, hbm),
        scratch_shapes=[
            pltpu.VMEM((R, 2, CTX, HD), BF),
            pltpu.VMEM((SH, D), BF),
            dma((R,)), dma((R,)), dma((2,)),
        ],
        compiler_params=pltpu.CompilerParams(vmem_limit_bytes=60 * 1024 * 1024),
        cost_estimate=pl.CostEstimate(flops=10**6, bytes_accessed=12 * 10**6, transcendentals=0),
    )(plan, patch, dec_out16, got, score_sum)


def solution(mesh):
    placed = (
        P("group", None),
        P("group", None, None, "tp"),
        P(),
        P(),
        P(),
        P(("group", "tp"), None),
        P("group", None),
        P(),
        P(),
        P(),
        P(None, "tp"),
        P(None, None, "tp"),
        P("tp", None),
    )
    return jax.shard_map(
        per_device,
        mesh=mesh,
        in_specs=placed,
        out_specs=(P("group", None), P("group", None, None, "tp"), P(("group", "tp"), None)),
        check_vma=False,
    )
```
